32 devices in a mesh: dp: 8 (over y, x, core), mp: 4 (over z).
Axes of the slice: x: 2, y: 2, z: 4, core: 2. Of those that a mesh axis runs over, the one named last changes fastest.
Arguments:
- tokens: bfloat16 [8192, 2048], P(('dp', 'mp')), may hold values from -8 to 8
- cotangent: bfloat16 [8192, 2048], P(('dp', 'mp')), may hold values from -6 to 6
- lengths: int32 [8, 4], P('dp'), may hold values from 1 to 512, 1024 in all within a row
- live_mask: int32 [8192], P(('dp', 'mp')), may hold values 0 or 1
- mixer_gain: float32 [2048], replicated, may hold values from 0.5 to 1.5
- value_proj: bfloat16 [2048, 2560], P(None, 'mp'), may hold values from -0.125 to 0.125
- gate_proj: bfloat16 [2048, 2560], P(None, 'mp'), may hold values from -0.125 to 0.125
- conv_taps: float32 [4, 2560], P(None, 'mp'), may hold values from -3 to 3
- conv_bias: float32 [2560], P('mp'), may hold values from -3 to 3
- rate_weight: float32 [16, 160, 160], P('mp'), may hold values from -0.5 to 0.5
- rate_bias: float32 [2560], P('mp'), may hold values from -3 to 3
- inlet_weight: float32 [16, 160, 160], P('mp'), may hold values from -0.5 to 0.5
- inlet_bias: float32 [2560], P('mp'), may hold values from -3 to 3
- decay_param: float32 [2560], P('mp'), may hold values from 1 to 6
- mixer_out: bfloat16 [2560, 2048], P('mp'), may hold values from -0.3125 to 0.3125
- dense_gain: float32 [2048], replicated, may hold values from 0.5 to 1.5
- dense_gate: bfloat16 [2048, 6144], P(None, 'mp'), may hold values from -0.125 to 0.125
- dense_value: bfloat16 [2048, 6144], P(None, 'mp'), may hold values from -0.125 to 0.125
- dense_down: bfloat16 [6144, 2048], P('mp'), may hold values from -0.15625 to 0.15625
Outputs:
- layer_out: bfloat16 [8192, 2048], P(('dp', 'mp'))
- input_grad: bfloat16 [8192, 2048], P(('dp', 'mp'))
- mixer_gain_grad: float32 [2048], replicated
- value_proj_grad: float32 [2048, 2560], P('dp', 'mp')
- gate_proj_grad: float32 [2048, 2560], P('dp', 'mp')
- conv_taps_grad: float32 [4, 2560], P(None, 'mp')
- conv_bias_grad: float32 [2560], P('mp')
- rate_weight_grad: float32 [16, 160, 160], P('mp')
- rate_bias_grad: float32 [2560], P('mp')
- inlet_weight_grad: float32 [16, 160, 160], P('mp')
- inlet_bias_grad: float32 [2560], P('mp')
- decay_param_grad: float32 [2560], P('mp')
- mixer_out_grad: float32 [2560, 2048], P('mp', 'dp')
- dense_gain_grad: float32 [2048], replicated
- dense_gate_grad: float32 [2048, 6144], P('dp', 'mp')
- dense_value_grad: float32 [2048, 6144], P('dp', 'mp')
- dense_down_grad: float32 [6144, 2048], P('mp', 'dp')
- branch_rms: float32 [3], replicated
The draws below stay inside these ranges and needn't reach their ends.
Inputs may be any that keep to these rules, and one draw needn't show every extreme that they name: Each row holds 4 lengths summing to 1024; the longest of each row is exactly 512.
All inputs are finite; a program needn't handle non-finite values. No bound on the sum of `live_mask` on one device may be relied on, other than what follows from the above.
Results may differ from the reference program's by a relative error of at most 0.011.
Values may be sent and summed in bfloat16 or wider, within the bound.
A program may use at most 320 MiB of HBM per device.

```python
import math
import jax
import jax.numpy as jnp
import numpy as np
from jax import lax

D = 2048
FF = 6144
HEADS = 16
HEAD_SIZE = 160
CONV = 4
SEQ_DEV = 4
TOK_DEV = 1024
R = 2560
MOST = 512
GROUPS = 8
TOKENS = 8192


def draw_tokens(key, part):
    key = jax.random.fold_in(key, 11)
    rows = jnp.arange(TOKENS, dtype=jnp.float32)[:, None]
    scales = 0.6 + 1.2 * rows / TOKENS
    base = jax.random.truncated_normal(key, -4.0, 4.0, (TOKENS, D), jnp.float32)
    return (scales * base).astype(jnp.bfloat16)


def with_ends(drawn, stream_key, smallest, largest):
    shape = drawn.shape
    spot = [jax.random.randint(jax.random.fold_in(stream_key, axis), (), 0, shape[axis]) for axis in range(len(shape))]
    drawn = drawn.at[tuple(spot)].set(smallest)
    longest = shape.index(max(shape))
    spot[longest] = (spot[longest] + 1) % shape[longest]
    return drawn.at[tuple(spot)].set(largest)


def with_spikes(result, own_key, source, target, blocks, factor):
    owner, partner = [(jnp.arange(result.shape[dim]) // (result.shape[dim] // blocks)).reshape([-1 if axis == dim else 1 for axis in range(result.ndim)]) for dim in (source, target)]
    chosen = jax.random.permutation(own_key, blocks)[partner]
    strong = (owner == chosen) | (owner == (partner + blocks // 2) % blocks)
    return jnp.where(strong, factor * result, result)


def block_levels(key, extent, split, low, top_value):
    def one(position, parts):
        draws = jax.random.uniform(jax.random.fold_in(jax.random.fold_in(key, 6), position), (parts,), jnp.float32, low / len(split), top_value / len(split))
        return jnp.repeat(jnp.exp(draws), extent[position] // parts).reshape((-1,) + (1,) * (len(extent) - position - 1))

    gain = one(*split[0])
    for cut in split[1:]:
        gain = gain * one(*cut)
    return gain


def profile(amount, total, reach, slope):
    portions = [(1 << 20) // math.isqrt(grade ** slope) + 1 for grade in range(2, amount + 1)]
    surplus, holding = total - reach - (amount - 1), [1] * (amount - 1)
    while surplus > 0:
        movable = [i for i in range(amount - 1) if holding[i] < reach]
        whole, budget = sum([portions[i] for i in movable]), surplus
        for i in movable:
            more = min(reach - holding[i], max(1, budget * portions[i] // whole), surplus)
            holding[i] = holding[i] + more
            surplus = surplus - more
    return np.array([reach] + holding)


def ragged_sizes(rng, count, total, reach, skew):
    if count == 2:
        one = jax.random.randint(rng, (), max(1, total - reach), min(reach, total - 1) + 1)
        return jnp.stack([one, total - one])
    sizes = jnp.asarray(profile(count, total, reach, skew), jnp.int32)
    twos = (count - 1) // 2
    donor, taker = sizes[1:1 + 2 * twos:2], sizes[2:2 + 2 * twos:2]
    slack = jnp.minimum(donor - 1, reach - taker)
    moved = jax.random.randint(jax.random.fold_in(rng, 1), (twos,), 0, 1 << 20) % (slack + 1)
    sizes = sizes.at[1:1 + 2 * twos:2].set(donor - moved).at[2:2 + 2 * twos:2].set(taker + moved)
    return sizes[jax.random.permutation(jax.random.fold_in(rng, 2), count)]


def noise(stream_key, shape, scale, most, cuts=(), kind=jnp.bfloat16):
    result = scale * jax.random.normal(stream_key, shape, jnp.float32)
    if cuts:
        result = result * block_levels(stream_key, shape, cuts, -0.22, 0.18)
    return jnp.clip(result, -most, most).astype(kind)


def noise_with(own_key, dims, width, bound, split, heavy, held_as=jnp.bfloat16):
    drawn = width * jax.random.normal(own_key, dims, jnp.float32)
    if split:
        drawn = drawn * block_levels(own_key, dims, split, -0.22, 0.18)
    return jnp.clip(with_spikes(drawn, jax.random.fold_in(own_key, 3), *heavy), -bound, bound).astype(held_as)


def setup_inputs(seed: int = 0) -> dict:
    keys = jax.random.split(jax.random.key(seed), 20)
    return {
        "tokens": draw_tokens(jax.random.fold_in(keys[19], 71), 0),
        "cotangent": noise_with(keys[1], (TOKENS, D), 1.0, 6.0, ((0, 32),), (0, 1, 32, 2.75)),
        "lengths": jax.vmap(lambda own: ragged_sizes(own, SEQ_DEV, TOK_DEV, MOST, 2))(jax.random.split(keys[2], GROUPS)).reshape((GROUPS, SEQ_DEV)).astype(jnp.int32),
        "live_mask": with_ends((jax.random.randint(keys[3], (TOKENS,), 0, 8) < 7).astype(jnp.int32), jax.random.fold_in(keys[3], 1), 0, 1),
        "mixer_gain": jnp.clip(1.0 + 0.1 * jax.random.normal(keys[4], (D,), jnp.float32), 0.5, 1.5),
        "value_proj": noise(keys[5], (D, R), D ** -0.5, 0.125, ((1, 4),)),
        "gate_proj": noise(keys[6], (D, R), D ** -0.5, 0.125, ((1, 4),)),
        "conv_taps": noise(keys[7], (CONV, R), CONV ** -0.5, 3.0, ((1, 4),), jnp.float32),
        "conv_bias": noise(keys[8], (R,), 0.5, 3.0, ((0, 4),), jnp.float32),
        "rate_weight": noise(keys[9], (HEADS, HEAD_SIZE, HEAD_SIZE), HEAD_SIZE ** -0.5, 0.5, ((0, 4),), jnp.float32),
        "rate_bias": noise(keys[10], (R,), 0.5, 3.0, ((0, 4),), jnp.float32),
        "inlet_weight": noise(keys[11], (HEADS, HEAD_SIZE, HEAD_SIZE), HEAD_SIZE ** -0.5, 0.5, ((0, 4),), jnp.float32),
        "inlet_bias": noise(keys[12], (R,), 0.5, 3.0, ((0, 4),), jnp.float32),
        "decay_param": jnp.clip(1.0 + 5.0 * jax.random.uniform(keys[13], (R,), jnp.float32) ** block_levels(keys[13], (R,), ((0, 4),), -0.2, 0.2), 1.0, 6.0),
        "mixer_out": noise(keys[14], (R, D), (R // 8) ** -0.5, 0.3125, ((0, 4),)),
        "dense_gain": jnp.clip(1.0 + 0.1 * jax.random.normal(keys[15], (D,), jnp.float32), 0.5, 1.5),
        "dense_gate": noise(keys[16], (D, FF), D ** -0.5, 0.125, ((1, 4),)),
        "dense_value": noise(keys[17], (D, FF), D ** -0.5, 0.125, ((1, 4),)),
        "dense_down": noise(keys[18], (FF, D), (FF // 4) ** -0.5, 0.15625, ((0, 4),)),
    }


EPS = 1e-06
HIGHEST = lax.Precision.HIGHEST

@jax.custom_vjp
def low(v):
    return lax.optimization_barrier(v.astype(jnp.bfloat16)).astype(jnp.float32)

@jax.custom_vjp
def low_back(v):
    return v

def low_keep(v):
    return (low(v), None)

def low_pass(kept, grad):
    return (grad,)

def back_keep(v):
    return (v, None)

def back_low(kept, grad):
    return (low(grad),)
low.defvjp(low_keep, low_pass)
low_back.defvjp(back_keep, back_low)

def doc_offsets(lengths_row, rows_total):
    doc_ends = jnp.cumsum(lengths_row).astype(jnp.int32)
    positions = jnp.arange(rows_total, dtype=jnp.int32)
    before = (doc_ends[None, :] <= positions[:, None]).astype(jnp.int32)
    starts = lax.optimization_barrier(jnp.sum(before * lengths_row[None, :].astype(jnp.int32), axis=1)).astype(jnp.int32)
    return positions - starts

def scaled_norm(values, gain_vec):
    return values * lax.rsqrt(lax.optimization_barrier(jnp.mean(values * values, axis=1, keepdims=True)) + EPS) * gain_vec[None, :]

def combine(first_pair, second_pair):
    first_mult, first_add = first_pair
    second_mult, second_add = second_pair
    return (first_mult * second_mult, second_mult * first_add + second_add)

def recurrent(value_pre, gate_pre, conv_taps, conv_bias, rate_weight, rate_bias, inlet_weight, inlet_bias, decay_param, offsets):
    rows_total, columns = value_pre.shape
    convolved = jnp.zeros_like(value_pre) + conv_bias[None, :]
    for tap_index in range(conv_taps.shape[0]):
        shifted = jnp.concatenate([jnp.zeros((tap_index, columns), value_pre.dtype), value_pre[:rows_total - tap_index]], axis=0)
        convolved = convolved + jnp.where((offsets >= tap_index)[:, None], shifted, 0.0) * conv_taps[tap_index][None, :]
    head_count, head_width = (rate_weight.shape[0], rate_weight.shape[1])
    blocks = convolved.reshape(rows_total, head_count, head_width)
    forget_gate = jax.nn.sigmoid(jnp.einsum('thi,hij->thj', blocks, rate_weight, precision=HIGHEST).reshape(rows_total, columns) + rate_bias[None, :])
    input_gate = jax.nn.sigmoid(jnp.einsum('thi,hij->thj', blocks, inlet_weight, precision=HIGHEST).reshape(rows_total, columns) + inlet_bias[None, :])
    log_decay = -8.0 * forget_gate * jax.nn.softplus(-decay_param)[None, :]
    carried = jnp.where((offsets > 0)[:, None], jnp.exp(log_decay), 0.0)
    normalizer = jnp.sqrt(-jnp.expm1(2.0 * log_decay))
    unused, states = lax.associative_scan(combine, (carried, normalizer * input_gate * convolved), axis=0)
    return states * jax.nn.gelu(gate_pre)

def product(left, right):
    return jnp.dot(left, right, precision=HIGHEST, preferred_element_type=jnp.float32)

def group_layer(params, group_item):
    mixer_gain, value_proj, gate_proj, conv_taps, conv_bias, rate_weight, rate_bias, inlet_weight, inlet_bias, decay_param, mixer_out, dense_gain, dense_gate, dense_value, dense_down = params
    residual, lengths_row, live_rows = group_item
    offsets = doc_offsets(lengths_row, residual.shape[0])
    normed_in = low(scaled_norm(residual, mixer_gain))
    value_pre = low_back(product(normed_in, value_proj))
    gate_pre = low_back(product(normed_in, gate_proj))
    mixed_act = low(recurrent(value_pre, gate_pre, conv_taps, conv_bias, rate_weight, rate_bias, inlet_weight, inlet_bias, decay_param, offsets))
    mixer_part = low_back(product(mixed_act, mixer_out))
    middle = residual + mixer_part
    normed_mid = low(scaled_norm(middle, dense_gain))
    gate_linear = low_back(product(normed_mid, dense_gate))
    value_linear = low_back(product(normed_mid, dense_value))
    hidden = low(jax.nn.gelu(gate_linear) * value_linear)
    dense_part = product(hidden, dense_down)
    weights_live = live_rows.astype(residual.dtype)
    totals = jnp.stack([jnp.sum(weights_live * lax.optimization_barrier(jnp.sum(residual * residual, axis=1))), jnp.sum(weights_live * lax.optimization_barrier(jnp.sum(mixer_part * mixer_part, axis=1))), jnp.sum(weights_live * lax.optimization_barrier(jnp.sum(dense_part * dense_part, axis=1))), jnp.sum(weights_live)])
    return (middle + dense_part, totals)

def reference(tokens, cotangent, lengths, live_mask, mixer_gain, value_proj, gate_proj, conv_taps, conv_bias, rate_weight, rate_bias, inlet_weight, inlet_bias, decay_param, mixer_out, dense_gain, dense_gate, dense_value, dense_down):
    group_count = lengths.shape[0]
    columns = tokens.shape[1]
    residual = tokens.astype(jnp.float32).reshape(group_count, -1, columns)
    live_rows = live_mask.reshape(group_count, -1)
    params = tuple((array_in.astype(jnp.float32) for array_in in (mixer_gain, value_proj, gate_proj, conv_taps, conv_bias, rate_weight, rate_bias, inlet_weight, inlet_bias, decay_param, mixer_out, dense_gain, dense_gate, dense_value, dense_down)))
    stepper = jax.checkpoint(group_layer)

    def whole_layer(params, residual):
        outputs, totals = lax.map(lambda group_item: stepper(params, group_item), (residual, lengths, live_rows))
        return (outputs, lax.optimization_barrier(jnp.sum(totals, axis=0)))
    outputs, pullback, totals = jax.vjp(whole_layer, params, residual, has_aux=True)
    gradients, input_grad = pullback(cotangent.astype(jnp.float32).reshape(residual.shape))
    branch_rms = jnp.sqrt(totals[:3] / (totals[3] * columns))
    return (outputs.reshape(tokens.shape).astype(jnp.bfloat16), input_grad.reshape(tokens.shape).astype(jnp.bfloat16), gradients[0], gradients[1], gradients[2], gradients[3], gradients[4], gradients[5], gradients[6], gradients[7], gradients[8], gradients[9], gradients[10], gradients[11], gradients[12], gradients[13], gradients[14], branch_rms)
```

```python
import functools

import jax
import jax.numpy as jnp
from jax import lax
from jax.experimental import pallas as pl
from jax.experimental.pallas import tpu as pltpu
from jax.sharding import PartitionSpec as P

EPS = 1e-06
BF = jnp.bfloat16
F32 = jnp.float32
GELU_C = 0.7978845608028654
GELU_A = 0.044715
CHUNK = 16
VMEM_LIMIT = 60 * 1024 * 1024


def doc_offsets(lengths_row, rows_total):
    doc_ends = jnp.cumsum(lengths_row)
    positions = jnp.arange(rows_total, dtype=jnp.int32)
    before = (doc_ends[None, :] <= positions[:, None]).astype(jnp.int32)
    starts = jnp.sum(before * lengths_row[None, :], axis=1)
    return positions - starts


def scaled_norm(values, gain_vec):
    return (
        values
        * lax.rsqrt(jnp.mean(values * values, axis=1, keepdims=True) + EPS)
        * gain_vec[None, :]
    )


def dot_nn(left, right):
    return jnp.dot(left, right, preferred_element_type=F32)


def dot_nt(left, right):
    return lax.dot_general(left, right, (((1,), (1,)), ((), ())), preferred_element_type=F32)


def dot_tn(left, right):
    return lax.dot_general(left, right, (((0,), (0,)), ((), ())), preferred_element_type=F32)


def gelu(x):
    return 0.5 * x * (1.0 + jnp.tanh(GELU_C * (x + GELU_A * x * x * x)))


def gelu_both(x):
    square = x * x
    tanh_in = jnp.tanh(GELU_C * x * (1.0 + GELU_A * square))
    half = 0.5 * (1.0 + tanh_in)
    slope = half + 0.5 * x * (1.0 - tanh_in * tanh_in) * (GELU_C * (1.0 + 3.0 * GELU_A * square))
    return half * x, slope


def sigmoid(x):
    return 1.0 / (1.0 + jnp.exp(-x))


def one_minus_square(log_decay, carried):
    y = 2.0 * log_decay
    series = 1.0 + y * (1.0 / 7.0)
    for k in (6.0, 5.0, 4.0, 3.0, 2.0):
        series = 1.0 + y * (1.0 / k) * series
    return jnp.where(y > -0.5, -y * series, 1.0 - carried * carried)


def row_in_tile(shape):
    return lax.broadcasted_iota(jnp.int32, shape, 0) % 8


def scan_tile_down(mult, add):
    row = row_in_tile(mult.shape)
    for step in (1, 2, 4):
        keep = row >= step
        add_up = jnp.where(keep, pltpu.roll(add, step, 0), 0.0)
        mult_up = jnp.where(keep, pltpu.roll(mult, step, 0), 1.0)
        add = add + mult * add_up
        mult = mult * mult_up
    return mult, add


def scan_tile_up(mult, add):
    row = row_in_tile(mult.shape)
    for step in (1, 2, 4):
        keep = row < 8 - step
        add_dn = jnp.where(keep, pltpu.roll(add, 8 - step, 0), 0.0)
        mult_dn = jnp.where(keep, pltpu.roll(mult, 8 - step, 0), 1.0)
        add = add + mult * add_dn
        mult = mult * mult_dn
    return mult, add


V_BIAS, V_RATE, V_INLET, V_DECAY = 4, 5, 6, 7


def rec_forward(rows, vp_ref, gp_ref, mask_ref, vec_ref, rate_ref, inlet_ref,
                mixed_ref, state_ref, conv_ref, forget_ref, input_ref, low_ref):
    bias = vec_ref[V_BIAS:V_BIAS + 1, :]

    def conv_step(index, unused):
        base = pl.multiple_of(index * CHUNK, CHUNK)
        ext = vp_ref[pl.ds(base, CHUNK + 8), :]
        masks = mask_ref[pl.ds(base, CHUNK), :]
        total = bias + vec_ref[0:1, :] * ext[8:8 + CHUNK, :]
        for tap in (1, 2, 3):
            total = total + (masks[:, tap:tap + 1] * ext[8 - tap:8 - tap + CHUNK, :]) * vec_ref[tap:tap + 1, :]
        conv_ref[pl.ds(base, CHUNK), :] = total
        low_ref[pl.ds(base, CHUNK), :] = total.astype(BF)
        return unused

    lax.fori_loop(0, rows // CHUNK, conv_step, 0)
    block = 256

    def gate_step(index, unused):
        base = pl.multiple_of(index * block, block)
        low = low_ref[pl.ds(base, block), :]
        forget_ref[pl.ds(base, block), :] = dot_nn(low, rate_ref[...])
        input_ref[pl.ds(base, block), :] = dot_nn(low, inlet_ref[...])
        return unused

    lax.fori_loop(0, rows // block, gate_step, 0)
    rate_bias = vec_ref[V_RATE:V_RATE + 1, :]
    inlet_bias = vec_ref[V_INLET:V_INLET + 1, :]
    decay = vec_ref[V_DECAY:V_DECAY + 1, :]

    def scan_step(index, carry):
        base = pl.multiple_of(index * CHUNK, CHUNK)
        window = pl.ds(base, CHUNK)
        forget = sigmoid(forget_ref[window, :] + rate_bias)
        inlet = sigmoid(input_ref[window, :] + inlet_bias)
        log_decay = decay * forget
        carried = jnp.exp(log_decay)
        normalizer = jnp.sqrt(one_minus_square(log_decay, carried))
        forget_ref[window, :] = forget
        input_ref[window, :] = inlet
        add = normalizer * inlet * conv_ref[window, :]
        mult = carried * mask_ref[window, 1:2]
        pieces = []
        for tile in range(CHUNK // 8):
            m, a = scan_tile_down(mult[8 * tile:8 * tile + 8], add[8 * tile:8 * tile + 8])
            states = a + m * carry
            carry = states[7:8, :]
            pieces.append(states)
        states = jnp.concatenate(pieces, axis=0)
        state_ref[window, :] = states
        mixed_ref[window, :] = (states * gelu(gp_ref[window, :])).astype(BF)
        return carry

    lax.fori_loop(0, rows // CHUNK, scan_step, jnp.zeros((1, conv_ref.shape[1]), F32))


def rec_backward(rows, dm_ref, vp_ref, gp_ref, mask_ref, vec_ref, rate_ref, inlet_ref,
                 state_ref, conv_ref, forget_ref, input_ref,
                 vlow_ref, glow_ref, dzf_ref, dzi_ref, dconv_ref, clow_ref, sums_ref):
    columns = conv_ref.shape[1]
    decay = vec_ref[V_DECAY:V_DECAY + 1, :]
    chunks = rows // CHUNK
    zero_row = jnp.zeros((1, columns), F32)

    def scan_step(step, carry):
        grad_next, mult_next, rate_sum, inlet_sum, decay_sum = carry
        base = pl.multiple_of((chunks - 1 - step) * CHUNK, CHUNK)
        window = pl.ds(base, CHUNK)
        mixed_grad = dm_ref[window, :]
        act, slope = gelu_both(gp_ref[window, :])
        ext = state_ref[pl.ds(base, CHUNK + 8), :]
        states = ext[8:, :]
        before = ext[7:7 + CHUNK, :]
        glow_ref[window, :] = (mixed_grad * states * slope).astype(BF)
        add = mixed_grad * act
        forget = forget_ref[window, :]
        inlet = input_ref[window, :]
        conv = conv_ref[window, :]
        clow_ref[window, :] = conv.astype(BF)
        log_decay = decay * forget
        carried = jnp.exp(log_decay)
        square = one_minus_square(log_decay, carried)
        inverse = lax.rsqrt(jnp.maximum(square, 1e-30))
        normalizer = square * inverse
        mult = carried * mask_ref[window, 1:2]
        pieces = []
        for tile in reversed(range(CHUNK // 8)):
            lo = 8 * tile
            after = mult[lo + 8:lo + 9, :] if lo + 8 < CHUNK else mult_next
            shifted = jnp.concatenate([mult[lo + 1:lo + 8, :], after], axis=0)
            m, a = scan_tile_up(shifted, add[lo:lo + 8])
            grads = a + m * grad_next
            grad_next = grads[0:1, :]
            pieces.append(grads)
        grads = jnp.concatenate(pieces[::-1], axis=0)
        gated = grads * inlet
        d_log = grads * before * mult - gated * conv * ((1.0 - square) * inverse)
        d_forget = d_log * decay
        dzf = d_forget * forget * (1.0 - forget)
        dzi = grads * normalizer * conv * inlet * (1.0 - inlet)
        dzf_ref[window, :] = dzf.astype(BF)
        dzi_ref[window, :] = dzi.astype(BF)
        dconv_ref[window, :] = gated * normalizer
        return (grad_next, mult[0:1, :],
                rate_sum + jnp.sum(dzf.reshape(CHUNK // 8, 8, columns), axis=0),
                inlet_sum + jnp.sum(dzi.reshape(CHUNK // 8, 8, columns), axis=0),
                decay_sum + jnp.sum((d_log * forget).reshape(CHUNK // 8, 8, columns), axis=0))

    zeros = jnp.zeros((8, columns), F32)
    unused, unused, rate_sum, inlet_sum, decay_sum = lax.fori_loop(
        0, chunks, scan_step, (zero_row, zero_row, zeros, zeros, zeros))
    sums_ref[V_RATE:V_RATE + 1, :] = jnp.sum(rate_sum, axis=0, keepdims=True)
    sums_ref[V_INLET:V_INLET + 1, :] = jnp.sum(inlet_sum, axis=0, keepdims=True)
    sums_ref[V_DECAY:V_DECAY + 1, :] = jnp.sum(decay_sum, axis=0, keepdims=True)
    block = 256

    def gate_step(index, unused):
        base = pl.multiple_of(index * block, block)
        window = pl.ds(base, block)
        dconv_ref[window, :] += (dot_nt(dzf_ref[window, :], rate_ref[...])
                                 + dot_nt(dzi_ref[window, :], inlet_ref[...]))
        return unused

    lax.fori_loop(0, rows // block, gate_step, 0)

    def conv_step(index, carry):
        base = pl.multiple_of(index * CHUNK, CHUNK)
        window = pl.ds(base, CHUNK)
        ext = dconv_ref[pl.ds(base, CHUNK + 8), :]
        masks = mask_ref[pl.ds(base, CHUNK + 8), :]
        values = vp_ref[pl.ds(base, CHUNK + 8), :]
        here = ext[:CHUNK, :]
        total = vec_ref[0:1, :] * here
        sums = [carry[0] + fold(here * values[8:, :], columns)]
        for tap in (1, 2, 3):
            gated = ext * masks[:, tap:tap + 1]
            total = total + vec_ref[tap:tap + 1, :] * gated[tap:tap + CHUNK, :]
            sums.append(carry[tap] + fold(gated[:CHUNK, :] * values[8 - tap:8 - tap + CHUNK, :], columns))
        sums.append(carry[4] + fold(here, columns))
        vlow_ref[window, :] = total.astype(BF)
        return tuple(sums)

    sums = lax.fori_loop(0, chunks, conv_step, (zeros,) * 5)
    for row in range(5):
        sums_ref[row:row + 1, :] = jnp.sum(sums[row], axis=0, keepdims=True)


def fold(values, columns):
    return jnp.sum(values.reshape(CHUNK // 8, 8, columns), axis=0)


def forward_kernel(vp_in, gp_ref, mask_ref, vec_ref, rate_ref, inlet_ref,
                   mixed_ref, state_ref, conv_ref, forget_ref, input_ref, vp_ref, low_ref):
    rows, columns = vp_in.shape
    vp_ref[0:8, :] = jnp.zeros((8, columns), F32)
    vp_ref[8:, :] = vp_in[...]
    rec_forward(rows, vp_ref, gp_ref, mask_ref, vec_ref, rate_ref, inlet_ref,
                mixed_ref, state_ref, conv_ref, forget_ref, input_ref, low_ref)


def backward_kernel(dm_ref, vp_in, gp_ref, mask_ref, vec_ref, rate_ref, inlet_ref,
                    state_in, conv_ref, forget_ref, input_ref,
                    vlow_ref, glow_ref, rate_grad_ref, inlet_grad_ref, sums_ref,
                    vp_ref, state_ref, dzf_ref, dzi_ref, dconv_ref, clow_ref):
    rows, columns = vp_in.shape
    zeros = jnp.zeros((8, columns), F32)
    vp_ref[0:8, :] = zeros
    vp_ref[8:, :] = vp_in[...]
    state_ref[0:8, :] = zeros
    state_ref[8:, :] = state_in[...]
    dconv_ref[rows:rows + 8, :] = zeros
    rec_backward(rows, dm_ref, vp_ref, gp_ref, mask_ref, vec_ref, rate_ref, inlet_ref,
                 state_ref, conv_ref, forget_ref, input_ref,
                 vlow_ref, glow_ref, dzf_ref, dzi_ref, dconv_ref, clow_ref, sums_ref)
    rate_grad_ref[...] = dot_tn(clow_ref[...], dzf_ref[...])
    inlet_grad_ref[...] = dot_tn(clow_ref[...], dzi_ref[...])


def call_forward(vp, gp, masks, vec, rate, inlet):
    rows, columns = vp.shape
    wide = jax.ShapeDtypeStruct((rows, columns), F32)
    return pl.pallas_call(
        forward_kernel,
        out_shape=(jax.ShapeDtypeStruct((rows, columns), BF), wide, wide, wide, wide),
        scratch_shapes=[pltpu.VMEM((rows + 8, columns), F32), pltpu.VMEM((rows, columns), BF)],
        compiler_params=pltpu.CompilerParams(vmem_limit_bytes=VMEM_LIMIT),
        cost_estimate=pl.CostEstimate(flops=4 * rows * columns * columns,
                                      bytes_accessed=30 * rows * columns, transcendentals=6 * rows * columns),
    )(vp, gp, masks, vec, rate, inlet)


def call_backward(dm, vp, gp, masks, vec, rate, inlet, state, conv, forget, inp):
    rows, columns = vp.shape
    low = jax.ShapeDtypeStruct((rows, columns), BF)
    square = jax.ShapeDtypeStruct((columns, columns), F32)
    return pl.pallas_call(
        backward_kernel,
        out_shape=(low, low, square, square, jax.ShapeDtypeStruct((8, columns), F32)),
        scratch_shapes=[
            pltpu.VMEM((rows + 8, columns), F32),
            pltpu.VMEM((rows + 8, columns), F32),
            pltpu.VMEM((rows, columns), BF),
            pltpu.VMEM((rows, columns), BF),
            pltpu.VMEM((rows + 8, columns), F32),
            pltpu.VMEM((rows, columns), BF),
        ],
        compiler_params=pltpu.CompilerParams(vmem_limit_bytes=VMEM_LIMIT),
        cost_estimate=pl.CostEstimate(flops=8 * rows * columns * columns,
                                      bytes_accessed=40 * rows * columns, transcendentals=4 * rows * columns),
    )(dm, vp, gp, masks, vec, rate, inlet, state, conv, forget, inp)


def block_diagonal(heads):
    count, width, unused = heads.shape
    spread = heads[:, :, None, :] * jnp.eye(count, dtype=heads.dtype)[:, None, :, None]
    return spread.reshape(count * width, count * width)


def diagonal_blocks(square, count):
    width = square.shape[0] // count
    return jnp.stack([square[h * width:(h + 1) * width, h * width:(h + 1) * width] for h in range(count)])


def scatter_mp(values):
    return lax.psum_scatter(values.astype(BF), "mp", scatter_dimension=0, tiled=True).astype(F32)


def scatter_dp(values, dimension):
    return lax.psum_scatter(values.astype(BF), "dp", scatter_dimension=dimension, tiled=True).astype(F32)


def gated_unit(gate_linear, value_linear):
    return gelu(gate_linear) * value_linear


def local(tokens, cotangent, lengths, live_mask, mixer_gain, value_proj, gate_proj, conv_taps, conv_bias,
          rate_weight, rate_bias, inlet_weight, inlet_bias, decay_param, mixer_out, dense_gain,
          dense_gate, dense_value, dense_down):
    residual = tokens.astype(F32)
    columns = residual.shape[1]
    head_count = rate_weight.shape[0]
    normed_first, norm_back_in = jax.vjp(scaled_norm, residual, mixer_gain)
    normed_all = lax.all_gather(normed_first.astype(BF), "mp", axis=0, tiled=True)
    rows_total = normed_all.shape[0]
    offsets = doc_offsets(lengths[0], rows_total)
    taps_here = jnp.arange(8, dtype=jnp.int32)
    masks = (offsets[:, None] >= taps_here[None, :]).astype(F32)
    masks_ext = jnp.concatenate([masks, jnp.zeros((8, 8), F32)], axis=0)
    vec = jnp.concatenate([
        conv_taps,
        jnp.stack([conv_bias, rate_bias, inlet_bias, -8.0 * jax.nn.softplus(-decay_param)]),
    ], axis=0)
    rate_square = block_diagonal(rate_weight).astype(BF)
    inlet_square = block_diagonal(inlet_weight).astype(BF)
    value_pre = dot_nn(normed_all, value_proj)
    gate_pre = dot_nn(normed_all, gate_proj)
    mixed_act, states, convolved, forget_gate, input_gate = call_forward(
        value_pre, gate_pre, masks_ext, vec, rate_square, inlet_square)
    mixer_part = scatter_mp(dot_nn(mixed_act, mixer_out))
    middle = residual + mixer_part
    normed_float, norm_back_mid = jax.vjp(scaled_norm, middle, dense_gain)
    normed_mid_all = lax.all_gather(normed_float.astype(BF), "mp", axis=0, tiled=True)
    gate_linear = dot_nn(normed_mid_all, dense_gate)
    value_linear = dot_nn(normed_mid_all, dense_value)
    hidden_float, gated_back = jax.vjp(gated_unit, gate_linear, value_linear)
    hidden = hidden_float.astype(BF)
    dense_part = scatter_mp(dot_nn(hidden, dense_down))
    layer_out = (middle + dense_part).astype(BF)
    weights_live = live_mask.astype(F32)
    squares = jnp.stack([
        jnp.sum(weights_live * jnp.sum(residual * residual, axis=1)),
        jnp.sum(weights_live * jnp.sum(mixer_part * mixer_part, axis=1)),
        jnp.sum(weights_live * jnp.sum(dense_part * dense_part, axis=1)),
    ])
    live_count = jnp.sum(weights_live)
    block_rows = lax.all_gather(cotangent, "mp", axis=0, tiled=True)
    hidden_grad = dot_nt(block_rows, dense_down)
    down_grad = dot_tn(hidden, block_rows)
    gate_grad_float, value_grad_float = gated_back(hidden_grad)
    gate_grad = gate_grad_float.astype(BF)
    value_grad = value_grad_float.astype(BF)
    normed_mid_grad = scatter_mp(dot_nt(gate_grad, dense_gate) + dot_nt(value_grad, dense_value))
    dense_gate_grad = dot_tn(normed_mid_all, gate_grad)
    dense_value_grad = dot_tn(normed_mid_all, value_grad)
    middle_norm_grad, dense_gain_grad = norm_back_mid(normed_mid_grad)
    middle_grad = cotangent.astype(F32) + middle_norm_grad
    middle_low = middle_grad.astype(BF)
    middle_rows = lax.all_gather(middle_low, "mp", axis=0, tiled=True)
    mixed_grad = dot_nt(middle_rows, mixer_out)
    mixer_out_grad = dot_tn(mixed_act, middle_rows)
    value_low, gate_low, rate_sq, inlet_sq, vec_grad = call_backward(
        mixed_grad, value_pre, gate_pre, masks_ext, vec, rate_square, inlet_square,
        states, convolved, forget_gate, input_gate)
    normed_in_grad = scatter_mp(dot_nt(value_low, value_proj) + dot_nt(gate_low, gate_proj))
    value_proj_grad = dot_tn(normed_all, value_low)
    gate_proj_grad = dot_tn(normed_all, gate_low)
    input_norm_grad, mixer_gain_grad = norm_back_in(normed_in_grad)
    input_grad = (middle_grad + input_norm_grad).astype(BF)
    small = (vec_grad, diagonal_blocks(rate_sq, head_count), diagonal_blocks(inlet_sq, head_count))
    vec_sum, rate_sum, inlet_sum = lax.psum(small, "dp")
    decay_scale = 8.0 * jax.nn.sigmoid(-decay_param)
    mixer_gain_sum, dense_gain_sum, squares, live_count = lax.psum(
        (mixer_gain_grad, dense_gain_grad, squares, live_count), ("dp", "mp"))
    branch_rms = jnp.sqrt(squares / (live_count * columns))
    return (
        layer_out,
        input_grad,
        mixer_gain_sum,
        scatter_dp(value_proj_grad, 0),
        scatter_dp(gate_proj_grad, 0),
        vec_sum[0:4],
        vec_sum[4],
        rate_sum,
        vec_sum[V_RATE],
        inlet_sum,
        vec_sum[V_INLET],
        vec_sum[V_DECAY] * decay_scale,
        scatter_dp(mixer_out_grad, 1),
        dense_gain_sum,
        scatter_dp(dense_gate_grad, 0),
        scatter_dp(dense_value_grad, 0),
        scatter_dp(down_grad, 1),
        branch_rms,
    )


def solution(mesh):
    rows = P(("dp", "mp"), None)
    return jax.shard_map(
        local,
        mesh=mesh,
        in_specs=(
            rows, rows, P("dp", None), P(("dp", "mp")), P(),
            P(None, "mp"), P(None, "mp"), P(None, "mp"), P("mp"),
            P("mp", None, None), P("mp"), P("mp", None, None), P("mp"), P("mp"),
            P("mp", None), P(), P(None, "mp"), P(None, "mp"), P("mp", None),
        ),
        out_specs=(
            rows, rows, P(), P("dp", "mp"), P("dp", "mp"),
            P(None, "mp"), P("mp"), P("mp", None, None), P("mp"), P("mp", None, None), P("mp"), P("mp"),
            P("mp", "dp"), P(), P("dp", "mp"), P("dp", "mp"), P("mp", "dp"), P(),
        ),
        check_vma=False,
    )
```

```python
import functools

import jax
import jax.numpy as jnp
from jax import lax
from jax.experimental import pallas as pl
from jax.experimental.pallas import tpu as pltpu
from jax.sharding import PartitionSpec as P

EPS = 1e-06
BF = jnp.bfloat16
F32 = jnp.float32
GELU_C = 0.7978845608028654
GELU_A = 0.044715
CHUNK = 16
VMEM_LIMIT = 60 * 1024 * 1024


def doc_offsets(lengths_row, rows_total):
    doc_ends = jnp.cumsum(lengths_row)
    positions = jnp.arange(rows_total, dtype=jnp.int32)
    before = (doc_ends[None, :] <= positions[:, None]).astype(jnp.int32)
    starts = jnp.sum(before * lengths_row[None, :], axis=1)
    return positions - starts


def scaled_norm(values, gain_vec):
    return (
        values
        * lax.rsqrt(jnp.mean(values * values, axis=1, keepdims=True) + EPS)
        * gain_vec[None, :]
    )


def dot_nn(left, right):
    return jnp.dot(left, right, preferred_element_type=F32)


def dot_nt(left, right):
    return lax.dot_general(left, right, (((1,), (1,)), ((), ())), preferred_element_type=F32)


def dot_tn(left, right):
    return lax.dot_general(left, right, (((0,), (0,)), ((), ())), preferred_element_type=F32)


def gelu(x):
    return 0.5 * x * (1.0 + jnp.tanh(GELU_C * (x + GELU_A * x * x * x)))


def gelu_both(x):
    square = x * x
    tanh_in = jnp.tanh(GELU_C * x * (1.0 + GELU_A * square))
    half = 0.5 * (1.0 + tanh_in)
    slope = half + 0.5 * x * (1.0 - tanh_in * tanh_in) * (GELU_C * (1.0 + 3.0 * GELU_A * square))
    return half * x, slope


def sigmoid(x):
    return 1.0 / (1.0 + jnp.exp(-x))


def one_minus_square(log_decay, carried):
    y = 2.0 * log_decay
    series = 1.0 + y * (1.0 / 7.0)
    for k in (6.0, 5.0, 4.0, 3.0, 2.0):
        series = 1.0 + y * (1.0 / k) * series
    return jnp.where(y > -0.5, -y * series, 1.0 - carried * carried)


def row_in_tile(shape):
    return lax.broadcasted_iota(jnp.int32, shape, 0) % 8


def scan_tile_down(mult, add):
    row = row_in_tile(mult.shape)
    for step in (1, 2, 4):
        keep = row >= step
        add_up = jnp.where(keep, pltpu.roll(add, step, 0), 0.0)
        mult_up = jnp.where(keep, pltpu.roll(mult, step, 0), 1.0)
        add = add + mult * add_up
        mult = mult * mult_up
    return mult, add


def scan_tile_up(mult, add):
    row = row_in_tile(mult.shape)
    for step in (1, 2, 4):
        keep = row < 8 - step
        add_dn = jnp.where(keep, pltpu.roll(add, 8 - step, 0), 0.0)
        mult_dn = jnp.where(keep, pltpu.roll(mult, 8 - step, 0), 1.0)
        add = add + mult * add_dn
        mult = mult * mult_dn
    return mult, add


V_BIAS, V_RATE, V_INLET, V_DECAY = 4, 5, 6, 7


def rec_forward(rows, vp_ref, gp_ref, mask_ref, vec_ref, rate_ref, inlet_ref,
                mixed_ref, state_ref, conv_ref, forget_ref, input_ref, low_ref):
    bias = vec_ref[V_BIAS:V_BIAS + 1, :]

    def conv_step(index, unused):
        base = pl.multiple_of(index * CHUNK, CHUNK)
        ext = vp_ref[pl.ds(base, CHUNK + 8), :]
        masks = mask_ref[pl.ds(base, CHUNK), :]
        total = bias + vec_ref[0:1, :] * ext[8:8 + CHUNK, :]
        for tap in (1, 2, 3):
            total = total + (masks[:, tap:tap + 1] * ext[8 - tap:8 - tap + CHUNK, :]) * vec_ref[tap:tap + 1, :]
        conv_ref[pl.ds(base, CHUNK), :] = total
        low_ref[pl.ds(base, CHUNK), :] = total.astype(BF)
        return unused

    lax.fori_loop(0, rows // CHUNK, conv_step, 0)
    block = 256

    def gate_step(index, unused):
        base = pl.multiple_of(index * block, block)
        low = low_ref[pl.ds(base, block), :]
        forget_ref[pl.ds(base, block), :] = dot_nn(low, rate_ref[...])
        input_ref[pl.ds(base, block), :] = dot_nn(low, inlet_ref[...])
        return unused

    lax.fori_loop(0, rows // block, gate_step, 0)
    rate_bias = vec_ref[V_RATE:V_RATE + 1, :]
    inlet_bias = vec_ref[V_INLET:V_INLET + 1, :]
    decay = vec_ref[V_DECAY:V_DECAY + 1, :]

    def scan_step(index, carry):
        base = pl.multiple_of(index * CHUNK, CHUNK)
        window = pl.ds(base, CHUNK)
        forget = sigmoid(forget_ref[window, :] + rate_bias)
        inlet = sigmoid(input_ref[window, :] + inlet_bias)
        log_decay = decay * forget
        carried = jnp.exp(log_decay)
        normalizer = jnp.sqrt(one_minus_square(log_decay, carried))
        forget_ref[window, :] = forget
        input_ref[window, :] = inlet
        add = normalizer * inlet * conv_ref[window, :]
        mult = carried * mask_ref[window, 1:2]
        pieces = []
        for tile in range(CHUNK // 8):
            m, a = scan_tile_down(mult[8 * tile:8 * tile + 8], add[8 * tile:8 * tile + 8])
            states = a + m * carry
            carry = states[7:8, :]
            pieces.append(states)
        states = jnp.concatenate(pieces, axis=0)
        state_ref[window, :] = states
        mixed_ref[window, :] = (states * gelu(gp_ref[window, :])).astype(BF)
        return carry

    lax.fori_loop(0, rows // CHUNK, scan_step, jnp.zeros((1, conv_ref.shape[1]), F32))


def rec_backward(rows, dm_ref, vp_ref, gp_ref, mask_ref, vec_ref, rate_ref, inlet_ref,
                 state_ref, conv_ref, forget_ref, input_ref,
                 vlow_ref, glow_ref, dzf_ref, dzi_ref, dconv_ref, clow_ref, sums_ref):
    columns = conv_ref.shape[1]
    decay = vec_ref[V_DECAY:V_DECAY + 1, :]
    chunks = rows // CHUNK
    zero_row = jnp.zeros((1, columns), F32)

    def scan_step(step, carry):
        grad_next, mult_next, rate_sum, inlet_sum, decay_sum = carry
        base = pl.multiple_of((chunks - 1 - step) * CHUNK, CHUNK)
        window = pl.ds(base, CHUNK)
        mixed_grad = dm_ref[window, :]
        act, slope = gelu_both(gp_ref[window, :])
        ext = state_ref[pl.ds(base, CHUNK + 8), :]
        states = ext[8:, :]
        before = ext[7:7 + CHUNK, :]
        glow_ref[window, :] = (mixed_grad * states * slope).astype(BF)
        add = mixed_grad * act
        forget = forget_ref[window, :]
        inlet = input_ref[window, :]
        conv = conv_ref[window, :]
        clow_ref[window, :] = conv.astype(BF)
        log_decay = decay * forget
        carried = jnp.exp(log_decay)
        square = one_minus_square(log_decay, carried)
        inverse = lax.rsqrt(jnp.maximum(square, 1e-30))
        normalizer = square * inverse
        mult = carried * mask_ref[window, 1:2]
        pieces = []
        for tile in reversed(range(CHUNK // 8)):
            lo = 8 * tile
            after = mult[lo + 8:lo + 9, :] if lo + 8 < CHUNK else mult_next
            shifted = jnp.concatenate([mult[lo + 1:lo + 8, :], after], axis=0)
            m, a = scan_tile_up(shifted, add[lo:lo + 8])
            grads = a + m * grad_next
            grad_next = grads[0:1, :]
            pieces.append(grads)
        grads = jnp.concatenate(pieces[::-1], axis=0)
        gated = grads * inlet
        d_log = grads * before * mult - gated * conv * ((1.0 - square) * inverse)
        d_forget = d_log * decay
        dzf = d_forget * forget * (1.0 - forget)
        dzi = grads * normalizer * conv * inlet * (1.0 - inlet)
        dzf_ref[window, :] = dzf.astype(BF)
        dzi_ref[window, :] = dzi.astype(BF)
        dconv_ref[window, :] = gated * normalizer
        return (grad_next, mult[0:1, :],
                rate_sum + jnp.sum(dzf.reshape(CHUNK // 8, 8, columns), axis=0),
                inlet_sum + jnp.sum(dzi.reshape(CHUNK // 8, 8, columns), axis=0),
                decay_sum + jnp.sum((d_log * forget).reshape(CHUNK // 8, 8, columns), axis=0))

    zeros = jnp.zeros((8, columns), F32)
    unused, unused, rate_sum, inlet_sum, decay_sum = lax.fori_loop(
        0, chunks, scan_step, (zero_row, zero_row, zeros, zeros, zeros))
    sums_ref[V_RATE:V_RATE + 1, :] = jnp.sum(rate_sum, axis=0, keepdims=True)
    sums_ref[V_INLET:V_INLET + 1, :] = jnp.sum(inlet_sum, axis=0, keepdims=True)
    sums_ref[V_DECAY:V_DECAY + 1, :] = jnp.sum(decay_sum, axis=0, keepdims=True)
    block = 256

    def gate_step(index, unused):
        base = pl.multiple_of(index * block, block)
        window = pl.ds(base, block)
        dconv_ref[window, :] += (dot_nt(dzf_ref[window, :], rate_ref[...])
                                 + dot_nt(dzi_ref[window, :], inlet_ref[...]))
        return unused

    lax.fori_loop(0, rows // block, gate_step, 0)

    def conv_step(index, carry):
        base = pl.multiple_of(index * CHUNK, CHUNK)
        window = pl.ds(base, CHUNK)
        ext = dconv_ref[pl.ds(base, CHUNK + 8), :]
        masks = mask_ref[pl.ds(base, CHUNK + 8), :]
        values = vp_ref[pl.ds(base, CHUNK + 8), :]
        here = ext[:CHUNK, :]
        total = vec_ref[0:1, :] * here
        sums = [carry[0] + fold(here * values[8:, :], columns)]
        for tap in (1, 2, 3):
            gated = ext * masks[:, tap:tap + 1]
            total = total + vec_ref[tap:tap + 1, :] * gated[tap:tap + CHUNK, :]
            sums.append(carry[tap] + fold(gated[:CHUNK, :] * values[8 - tap:8 - tap + CHUNK, :], columns))
        sums.append(carry[4] + fold(here, columns))
        vlow_ref[window, :] = total.astype(BF)
        return tuple(sums)

    sums = lax.fori_loop(0, chunks, conv_step, (zeros,) * 5)
    for row in range(5):
        sums_ref[row:row + 1, :] = jnp.sum(sums[row], axis=0, keepdims=True)


def fold(values, columns):
    return jnp.sum(values.reshape(CHUNK // 8, 8, columns), axis=0)


def forward_kernel(vp_in, gp_ref, mask_ref, vec_ref, rate_ref, inlet_ref,
                   mixed_ref, state_ref, conv_ref, forget_ref, input_ref, vp_ref, low_ref):
    rows, columns = vp_in.shape
    vp_ref[0:8, :] = jnp.zeros((8, columns), F32)
    vp_ref[8:, :] = vp_in[...]
    rec_forward(rows, vp_ref, gp_ref, mask_ref, vec_ref, rate_ref, inlet_ref,
                mixed_ref, state_ref, conv_ref, forget_ref, input_ref, low_ref)


def backward_kernel(dm_ref, vp_in, gp_ref, mask_ref, vec_ref, rate_ref, inlet_ref,
                    state_in, conv_ref, forget_ref, input_ref,
                    vlow_ref, glow_ref, rate_grad_ref, inlet_grad_ref, sums_ref,
                    vp_ref, state_ref, dzf_ref, dzi_ref, dconv_ref, clow_ref):
    rows, columns = vp_in.shape
    zeros = jnp.zeros((8, columns), F32)
    vp_ref[0:8, :] = zeros
    vp_ref[8:, :] = vp_in[...]
    state_ref[0:8, :] = zeros
    state_ref[8:, :] = state_in[...]
    dconv_ref[rows:rows + 8, :] = zeros
    rec_backward(rows, dm_ref, vp_ref, gp_ref, mask_ref, vec_ref, rate_ref, inlet_ref,
                 state_ref, conv_ref, forget_ref, input_ref,
                 vlow_ref, glow_ref, dzf_ref, dzi_ref, dconv_ref, clow_ref, sums_ref)
    rate_grad_ref[...] = dot_tn(clow_ref[...], dzf_ref[...])
    inlet_grad_ref[...] = dot_tn(clow_ref[...], dzi_ref[...])


def call_forward(vp, gp, masks, vec, rate, inlet):
    rows, columns = vp.shape
    wide = jax.ShapeDtypeStruct((rows, columns), F32)
    return pl.pallas_call(
        forward_kernel,
        out_shape=(jax.ShapeDtypeStruct((rows, columns), BF), wide, wide, wide, wide),
        scratch_shapes=[pltpu.VMEM((rows + 8, columns), F32), pltpu.VMEM((rows, columns), BF)],
        compiler_params=pltpu.CompilerParams(vmem_limit_bytes=VMEM_LIMIT),
        cost_estimate=pl.CostEstimate(flops=4 * rows * columns * columns,
                                      bytes_accessed=30 * rows * columns, transcendentals=6 * rows * columns),
    )(vp, gp, masks, vec, rate, inlet)


def call_backward(dm, vp, gp, masks, vec, rate, inlet, state, conv, forget, inp):
    rows, columns = vp.shape
    low = jax.ShapeDtypeStruct((rows, columns), BF)
    square = jax.ShapeDtypeStruct((columns, columns), F32)
    return pl.pallas_call(
        backward_kernel,
        out_shape=(low, low, square, square, jax.ShapeDtypeStruct((8, columns), F32)),
        scratch_shapes=[
            pltpu.VMEM((rows + 8, columns), F32),
            pltpu.VMEM((rows + 8, columns), F32),
            pltpu.VMEM((rows, columns), BF),
            pltpu.VMEM((rows, columns), BF),
            pltpu.VMEM((rows + 8, columns), F32),
            pltpu.VMEM((rows, columns), BF),
        ],
        compiler_params=pltpu.CompilerParams(vmem_limit_bytes=VMEM_LIMIT),
        cost_estimate=pl.CostEstimate(flops=8 * rows * columns * columns,
                                      bytes_accessed=40 * rows * columns, transcendentals=4 * rows * columns),
    )(dm, vp, gp, masks, vec, rate, inlet, state, conv, forget, inp)


MESH = pl.DeviceIdType.MESH
PARTS = 4


def greet(axis, count):
    me = lax.axis_index(axis)
    barrier = pltpu.get_barrier_semaphore()

    @pl.when(me > 0)
    def _():
        pl.semaphore_signal(barrier, inc=1, device_id={axis: me - 1}, device_id_type=MESH)

    @pl.when(me < count - 1)
    def _():
        pl.semaphore_signal(barrier, inc=1, device_id={axis: me + 1}, device_id_type=MESH)

    inner = (me > 0) & (me < count - 1)

    @pl.when(inner)
    def _():
        pl.semaphore_wait(barrier, 2)

    @pl.when(jnp.logical_not(inner))
    def _():
        pl.semaphore_wait(barrier, 1)


class Gather:
    def __init__(self, count, buf, send, recv):
        self.count, self.buf, self.send, self.recv = count, buf, send, recv
        self.me = lax.axis_index("mp")

    def copy(self, block, way):
        return pltpu.make_async_remote_copy(
            src_ref=self.buf.at[block],
            dst_ref=self.buf.at[block],
            send_sem=self.send.at[0 if way < 0 else 1, block],
            recv_sem=self.recv.at[block],
            device_id={"mp": self.me + way},
            device_id_type=MESH,
        )

    def hand_on(self, block, way):
        pl.when(self.me < self.count - 1 if way > 0 else self.me > 0)(self.copy(block, way).start)

    def start(self):
        self.hand_on(self.me, 1)
        self.hand_on(self.me, -1)

    def take(self, distance):
        low, high = self.me - distance, self.me + distance

        @pl.when(low >= 0)
        def _():
            self.copy(low, -1).wait_recv()
            self.hand_on(low, 1)

        @pl.when(high < self.count)
        def _():
            self.copy(high, 1).wait_recv()
            self.hand_on(high, -1)

    def drain(self):
        def step(block, unused):
            pl.when((block <= self.me) & (self.me < self.count - 1))(self.copy(block, 1).wait_send)
            pl.when((block >= self.me) & (self.me > 0))(self.copy(block, -1).wait_send)
            return unused

        lax.fori_loop(0, self.count, step, 0)


class Scatter:
    def __init__(self, count, held, slots, send, recv):
        self.count, self.held, self.slots, self.send, self.recv = count, held, slots, send, recv
        self.me = lax.axis_index("mp")

    def copy(self, block, part, way):
        slot = block + 1 if way > 0 else block
        return pltpu.make_async_remote_copy(
            src_ref=self.held.at[block, part],
            dst_ref=self.slots.at[slot, part],
            send_sem=self.send.at[block, part],
            recv_sem=self.recv.at[slot, part],
            device_id={"mp": self.me + way},
            device_id_type=MESH,
        )

    def first(self, block, part):
        pl.when((self.me == 0) & (block > 0))(self.copy(block, part, 1).start)
        pl.when((self.me == self.count - 1) & (block < self.count - 1))(self.copy(block, part, -1).start)

    def pass_part(self, block, part, way):
        self.arrived(block, part, way)
        slot = block + 1 if way > 0 else block
        self.held[block, part] = (
            self.held[block, part].astype(F32) + self.slots[slot, part].astype(F32)).astype(BF)
        self.copy(block, part, way).start()

    def arrived(self, block, part, way):
        slot = block + 1 if way > 0 else block
        pltpu.make_async_remote_copy(
            src_ref=self.held.at[block, part],
            dst_ref=self.slots.at[slot, part],
            send_sem=self.send.at[block, part],
            recv_sem=self.recv.at[slot, part],
            device_id={"mp": self.me - way},
            device_id_type=MESH,
        ).wait_recv()

    def pass_on(self, time):
        last = self.count - 1
        up = time + 1 - self.me
        down = last - 1 + last - self.me - time
        up_here = (self.me > 0) & (up > self.me) & (up <= last)
        down_here = (self.me < last) & (down < self.me) & (down >= 0)

        def step(part, unused):
            pl.when(up_here)(lambda: self.pass_part(up, part, 1))
            pl.when(down_here)(lambda: self.pass_part(down, part, -1))
            return unused

        lax.fori_loop(0, PARTS, step, 0)

    def total(self, part):
        pl.when(self.me > 0)(lambda: self.arrived(self.me, part, 1))
        pl.when(self.me < self.count - 1)(lambda: self.arrived(self.me, part, -1))
        below = jnp.where(self.me > 0, self.slots[self.me + 1, part].astype(F32), 0.0)
        above = jnp.where(self.me < self.count - 1, self.slots[self.me, part].astype(F32), 0.0)
        return self.held[self.me, part].astype(F32) + below + above

    def drain(self):
        def step(block, unused):
            for part in range(PARTS):
                pl.when(block > self.me)(self.copy(block, part, 1).wait_send)
                pl.when(block < self.me)(self.copy(block, part, -1).wait_send)
            return unused

        lax.fori_loop(0, self.count, step, 0)


def spans(total):
    size = 512 if total % 512 == 0 else 256
    return [slice(at, at + size) for at in range(0, total, size)]


def dense_kernel(count, groups, middle_ref, gain_ref, cot_hbm, gate_hbm, value_hbm, down_hbm,
                 middle_grad_ref, gain_grad_ref, dense_part_hbm, gate_out, value_out, down_out,
                 normed, cot, gate_w, value_w, down_w, hidden, gate_g, value_g, dense_part, held, slots, stage,
                 load_sem, cot_sem, part_sem, stage_sem, ag_send, ag_recv, rs_send, rs_recv):
    me = lax.axis_index("mp")
    rows, columns = middle_ref.shape
    units = gate_w.shape[1]
    width = columns // PARTS
    loads = [pltpu.make_async_copy(gate_hbm, gate_w, load_sem.at[0]),
             pltpu.make_async_copy(value_hbm, value_w, load_sem.at[1]),
             pltpu.make_async_copy(down_hbm, down_w, load_sem.at[2])]
    for load in loads:
        load.start()

    def cot_copy(block):
        return pltpu.make_async_copy(cot_hbm.at[pl.ds(pl.multiple_of(block * rows, rows), rows)],
                                     cot.at[block], cot_sem.at[block])

    for block in range(count):
        cot_copy(block).start()
    greet("mp", count)
    gather = Gather(count, normed, ag_send, ag_recv)
    scatter = Scatter(count, held, slots, rs_send, rs_recv)
    step_rows = 64

    def norm_step(index, unused):
        window = pl.ds(pl.multiple_of(index * step_rows, step_rows), step_rows)
        middle = middle_ref[window, :]
        scale = lax.rsqrt(jnp.mean(middle * middle, axis=1, keepdims=True) + EPS)
        normed[me, window, :] = (middle * scale * gain_ref[...]).astype(BF)
        return unused

    lax.fori_loop(0, rows // step_rows, norm_step, 0)
    gather.start()
    for load in loads:
        load.wait()
    pieces = 3
    piece = units // pieces

    def part_copy(block, slot):
        return pltpu.make_async_copy(dense_part.at[slot], dense_part_hbm.at[block], part_sem.at[slot])

    def compute(block, slot, reuse):
        cot_copy(block).wait()
        rows_in = normed[block]
        rows_cot = cot[block]
        for index in range(pieces):
            span = slice(index * piece, (index + 1) * piece)
            gate_linear = dot_nn(rows_in, gate_w[:, span])
            value_linear = dot_nn(rows_in, value_w[:, span])
            hidden_grad = dot_nt(rows_cot, down_w[span, :])
            act, slope = gelu_both(gate_linear)
            hidden[block, :, span] = (act * value_linear).astype(BF)
            gate_g[block, :, span] = (hidden_grad * value_linear * slope).astype(BF)
            value_g[block, :, span] = (hidden_grad * act).astype(BF)
        for part in range(PARTS):
            span = slice(part * width, (part + 1) * width)
            held[block, part] = (dot_nt(gate_g[block], gate_w[span, :])
                                 + dot_nt(value_g[block], value_w[span, :])).astype(BF)
            scatter.first(block, part)
        pl.when(reuse)(lambda: part_copy(block, slot).wait())
        for part in range(PARTS):
            span = slice(part * width, (part + 1) * width)
            dense_part[slot, part] = dot_nn(hidden[block], down_w[:, span]).astype(BF)
        part_copy(block, slot).start()

    def arrive(distance, unused):
        pl.when(distance > 0)(lambda: gather.take(distance))

        def side(which, inner):
            block = me - distance + 2 * distance * which
            pl.when((block >= 0) & (block < count) & ((distance > 0) | (which == 0)))(
                lambda: compute(block, which, (distance > 1) | ((distance == 1) & (which == 0))))
            return inner

        return lax.fori_loop(0, 2, side, unused)

    lax.fori_loop(0, count, arrive, 0)

    total_rows = count * rows
    left_rows = columns // 4
    unit_rows = units // 4
    group_width = columns // groups

    def stage_copy(kind, index, slot):
        if kind == 2:
            half = columns // 2
            return pltpu.make_async_copy(
                stage.at[slot, pl.ds(0, unit_rows), pl.ds(0, half)],
                down_out.at[pl.ds(index // 2 * unit_rows, unit_rows), pl.ds(index % 2 * half, half)],
                stage_sem.at[slot])
        target = gate_out if kind == 0 else value_out
        return pltpu.make_async_copy(
            stage.at[slot, pl.ds(0, left_rows), pl.ds(0, units)],
            target.at[pl.ds(index * left_rows, left_rows)], stage_sem.at[slot])

    def grads(kind, index, slot):
        if kind == 2:
            low = index // 2 * unit_rows
            left = hidden[:, :, low:low + unit_rows].reshape(total_rows, unit_rows)
            for span in spans(columns // 2):
                at = index % 2 * (columns // 2) + span.start
                size = span.stop - span.start
                right = cot[:, :, at:at + size].reshape(total_rows, size)
                stage[slot, 0:unit_rows, span] = dot_tn(left, right).astype(BF)
        else:
            left = normed[:, :, index * left_rows:(index + 1) * left_rows].reshape(total_rows, left_rows)
            source = gate_g if kind == 0 else value_g
            for span in spans(units):
                right = source[:, :, span].reshape(total_rows, span.stop - span.start)
                stage[slot, 0:left_rows, span] = dot_tn(left, right).astype(BF)

    work = [(kind, index) for kind in (0, 1, 2) for index in range((4, 4, 8)[kind])]
    started = []
    times = max(2 * count - 5, 0)
    per_step = -(-len(work) // (times + 1))
    for step in range(times + 1):
        if step > 0:
            scatter.pass_on(step + 1)
        for kind, index in work[step * per_step:(step + 1) * per_step]:
            slot = len(started) % 2
            if len(started) >= 2:
                stage_copy(*started[-2], slot).wait()
            grads(kind, index, slot)
            stage_copy(kind, index, slot).start()
            started.append((kind, index))
    for back in (2, 1):
        stage_copy(*started[-back], (len(started) - back) % 2).wait()

    dot_sum = jnp.zeros((rows, 1), F32)
    square_sum = jnp.zeros((rows, 1), F32)
    for part in range(PARTS):
        span = slice(part * width, (part + 1) * width)
        grad = scatter.total(part)
        middle = middle_ref[:, span]
        middle_grad_ref[:, span] = grad
        dot_sum = dot_sum + jnp.sum(grad * gain_ref[:, span] * middle, axis=1, keepdims=True)
        square_sum = square_sum + jnp.sum(middle * middle, axis=1, keepdims=True)
    scale = lax.rsqrt(square_sum * (1.0 / columns) + EPS)
    pull = scale * scale * scale * (dot_sum * (1.0 / columns))
    for part in range(PARTS):
        span = slice(part * width, (part + 1) * width)
        grad = middle_grad_ref[:, span]
        middle = middle_ref[:, span]
        gain_grad_ref[:, span] = jnp.sum(grad * middle * scale, axis=0, keepdims=True)
        result = cot[me, :, span].astype(F32) + scale * (grad * gain_ref[:, span]) - middle * pull
        middle_grad_ref[:, span] = result
    part_copy(0, 0).wait()
    pl.when(me < count - 1)(part_copy(0, 1).wait)
    gather.drain()
    scatter.drain()


def call_dense(count, groups, middle, gain, cot_all, dense_gate, dense_value, dense_down):
    rows, columns = middle.shape
    units = dense_gate.shape[1]
    width = columns // PARTS
    any_spec = pl.BlockSpec(memory_space=pl.ANY)
    vmem = pl.BlockSpec(memory_space=pltpu.VMEM)
    dma = pltpu.SemaphoreType.DMA
    return pl.pallas_call(
        functools.partial(dense_kernel, count, groups),
        out_shape=(
            jax.ShapeDtypeStruct((rows, columns), F32),
            jax.ShapeDtypeStruct((1, columns), F32),
            jax.ShapeDtypeStruct((count, PARTS, rows, width), BF),
            jax.ShapeDtypeStruct((columns, units), BF),
            jax.ShapeDtypeStruct((columns, units), BF),
            jax.ShapeDtypeStruct((units, columns), BF),
        ),
        in_specs=[vmem, vmem, any_spec, any_spec, any_spec, any_spec],
        out_specs=(vmem, vmem, any_spec, any_spec, any_spec, any_spec),
        scratch_shapes=[
            pltpu.VMEM((count, rows, columns), BF),
            pltpu.VMEM((count, rows, columns), BF),
            pltpu.VMEM((columns, units), BF),
            pltpu.VMEM((columns, units), BF),
            pltpu.VMEM((units, columns), BF),
            pltpu.VMEM((count, rows, units), BF),
            pltpu.VMEM((count, rows, units), BF),
            pltpu.VMEM((count, rows, units), BF),
            pltpu.VMEM((2, PARTS, rows, width), BF),
            pltpu.VMEM((count, PARTS, rows, width), BF),
            pltpu.VMEM((count + 1, PARTS, rows, width), BF),
            pltpu.VMEM((2, columns // 4, max(units, columns // 2)), BF),
            dma((3,)), dma((count,)), dma((2,)), dma((2,)),
            dma((2, count)), dma((count,)), dma((count, PARTS)), dma((count + 1, PARTS)),
        ],
        compiler_params=pltpu.CompilerParams(
            vmem_limit_bytes=VMEM_LIMIT, collective_id=0, has_side_effects=True),
        cost_estimate=pl.CostEstimate(flops=18 * count * rows * columns * units,
                                      bytes_accessed=12 * columns * units, transcendentals=count * rows * units),
    )(middle, gain, cot_all, dense_gate, dense_value, dense_down)


def block_diagonal(heads):
    count, width, unused = heads.shape
    spread = heads[:, :, None, :] * jnp.eye(count, dtype=heads.dtype)[:, None, :, None]
    return spread.reshape(count * width, count * width)


def diagonal_blocks(square, count):
    width = square.shape[0] // count
    return jnp.stack([square[h * width:(h + 1) * width, h * width:(h + 1) * width] for h in range(count)])


def scatter_mp(values):
    return lax.psum_scatter(values.astype(BF), "mp", scatter_dimension=0, tiled=True).astype(F32)


def scatter_dp(values, dimension):
    return lax.psum_scatter(values.astype(BF), "dp", scatter_dimension=dimension, tiled=True).astype(F32)


def local(groups, tokens, cotangent, lengths, live_mask, mixer_gain, value_proj, gate_proj, conv_taps, conv_bias,
          rate_weight, rate_bias, inlet_weight, inlet_bias, decay_param, mixer_out, dense_gain,
          dense_gate, dense_value, dense_down):
    residual = tokens.astype(F32)
    columns = residual.shape[1]
    head_count = rate_weight.shape[0]
    normed_first, norm_back_in = jax.vjp(scaled_norm, residual, mixer_gain)
    normed_all = lax.all_gather(normed_first.astype(BF), "mp", axis=0, tiled=True)
    rows_total = normed_all.shape[0]
    offsets = doc_offsets(lengths[0], rows_total)
    taps_here = jnp.arange(8, dtype=jnp.int32)
    masks = (offsets[:, None] >= taps_here[None, :]).astype(F32)
    masks_ext = jnp.concatenate([masks, jnp.zeros((8, 8), F32)], axis=0)
    vec = jnp.concatenate([
        conv_taps,
        jnp.stack([conv_bias, rate_bias, inlet_bias, -8.0 * jax.nn.softplus(-decay_param)]),
    ], axis=0)
    rate_square = block_diagonal(rate_weight).astype(BF)
    inlet_square = block_diagonal(inlet_weight).astype(BF)
    value_pre = dot_nn(normed_all, value_proj)
    gate_pre = dot_nn(normed_all, gate_proj)
    mixed_act, states, convolved, forget_gate, input_gate = call_forward(
        value_pre, gate_pre, masks_ext, vec, rate_square, inlet_square)
    mixer_part = scatter_mp(dot_nn(mixed_act, mixer_out))
    middle = residual + mixer_part
    block_rows = lax.all_gather(cotangent, "mp", axis=0, tiled=True)
    count = rows_total // tokens.shape[0]
    middle_grad, dense_gain_grad, dense_terms, dense_gate_grad, dense_value_grad, down_grad = call_dense(
        count, groups, middle, dense_gain[None, :], block_rows, dense_gate, dense_value, dense_down)
    dense_gain_grad = dense_gain_grad[0]
    middle_low = middle_grad.astype(BF)
    dense_part = lax.psum_scatter(dense_terms, "mp", scatter_dimension=0, tiled=True)[0].astype(F32)
    dense_part = dense_part.transpose(1, 0, 2).reshape(tokens.shape)
    layer_out = (middle + dense_part).astype(BF)
    weights_live = live_mask.astype(F32)
    squares = jnp.stack([
        jnp.sum(weights_live * jnp.sum(residual * residual, axis=1)),
        jnp.sum(weights_live * jnp.sum(mixer_part * mixer_part, axis=1)),
        jnp.sum(weights_live * jnp.sum(dense_part * dense_part, axis=1)),
    ])
    live_count = jnp.sum(weights_live)
    middle_rows = lax.all_gather(middle_low, "mp", axis=0, tiled=True)
    mixed_grad = dot_nt(middle_rows, mixer_out)
    mixer_out_grad = dot_tn(mixed_act, middle_rows)
    value_low, gate_low, rate_sq, inlet_sq, vec_grad = call_backward(
        mixed_grad, value_pre, gate_pre, masks_ext, vec, rate_square, inlet_square,
        states, convolved, forget_gate, input_gate)
    normed_in_grad = scatter_mp(dot_nt(value_low, value_proj) + dot_nt(gate_low, gate_proj))
    value_proj_grad = dot_tn(normed_all, value_low)
    gate_proj_grad = dot_tn(normed_all, gate_low)
    input_norm_grad, mixer_gain_grad = norm_back_in(normed_in_grad)
    input_grad = (middle_grad + input_norm_grad).astype(BF)
    small = (vec_grad, diagonal_blocks(rate_sq, head_count), diagonal_blocks(inlet_sq, head_count))
    vec_sum, rate_sum, inlet_sum = lax.psum(small, "dp")
    decay_scale = 8.0 * jax.nn.sigmoid(-decay_param)
    mixer_gain_sum, dense_gain_sum, squares, live_count = lax.psum(
        (mixer_gain_grad, dense_gain_grad, squares, live_count), ("dp", "mp"))
    branch_rms = jnp.sqrt(squares / (live_count * columns))
    return (
        layer_out,
        input_grad,
        mixer_gain_sum,
        scatter_dp(value_proj_grad, 0),
        scatter_dp(gate_proj_grad, 0),
        vec_sum[0:4],
        vec_sum[4],
        rate_sum,
        vec_sum[V_RATE],
        inlet_sum,
        vec_sum[V_INLET],
        vec_sum[V_DECAY] * decay_scale,
        scatter_dp(mixer_out_grad, 1),
        dense_gain_sum,
        scatter_dp(dense_gate_grad, 0),
        scatter_dp(dense_value_grad, 0),
        scatter_dp(down_grad, 1),
        branch_rms,
    )


def solution(mesh):
    rows = P(("dp", "mp"), None)
    return jax.shard_map(
        functools.partial(local, mesh.shape["dp"]),
        mesh=mesh,
        in_specs=(
            rows, rows, P("dp", None), P(("dp", "mp")), P(),
            P(None, "mp"), P(None, "mp"), P(None, "mp"), P("mp"),
            P("mp", None, None), P("mp"), P("mp", None, None), P("mp"), P("mp"),
            P("mp", None), P(), P(None, "mp"), P(None, "mp"), P("mp", None),
        ),
        out_specs=(
            rows, rows, P(), P("dp", "mp"), P("dp", "mp"),
            P(None, "mp"), P("mp"), P("mp", None, None), P("mp"), P("mp", None, None), P("mp"), P("mp"),
            P("mp", "dp"), P(), P("dp", "mp"), P("dp", "mp"), P("mp", "dp"), P(),
        ),
        check_vma=False,
    )
```

```python
import functools

import jax
import jax.numpy as jnp
from jax import lax
from jax.experimental import pallas as pl
from jax.experimental.pallas import tpu as pltpu
from jax.sharding import PartitionSpec as P

EPS = 1e-06
BF = jnp.bfloat16
F32 = jnp.float32
GELU_C = 0.7978845608028654
GELU_A = 0.044715
CHUNK = 16
VMEM_LIMIT = 60 * 1024 * 1024


def doc_offsets(lengths_row, rows_total):
    doc_ends = jnp.cumsum(lengths_row)
    positions = jnp.arange(rows_total, dtype=jnp.int32)
    before = (doc_ends[None, :] <= positions[:, None]).astype(jnp.int32)
    starts = jnp.sum(before * lengths_row[None, :], axis=1)
    return positions - starts


def dot_nn(left, right):
    return jnp.dot(left, right, preferred_element_type=F32)


def dot_nt(left, right):
    return lax.dot_general(left, right, (((1,), (1,)), ((), ())), preferred_element_type=F32)


def dot_tn(left, right):
    return lax.dot_general(left, right, (((0,), (0,)), ((), ())), preferred_element_type=F32)


def gelu(x):
    return 0.5 * x * (1.0 + jnp.tanh(GELU_C * (x + GELU_A * x * x * x)))


def gelu_both(x):
    square = x * x
    tanh_in = jnp.tanh(GELU_C * x * (1.0 + GELU_A * square))
    half = 0.5 * (1.0 + tanh_in)
    slope = half + 0.5 * x * (1.0 - tanh_in * tanh_in) * (GELU_C * (1.0 + 3.0 * GELU_A * square))
    return half * x, slope


def sigmoid(x):
    return 1.0 / (1.0 + jnp.exp(-x))


def one_minus_square(log_decay, carried):
    y = 2.0 * log_decay
    series = 1.0 + y * (1.0 / 7.0)
    for k in (6.0, 5.0, 4.0, 3.0, 2.0):
        series = 1.0 + y * (1.0 / k) * series
    return jnp.where(y > -0.5, -y * series, 1.0 - carried * carried)


def row_in_tile(shape):
    return lax.broadcasted_iota(jnp.int32, shape, 0) % 8


def scan_tile_down(mult, add):
    row = row_in_tile(mult.shape)
    for step in (1, 2, 4):
        keep = row >= step
        add_up = jnp.where(keep, pltpu.roll(add, step, 0), 0.0)
        mult_up = jnp.where(keep, pltpu.roll(mult, step, 0), 1.0)
        add = add + mult * add_up
        mult = mult * mult_up
    return mult, add


def scan_tile_up(mult, add):
    row = row_in_tile(mult.shape)
    for step in (1, 2, 4):
        keep = row < 8 - step
        add_dn = jnp.where(keep, pltpu.roll(add, 8 - step, 0), 0.0)
        mult_dn = jnp.where(keep, pltpu.roll(mult, 8 - step, 0), 1.0)
        add = add + mult * add_dn
        mult = mult * mult_dn
    return mult, add


V_BIAS, V_RATE, V_INLET, V_DECAY = 4, 5, 6, 7


def fold(values, columns):
    return jnp.sum(values.reshape(values.shape[0] // 8, 8, columns), axis=0)


def rec_forward(base, rows, vp_ref, gp_ref, mask_ref, vec_ref, rate_ref, inlet_ref,
                mixed_ref, state_ref, conv_ref, forget_ref, input_ref, low_ref, carry_ref):
    bias = vec_ref[V_BIAS:V_BIAS + 1, :]

    def conv_step(index, unused):
        at = pl.multiple_of(base + index * CHUNK, CHUNK)
        ext = vp_ref[pl.ds(at, CHUNK + 8), :]
        masks = mask_ref[pl.ds(at, CHUNK), :]
        total = bias + vec_ref[0:1, :] * ext[8:8 + CHUNK, :]
        for tap in (1, 2, 3):
            total = total + (masks[:, tap:tap + 1] * ext[8 - tap:8 - tap + CHUNK, :]) * vec_ref[tap:tap + 1, :]
        conv_ref[pl.ds(at, CHUNK), :] = total
        low_ref[pl.ds(pl.multiple_of(index * CHUNK, CHUNK), CHUNK), :] = total.astype(BF)
        return unused

    lax.fori_loop(0, rows // CHUNK, conv_step, 0)
    block = pl.ds(pl.multiple_of(base, rows), rows)
    forget_ref[block, :] = dot_nn(low_ref[...], rate_ref[...])
    input_ref[block, :] = dot_nn(low_ref[...], inlet_ref[...])
    rate_bias = vec_ref[V_RATE:V_RATE + 1, :]
    inlet_bias = vec_ref[V_INLET:V_INLET + 1, :]
    decay = vec_ref[V_DECAY:V_DECAY + 1, :]

    def scan_step(index, carry):
        at = pl.multiple_of(base + index * CHUNK, CHUNK)
        window = pl.ds(at, CHUNK)
        forget = sigmoid(forget_ref[window, :] + rate_bias)
        inlet = sigmoid(input_ref[window, :] + inlet_bias)
        log_decay = decay * forget
        carried = jnp.exp(log_decay)
        normalizer = jnp.sqrt(one_minus_square(log_decay, carried))
        forget_ref[window, :] = forget
        input_ref[window, :] = inlet
        add = normalizer * inlet * conv_ref[window, :]
        mult = carried * mask_ref[window, 1:2]
        pieces = []
        for tile in range(CHUNK // 8):
            m, a = scan_tile_down(mult[8 * tile:8 * tile + 8], add[8 * tile:8 * tile + 8])
            states = a + m * carry
            carry = states[7:8, :]
            pieces.append(states)
        states = jnp.concatenate(pieces, axis=0)
        state_ref[pl.ds(at + 8, CHUNK), :] = states
        mixed_ref[window, :] = (states * gelu(gp_ref[window, :])).astype(BF)
        return carry

    carry_ref[0:1, :] = lax.fori_loop(0, rows // CHUNK, scan_step, carry_ref[0:1, :])


def rec_backward(base, rows, dm_ref, vp_ref, gp_ref, mask_ref, vec_ref, rate_ref, inlet_ref,
                 state_ref, conv_ref, forget_ref, input_ref,
                 vlow_ref, glow_ref, dzf_ref, dzi_ref, dconv_ref, clow_ref, sums_ref, carry_ref):
    columns = conv_ref.shape[1]
    decay = vec_ref[V_DECAY:V_DECAY + 1, :]
    chunks = rows // CHUNK

    def scan_step(step, carry):
        grad_next, mult_next, rate_sum, inlet_sum, decay_sum = carry
        low = pl.multiple_of((chunks - 1 - step) * CHUNK, CHUNK)
        here = pl.ds(low, CHUNK)
        window = pl.ds(pl.multiple_of(base + low, CHUNK), CHUNK)
        mixed_grad = dm_ref[here, :]
        act, slope = gelu_both(gp_ref[here, :])
        ext = state_ref[pl.ds(low, CHUNK + 8), :]
        states = ext[8:, :]
        before = ext[7:7 + CHUNK, :]
        glow_ref[window, :] = (mixed_grad * states * slope).astype(BF)
        add = mixed_grad * act
        forget = forget_ref[here, :]
        inlet = input_ref[here, :]
        conv = conv_ref[here, :]
        clow_ref[window, :] = conv.astype(BF)
        log_decay = decay * forget
        carried = jnp.exp(log_decay)
        square = one_minus_square(log_decay, carried)
        inverse = lax.rsqrt(jnp.maximum(square, 1e-30))
        normalizer = square * inverse
        mult = carried * mask_ref[window, 1:2]
        pieces = []
        for tile in reversed(range(CHUNK // 8)):
            lo = 8 * tile
            after = mult[lo + 8:lo + 9, :] if lo + 8 < CHUNK else mult_next
            shifted = jnp.concatenate([mult[lo + 1:lo + 8, :], after], axis=0)
            m, a = scan_tile_up(shifted, add[lo:lo + 8])
            grads = a + m * grad_next
            grad_next = grads[0:1, :]
            pieces.append(grads)
        grads = jnp.concatenate(pieces[::-1], axis=0)
        gated = grads * inlet
        d_log = grads * before * mult - gated * conv * ((1.0 - square) * inverse)
        dzf = d_log * decay * forget * (1.0 - forget)
        dzi = grads * normalizer * conv * inlet * (1.0 - inlet)
        dzf_ref[window, :] = dzf.astype(BF)
        dzi_ref[window, :] = dzi.astype(BF)
        dconv_ref[here, :] = gated * normalizer
        return (grad_next, mult[0:1, :], rate_sum + fold(dzf, columns), inlet_sum + fold(dzi, columns),
                decay_sum + fold(d_log * forget, columns))

    grad_next, mult_next, rate_sum, inlet_sum, decay_sum = lax.fori_loop(
        0, chunks, scan_step,
        (carry_ref[0:1, :], carry_ref[1:2, :], sums_ref[V_RATE], sums_ref[V_INLET], sums_ref[V_DECAY]))
    carry_ref[0:1, :] = grad_next
    carry_ref[1:2, :] = mult_next
    sums_ref[V_RATE] = rate_sum
    sums_ref[V_INLET] = inlet_sum
    sums_ref[V_DECAY] = decay_sum
    block = pl.ds(pl.multiple_of(base, rows), rows)
    dconv_ref[0:rows, :] += dot_nt(dzf_ref[block, :], rate_ref[...]) + dot_nt(dzi_ref[block, :], inlet_ref[...])

    def conv_step(index, carry):
        low = pl.multiple_of(index * CHUNK, CHUNK)
        at = pl.multiple_of(base + low, CHUNK)
        ext = dconv_ref[pl.ds(low, CHUNK + 8), :]
        masks = mask_ref[pl.ds(at, CHUNK + 8), :]
        values = vp_ref[pl.ds(low, CHUNK + 8), :]
        here = ext[:CHUNK, :]
        total = vec_ref[0:1, :] * here
        sums = [carry[0] + fold(here * values[8:, :], columns)]
        for tap in (1, 2, 3):
            gated = ext * masks[:, tap:tap + 1]
            total = total + vec_ref[tap:tap + 1, :] * gated[tap:tap + CHUNK, :]
            sums.append(carry[tap] + fold(gated[:CHUNK, :] * values[8 - tap:8 - tap + CHUNK, :], columns))
        sums.append(carry[4] + fold(here, columns))
        vlow_ref[pl.ds(at, CHUNK), :] = total.astype(BF)
        return tuple(sums)

    sums = lax.fori_loop(0, chunks, conv_step, tuple(sums_ref[row] for row in range(5)))
    for row in range(5):
        sums_ref[row] = sums[row]
    dconv_ref[rows:rows + 8, :] = dconv_ref[0:8, :]


MESH = pl.DeviceIdType.MESH
PARTS = 4


IN_VMEM = pl.BlockSpec(memory_space=pltpu.VMEM)
ANYWHERE = pl.BlockSpec(memory_space=pl.ANY)
DMA = pltpu.SemaphoreType.DMA


def greet(count, groups=1):
    me = lax.axis_index("mp")
    barrier = pltpu.get_barrier_semaphore()

    @pl.when(me > 0)
    def _():
        pl.semaphore_signal(barrier, inc=1, device_id={"mp": me - 1}, device_id_type=MESH)

    @pl.when(me < count - 1)
    def _():
        pl.semaphore_signal(barrier, inc=1, device_id={"mp": me + 1}, device_id_type=MESH)

    levels = groups.bit_length() - 1
    for bit in range(levels):
        pl.semaphore_signal(barrier, inc=1, device_id={"dp": partner_of(bit)}, device_id_type=MESH)
    inner = (me > 0) & (me < count - 1)

    @pl.when(inner)
    def _():
        pl.semaphore_wait(barrier, 2 + levels)

    @pl.when(jnp.logical_not(inner))
    def _():
        pl.semaphore_wait(barrier, 1 + levels)


def bit_of(value, bit):
    return (value // (1 << bit)) % 2


def partner_of(bit):
    me = lax.axis_index("dp")
    return me + (1 << bit) * (1 - 2 * bit_of(me, bit))


class Cube:
    def __init__(self, count, order, held, slots, send, recv):
        self.count, self.order, self.held, self.slots, self.send, self.recv = count, order, held, slots, send, recv
        self.me = lax.axis_index("dp")

    def places(self, level):
        total = self.count >> (level + 1)
        start = self.count - (self.count >> level)
        return [(index, start + index) for index in range(total)]

    def chunk(self, level, index, mine):
        at = 0
        for rank, bit in enumerate(self.order):
            own = bit_of(self.me, bit)
            if rank < level:
                at = at + own * (1 << bit)
            elif rank == level:
                at = at + (own if mine else 1 - own) * (1 << bit)
            else:
                at = at + ((index >> (rank - level - 1)) & 1) * (1 << bit)
        return at

    def copy(self, level, index, slot):
        return pltpu.make_async_remote_copy(
            src_ref=self.held.at[self.chunk(level, index, False)],
            dst_ref=self.slots.at[slot],
            send_sem=self.send.at[slot],
            recv_sem=self.recv.at[slot],
            device_id={"dp": partner_of(self.order[level])},
            device_id_type=MESH,
        )

    def start(self, level):
        for index, slot in self.places(level):
            self.copy(level, index, slot).start()

    def finish(self, level):
        for index, slot in self.places(level):
            self.copy(level, index, slot).wait()
            chunk = self.chunk(level, index, True)
            if level < len(self.order) - 1:
                self.held[chunk] = (
                    self.held[chunk].astype(F32) + self.slots[slot].astype(F32)).astype(self.held.dtype)

    def result(self):
        return self.held[self.me].astype(F32) + self.slots[self.count - 2].astype(F32)


class Spread:
    def __init__(self, cube, full, send, recv):
        self.cube, self.full, self.send, self.recv = cube, full, send, recv

    def copy(self, level, index, slot, mine=True):
        chunk = self.cube.chunk(level, index, mine)
        return pltpu.make_async_remote_copy(
            src_ref=self.full.at[chunk],
            dst_ref=self.full.at[chunk],
            send_sem=self.send.at[slot],
            recv_sem=self.recv.at[slot],
            device_id={"dp": partner_of(self.cube.order[level])},
            device_id_type=MESH,
        )

    def start(self, level):
        for index, slot in self.cube.places(level):
            self.copy(level, index, slot).start()

    def finish(self, level):
        for index, slot in self.cube.places(level):
            self.copy(level, index, slot).wait_send()
            self.copy(level, index, slot, False).wait_recv()


def orders(groups):
    bits = list(range(groups.bit_length() - 1))
    return bits, bits[:1] + bits[:0:-1]


class Gather:
    def __init__(self, count, buf, send, recv):
        self.count, self.buf, self.send, self.recv = count, buf, send, recv
        self.me = lax.axis_index("mp")

    def copy(self, block, way):
        return pltpu.make_async_remote_copy(
            src_ref=self.buf.at[block],
            dst_ref=self.buf.at[block],
            send_sem=self.send.at[0 if way < 0 else 1, block],
            recv_sem=self.recv.at[block],
            device_id={"mp": self.me + way},
            device_id_type=MESH,
        )

    def hand_on(self, block, way):
        pl.when(self.me < self.count - 1 if way > 0 else self.me > 0)(self.copy(block, way).start)

    def start(self):
        self.hand_on(self.me, 1)
        self.hand_on(self.me, -1)

    def take(self, distance):
        low, high = self.me - distance, self.me + distance

        @pl.when(low >= 0)
        def _():
            self.copy(low, -1).wait_recv()
            self.hand_on(low, 1)

        @pl.when(high < self.count)
        def _():
            self.copy(high, 1).wait_recv()
            self.hand_on(high, -1)

    def drain(self):
        def step(block, unused):
            pl.when((block <= self.me) & (self.me < self.count - 1))(self.copy(block, 1).wait_send)
            pl.when((block >= self.me) & (self.me > 0))(self.copy(block, -1).wait_send)
            return unused

        lax.fori_loop(0, self.count, step, 0)


class Scatter:
    def __init__(self, count, held, slots, send, recv):
        self.count, self.held, self.slots, self.send, self.recv = count, held, slots, send, recv
        self.me = lax.axis_index("mp")

    def copy(self, block, part, way):
        slot = block + 1 if way > 0 else block
        return pltpu.make_async_remote_copy(
            src_ref=self.held.at[block, part],
            dst_ref=self.slots.at[slot, part],
            send_sem=self.send.at[block, part],
            recv_sem=self.recv.at[slot, part],
            device_id={"mp": self.me + way},
            device_id_type=MESH,
        )

    def times(self):
        return range(1, 2 * self.count - 3)

    def first(self, block, part):
        pl.when((self.me == 0) & (block > 0))(self.copy(block, part, 1).start)
        pl.when((self.me == self.count - 1) & (block < self.count - 1))(self.copy(block, part, -1).start)

    def pass_part(self, block, part, way):
        self.arrived(block, part, way)
        slot = block + 1 if way > 0 else block
        self.held[block, part] = (
            self.held[block, part].astype(F32) + self.slots[slot, part].astype(F32)).astype(BF)
        self.copy(block, part, way).start()

    def arrived(self, block, part, way):
        slot = block + 1 if way > 0 else block
        pltpu.make_async_remote_copy(
            src_ref=self.held.at[block, part],
            dst_ref=self.slots.at[slot, part],
            send_sem=self.send.at[block, part],
            recv_sem=self.recv.at[slot, part],
            device_id={"mp": self.me - way},
            device_id_type=MESH,
        ).wait_recv()

    def pass_on(self, time, up_near, down_near):
        last = self.count - 1
        up = time + 1 - self.me if up_near else last + self.me - time
        down = 2 * last - 1 - self.me - time if down_near else time - last + self.me
        up_here = (self.me > 0) & (up > self.me) & (up <= last)
        down_here = (self.me < last) & (down < self.me) & (down >= 0)

        def step(part, unused):
            pl.when(up_here)(lambda: self.pass_part(up, part, 1))
            pl.when(down_here)(lambda: self.pass_part(down, part, -1))
            return unused

        lax.fori_loop(0, PARTS, step, 0)

    def wait_total(self, part):
        pl.when(self.me > 0)(lambda: self.arrived(self.me, part, 1))
        pl.when(self.me < self.count - 1)(lambda: self.arrived(self.me, part, -1))

    def total(self, part):
        below = jnp.where(self.me > 0, self.slots[self.me + 1, part].astype(F32), 0.0)
        above = jnp.where(self.me < self.count - 1, self.slots[self.me, part].astype(F32), 0.0)
        return self.held[self.me, part].astype(F32) + below + above

    def drain(self):
        def step(block, unused):
            for part in range(PARTS):
                pl.when(block > self.me)(self.copy(block, part, 1).wait_send)
                pl.when(block < self.me)(self.copy(block, part, -1).wait_send)
            return unused

        lax.fori_loop(0, self.count, step, 0)


def norm_rows(source_ref, gain_ref, target_ref):
    step_rows = 64

    def step(index, unused):
        window = pl.ds(pl.multiple_of(index * step_rows, step_rows), step_rows)
        values = source_ref[window, :].astype(F32)
        scale = lax.rsqrt(jnp.mean(values * values, axis=1, keepdims=True) + EPS)
        target_ref[window, :] = (values * scale * gain_ref[...]).astype(BF)
        return unused

    lax.fori_loop(0, source_ref.shape[0] // step_rows, step, 0)


def norm_back(values_ref, gain_ref, scatter, gain_grad_ref, write):
    rows, columns = values_ref.shape
    width = columns // PARTS
    dot_sum = jnp.zeros((rows, 1), F32)
    square_sum = jnp.zeros((rows, 1), F32)
    for part in range(PARTS):
        span = slice(part * width, (part + 1) * width)
        scatter.wait_total(part)
        grad = scatter.total(part)
        values = values_ref[:, span].astype(F32)
        dot_sum = dot_sum + jnp.sum(grad * gain_ref[:, span] * values, axis=1, keepdims=True)
        square_sum = square_sum + jnp.sum(values * values, axis=1, keepdims=True)
    scale = lax.rsqrt(square_sum * (1.0 / columns) + EPS)
    pull = scale * scale * scale * (dot_sum * (1.0 / columns))
    for part in range(PARTS):
        span = slice(part * width, (part + 1) * width)
        grad = scatter.total(part)
        values = values_ref[:, span].astype(F32)
        gain_grad_ref[:, span] = jnp.sum(grad * values * scale, axis=0, keepdims=True)
        write(span, scale * (grad * gain_ref[:, span]) - values * pull)


def live_squares(live_ref, row_sums, stat_ref):
    stat_ref[...] = jnp.zeros(stat_ref.shape, F32) + jnp.sum(live_ref[...] * row_sums, axis=0, keepdims=True)


def mixer_kernel(count, tokens_ref, gain_ref, live_ref, mask_ref, vec_ref, rate_ref, inlet_ref,
                 cot_hbm, value_hbm, gate_hbm, out_hbm,
                 middle_ref, stat_ref, normed_all, cot_all, mixed_out, vp_out, gp_out, state_out, conv_out,
                 forget_out, input_out,
                 normed, value_w, gate_w, out_w, vp, gp, mixed, state, conv, forget, inlet_gate, low, carry, held,
                 slots, load_sem, own_sem, out_sem, block_sem, ag_send, ag_recv, cot_send, cot_recv, rs_send, rs_recv):
    me = lax.axis_index("mp")
    rows, columns = tokens_ref.shape
    channels = value_w.shape[1]
    width = columns // PARTS
    own_copy = pltpu.make_async_copy(cot_hbm, cot_all.at[me], own_sem)
    own_copy.start()
    loads = [pltpu.make_async_copy(source, target, load_sem.at[index]) for index, (source, target) in enumerate(
        ((value_hbm, value_w), (gate_hbm, gate_w), (out_hbm, out_w)))]
    for load in loads:
        load.start()
    norm_rows(tokens_ref, gain_ref, normed.at[me])
    greet(count)
    gather = Gather(count, normed, ag_send, ag_recv)
    cots = Gather(count, cot_all, cot_send, cot_recv)
    scatter = Scatter(count, held, slots, rs_send, rs_recv)
    gather.start()
    zeros = jnp.zeros((8, channels), F32)
    vp[0:8, :] = zeros
    state[0:8, :] = zeros
    carry[...] = zeros
    own_copy.wait()
    for load in loads:
        load.wait()

    def block_copy(block):
        return pltpu.make_async_copy(normed.at[block], normed_all.at[block], block_sem.at[block])

    def project(block):
        block_copy(block).start()
        rows_in = normed[block]
        vp[pl.ds(pl.multiple_of(block * rows + 8, 8), rows), :] = dot_nn(rows_in, value_w[...])
        gp[pl.ds(pl.multiple_of(block * rows, rows), rows), :] = dot_nn(rows_in, gate_w[...])

    def arrive(distance, unused):
        pl.when(distance > 0)(lambda: gather.take(distance))

        def side(which, inner):
            block = me - distance + 2 * distance * which
            pl.when((block >= 0) & (block < count) & ((distance > 0) | (which == 0)))(lambda: project(block))
            return inner

        return lax.fori_loop(0, 2, side, unused)

    lax.fori_loop(0, count, arrive, 0)
    cots.start()

    def mix(block, unused):
        base = block * rows
        rec_forward(base, rows, vp, gp, mask_ref, vec_ref, rate_ref, inlet_ref,
                    mixed, state, conv, forget, inlet_gate, low, carry)
        rows_in = mixed[pl.ds(pl.multiple_of(base, rows), rows), :]
        for part in range(PARTS):
            held[block, part] = dot_nn(rows_in, out_w[:, part * width:(part + 1) * width]).astype(BF)
            scatter.first(block, part)
        return unused

    lax.fori_loop(0, count, mix, 0)
    saves = [pltpu.make_async_copy(source, target, out_sem.at[index]) for index, (source, target) in enumerate(
        ((mixed, mixed_out), (vp, vp_out), (gp, gp_out), (state, state_out), (conv, conv_out),
         (forget, forget_out), (inlet_gate, input_out)))]
    for save in saves:
        save.start()
    taken = 1
    for time in scatter.times():
        if taken < count and time >= 2 * taken - 1:
            cots.take(taken)
            taken += 1
        scatter.pass_on(time, True, False)
    for distance in range(taken, count):
        cots.take(distance)
    row_sums = jnp.zeros((rows, 1), F32)
    for part in range(PARTS):
        span = slice(part * width, (part + 1) * width)
        scatter.wait_total(part)
        total = scatter.total(part)
        row_sums = row_sums + jnp.sum(total * total, axis=1, keepdims=True)
        middle_ref[:, span] = tokens_ref[:, span].astype(F32) + total
    live_squares(live_ref, row_sums, stat_ref)
    for save in saves:
        save.wait()
    for block in range(count):
        block_copy(block).wait()
    gather.drain()
    cots.drain()
    scatter.drain()


def call_mixer(count, tokens, gain, live, masks, vec, rate, inlet, cotangent, value_proj, gate_proj, mixer_out):
    rows, columns = tokens.shape
    channels = value_proj.shape[1]
    total = count * rows
    wide = jax.ShapeDtypeStruct((total, channels), F32)
    ahead = jax.ShapeDtypeStruct((total + 8, channels), F32)
    blocks = jax.ShapeDtypeStruct((count, rows, columns), BF)
    return pl.pallas_call(
        functools.partial(mixer_kernel, count),
        out_shape=(
            jax.ShapeDtypeStruct((rows, columns), F32), jax.ShapeDtypeStruct((8, 128), F32),
            blocks, blocks, jax.ShapeDtypeStruct((total, channels), BF), ahead, wide, ahead, wide, wide, wide,
        ),
        in_specs=[IN_VMEM] * 7 + [ANYWHERE] * 4,
        out_specs=(IN_VMEM,) * 2 + (ANYWHERE,) * 9,
        scratch_shapes=[
            pltpu.VMEM((count, rows, columns), BF),
            pltpu.VMEM((columns, channels), BF),
            pltpu.VMEM((columns, channels), BF),
            pltpu.VMEM((channels, columns), BF),
            pltpu.VMEM((total + 8, channels), F32),
            pltpu.VMEM((total, channels), F32),
            pltpu.VMEM((total, channels), BF),
            pltpu.VMEM((total + 8, channels), F32),
            pltpu.VMEM((total, channels), F32),
            pltpu.VMEM((total, channels), F32),
            pltpu.VMEM((total, channels), F32),
            pltpu.VMEM((rows, channels), BF),
            pltpu.VMEM((8, channels), F32),
            pltpu.VMEM((count, PARTS, rows, columns // PARTS), BF),
            pltpu.VMEM((count + 1, PARTS, rows, columns // PARTS), BF),
            DMA((3,)), DMA, DMA((7,)), DMA((count,)),
            DMA((2, count)), DMA((count,)), DMA((2, count)), DMA((count,)),
            DMA((count, PARTS)), DMA((count + 1, PARTS)),
        ],
        compiler_params=pltpu.CompilerParams(vmem_limit_bytes=VMEM_LIMIT, collective_id=1, has_side_effects=True),
        cost_estimate=pl.CostEstimate(flops=6 * total * columns * channels, bytes_accessed=40 * total * channels,
                                      transcendentals=6 * total * channels),
    )(tokens, gain, live, masks, vec, rate, inlet, cotangent, value_proj, gate_proj, mixer_out)


def middle_kernel(count, groups, middle_grad_ref, middle_ref, live_ref, terms_hbm, out_hbm, mixed_hbm,
                  layer_ref, stat_ref, out_grad_ref, dm_hbm,
                  low, out_w, mixed, dm, held, slots, cube_a, slots_a, cube_b, slots_b,
                  load_sem, dm_sem, ag_send, ag_recv, rs_send, rs_recv, a_send, a_recv, b_send, b_recv):
    me = lax.axis_index("mp")
    rows, columns = middle_ref.shape
    channels = out_w.shape[0]
    width = columns // PARTS
    chunk = columns // groups
    half = channels // 2
    loads = [pltpu.make_async_copy(source, target, load_sem.at[index]) for index, (source, target) in enumerate(
        ((out_hbm, out_w), (mixed_hbm, mixed), (terms_hbm, held)))]
    for load in loads:
        load.start()
    low[me] = middle_grad_ref[...].astype(BF)
    greet(count, groups)
    gather = Gather(count, low, ag_send, ag_recv)
    scatter = Scatter(count, held, slots, rs_send, rs_recv)
    order_a, order_b = orders(groups)
    cubes = (Cube(groups, order_a, cube_a, slots_a, a_send, a_recv),
             Cube(groups, order_b, cube_b, slots_b, b_send, b_recv))
    gather.start()
    for load in loads:
        load.wait()

    def dm_copy(block):
        return pltpu.make_async_copy(dm.at[block], dm_hbm.at[pl.ds(pl.multiple_of(block * rows, rows), rows)],
                                     dm_sem.at[block])

    def back(block):
        dm[block] = dot_nt(low[block], out_w[...])
        dm_copy(block).start()

    back(me)
    for distance in range(1, count):
        gather.take(distance)
        if distance == 1:
            for step in range(count - 1):
                for part in range(PARTS):
                    pl.when(me == 0)(scatter.copy(count - 1 - step, part, 1).start)
                    pl.when(me == count - 1)(scatter.copy(step, part, -1).start)
        pl.when(me - distance >= 0)(lambda: back(me - distance))
        pl.when(me + distance < count)(lambda: back(me + distance))

    def out_grad(index, unused):
        right = low[:, :, pl.ds(pl.multiple_of(index * chunk, chunk), chunk)].reshape(count * rows, chunk)
        both = dot_tn(mixed[...], right).astype(BF)
        cube_a[index] = both[:half]
        cube_b[index] = both[half:]
        return unused

    lax.fori_loop(0, groups, out_grad, 0)
    levels = len(order_a)
    for cube in cubes:
        cube.start(0)
    level = 0
    for time in scatter.times():
        scatter.pass_on(time, False, False)
        if level < levels and time > 1:
            for cube in cubes:
                cube.finish(level)
                if level + 1 < levels:
                    cube.start(level + 1)
            level += 1
    for rest in range(level, levels):
        for cube in cubes:
            cube.finish(rest)
            if rest + 1 < levels:
                cube.start(rest + 1)
    out_grad_ref[0:half, :] = cubes[0].result()
    out_grad_ref[half:channels, :] = cubes[1].result()
    row_sums = jnp.zeros((rows, 1), F32)
    for part in range(PARTS):
        span = slice(part * width, (part + 1) * width)
        scatter.wait_total(part)
        total = scatter.total(part)
        row_sums = row_sums + jnp.sum(total * total, axis=1, keepdims=True)
        layer_ref[:, span] = (middle_ref[:, span] + total).astype(BF)
    live_squares(live_ref, row_sums, stat_ref)
    for block in range(count):
        dm_copy(block).wait()
    gather.drain()
    scatter.drain()


def call_middle(count, groups, middle_grad, middle, live, terms, mixer_out, mixed):
    rows, columns = middle.shape
    channels = mixer_out.shape[0]
    total = count * rows
    chunk = columns // groups
    return pl.pallas_call(
        functools.partial(middle_kernel, count, groups),
        out_shape=(
            jax.ShapeDtypeStruct((rows, columns), BF), jax.ShapeDtypeStruct((8, 128), F32),
            jax.ShapeDtypeStruct((channels, chunk), F32), jax.ShapeDtypeStruct((total, channels), F32),
        ),
        in_specs=[IN_VMEM] * 3 + [ANYWHERE] * 3,
        out_specs=(IN_VMEM, IN_VMEM, IN_VMEM, ANYWHERE),
        scratch_shapes=[
            pltpu.VMEM((count, rows, columns), BF),
            pltpu.VMEM((channels, columns), BF),
            pltpu.VMEM((total, channels), BF),
            pltpu.VMEM((count, rows, channels), F32),
            pltpu.VMEM((count, PARTS, rows, columns // PARTS), BF),
            pltpu.VMEM((count + 1, PARTS, rows, columns // PARTS), BF),
            pltpu.VMEM((groups, channels // 2, chunk), BF),
            pltpu.VMEM((groups - 1, channels // 2, chunk), BF),
            pltpu.VMEM((groups, channels // 2, chunk), BF),
            pltpu.VMEM((groups - 1, channels // 2, chunk), BF),
            DMA((3,)), DMA((count,)), DMA((2, count)), DMA((count,)), DMA((count, PARTS)), DMA((count + 1, PARTS)),
            DMA((groups - 1,)), DMA((groups - 1,)), DMA((groups - 1,)), DMA((groups - 1,)),
        ],
        compiler_params=pltpu.CompilerParams(vmem_limit_bytes=VMEM_LIMIT, collective_id=2, has_side_effects=True),
        cost_estimate=pl.CostEstimate(flops=4 * total * columns * channels, bytes_accessed=40 * total * channels,
                                      transcendentals=0),
    )(middle_grad, middle, live, terms, mixer_out, mixed)


def input_kernel(count, groups, heads, tokens_ref, gain_ref, middle_grad_ref, mask_ref, vec_ref, rate_ref, inlet_ref,
                 value_hbm, gate_hbm, normed_hbm, dm_hbm, vp_hbm, gp_hbm, state_hbm, conv_hbm, forget_hbm, input_hbm,
                 input_grad_ref, gain_grad_ref, value_grad_ref, gate_grad_ref, small_ref, vec_grad_ref,
                 value_w, gate_w, dm, vp, gp, state, conv, forget, inlet_gate, normed, vlow, glow, dzf, dzi, dconv,
                 clow, sums, carry, held, slots, cube_a, slots_a, cube_b, slots_b, cube_c, slots_c, full,
                 vec_held, vec_slots,
                 load_sem, block_sem, normed_sem, rs_send, rs_recv, a_send, a_recv, b_send, b_recv, c_send, c_recv,
                 f_send, f_recv, v_send, v_recv):
    me = lax.axis_index("mp")
    rows, columns = tokens_ref.shape
    channels = value_w.shape[1]
    width = columns // PARTS
    chunk = columns // groups
    total_rows = count * rows
    head = channels // heads
    loads = [pltpu.make_async_copy(value_hbm, value_w, load_sem.at[0]),
             pltpu.make_async_copy(gate_hbm, gate_w, load_sem.at[1])]
    for load in loads:
        load.start()

    def block_loads(block, slot):
        at = pl.multiple_of(block * rows, rows)
        plain = pl.ds(at, rows)
        ahead = pl.ds(at, rows + 8)
        return [pltpu.make_async_copy(source.at[window], target.at[slot], block_sem.at[slot, index])
                for index, (source, window, target) in enumerate((
                    (dm_hbm, plain, dm), (vp_hbm, ahead, vp), (gp_hbm, plain, gp), (state_hbm, ahead, state),
                    (conv_hbm, plain, conv), (forget_hbm, plain, forget), (input_hbm, plain, inlet_gate)))]

    for load in block_loads(count - 1, 0):
        load.start()
    zeros = jnp.zeros((8, channels), F32)
    dconv[rows:rows + 8, :] = zeros
    carry[...] = zeros
    for row in range(8):
        sums[row] = zeros
    greet(count, groups)
    scatter = Scatter(count, held, slots, rs_send, rs_recv)
    order_a, order_b = orders(groups)
    cubes = (Cube(groups, order_a, cube_a, slots_a, a_send, a_recv),
             Cube(groups, order_b, cube_b, slots_b, b_send, b_recv),
             Cube(groups, order_b, cube_c, slots_c, c_send, c_recv))
    spread = Spread(cubes[2], full, f_send, f_recv)
    for load in loads:
        load.wait()

    def back(step, unused):
        block = count - 1 - step
        slot = step % 2
        for load in block_loads(block, slot):
            load.wait()

        @pl.when(step + 1 < count)
        def _():
            for load in block_loads(block - 1, 1 - slot):
                load.start()

        base = block * rows
        rec_backward(base, rows, dm.at[slot], vp.at[slot], gp.at[slot], mask_ref, vec_ref, rate_ref, inlet_ref,
                     state.at[slot], conv.at[slot], forget.at[slot], inlet_gate.at[slot],
                     vlow, glow, dzf, dzi, dconv, clow, sums, carry)
        window = pl.ds(pl.multiple_of(base, rows), rows)
        for part in range(PARTS):
            span = slice(part * width, (part + 1) * width)
            held[block, part] = (dot_nt(vlow[window, :], value_w[span, :])
                                 + dot_nt(glow[window, :], gate_w[span, :])).astype(BF)
            scatter.first(block, part)
        return unused

    def normed_copy(index, slot):
        return pltpu.make_async_copy(
            normed_hbm.at[:, :, pl.ds(pl.multiple_of(index * chunk, chunk), chunk)], normed.at[slot],
            normed_sem.at[slot])

    normed_copy(0, 0).start()
    lax.fori_loop(0, count, back, 0)

    def weights(index, unused):
        slot = index % 2
        normed_copy(index, slot).wait()
        pl.when(index + 1 < groups)(lambda: normed_copy(index + 1, 1 - slot).start())
        left = normed[slot].reshape(total_rows, chunk)
        cube_a[index] = dot_tn(left, vlow[...]).astype(BF)
        cube_b[index] = dot_tn(left, glow[...]).astype(BF)
        return unused

    lax.fori_loop(0, groups, weights, 0)
    cubes[0].start(0)
    cubes[1].start(0)
    slab = 2 * channels // groups
    for which, source in enumerate((dzf, dzi)):
        for index in range(heads):
            span = slice(index * head, (index + 1) * head)
            at = which * channels + index * head
            small_ref[at:at + head, :] = dot_tn(clow[:, span], source[:, span])
    for index in range(groups):
        cube_c[index] = small_ref[index * slab:(index + 1) * slab, :]
    cubes[2].start(0)
    for row in range(8):
        vec_held[0, row:row + 1, :] = jnp.sum(sums[row], axis=0, keepdims=True)

    def vec_copy(level):
        return pltpu.make_async_remote_copy(
            src_ref=vec_held.at[level], dst_ref=vec_slots.at[level], send_sem=v_send.at[level],
            recv_sem=v_recv.at[level], device_id={"dp": partner_of(level)}, device_id_type=MESH)

    levels = len(order_a)
    vec_copy(0).start()

    def advance(level):
        if level < levels:
            for cube in cubes:
                cube.finish(level)
                if level + 1 < levels:
                    cube.start(level + 1)
            vec_copy(level).wait()
            if level + 1 < levels:
                vec_held[level + 1] = vec_held[level] + vec_slots[level]
                vec_copy(level + 1).start()
            else:
                vec_grad_ref[...] = vec_held[level] + vec_slots[level]
                value_grad_ref[...] = cubes[0].result()
                gate_grad_ref[...] = cubes[1].result()
                full[lax.axis_index("dp")] = cubes[2].result()
                spread.start(levels - 1)
        elif level < 2 * levels:
            back_level = 2 * levels - 1 - level
            spread.finish(back_level)
            if back_level > 0:
                spread.start(back_level - 1)

    level = 0
    for time in scatter.times():
        scatter.pass_on(time, False, True)
        if time > 1:
            advance(level)
            level += 1
    for rest in range(level, 2 * levels):
        advance(rest)
    for index in range(groups):
        small_ref[index * slab:(index + 1) * slab, :] = full[index]

    def write(span, change):
        input_grad_ref[:, span] = (middle_grad_ref[:, span] + change).astype(BF)

    norm_back(tokens_ref, gain_ref, scatter, gain_grad_ref, write)
    scatter.drain()


def call_input(count, groups, heads, tokens, gain, middle_grad, masks, vec, rate, inlet, value_proj, gate_proj,
               normed_all, dm, vp, gp, state, conv, forget, inp):
    rows, columns = tokens.shape
    channels = value_proj.shape[1]
    total = count * rows
    chunk = columns // groups
    head = channels // heads
    slab = 2 * channels // groups
    plain = pltpu.VMEM((2, rows, channels), F32)
    ahead = pltpu.VMEM((2, rows + 8, channels), F32)
    low = pltpu.VMEM((total, channels), BF)
    levels = groups.bit_length() - 1
    return pl.pallas_call(
        functools.partial(input_kernel, count, groups, heads),
        out_shape=(
            jax.ShapeDtypeStruct((rows, columns), BF), jax.ShapeDtypeStruct((1, columns), F32),
            jax.ShapeDtypeStruct((chunk, channels), F32), jax.ShapeDtypeStruct((chunk, channels), F32),
            jax.ShapeDtypeStruct((2 * channels, head), F32), jax.ShapeDtypeStruct((8, channels), F32),
        ),
        in_specs=[IN_VMEM] * 7 + [ANYWHERE] * 10,
        out_specs=(IN_VMEM,) * 6,
        scratch_shapes=[
            pltpu.VMEM((columns, channels), BF),
            pltpu.VMEM((columns, channels), BF),
            plain, ahead, plain, ahead, plain, plain, plain,
            pltpu.VMEM((2, count, rows, chunk), BF),
            low, low, low, low,
            pltpu.VMEM((rows + 8, channels), F32),
            low,
            pltpu.VMEM((8, 8, channels), F32),
            pltpu.VMEM((8, channels), F32),
            pltpu.VMEM((count, PARTS, rows, columns // PARTS), BF),
            pltpu.VMEM((count + 1, PARTS, rows, columns // PARTS), BF),
            pltpu.VMEM((groups, chunk, channels), BF), pltpu.VMEM((groups - 1, chunk, channels), BF),
            pltpu.VMEM((groups, chunk, channels), BF), pltpu.VMEM((groups - 1, chunk, channels), BF),
            pltpu.VMEM((groups, slab, head), F32), pltpu.VMEM((groups - 1, slab, head), F32),
            pltpu.VMEM((groups, slab, head), F32),
            pltpu.VMEM((levels, 8, channels), F32), pltpu.VMEM((levels, 8, channels), F32),
            DMA((2,)), DMA((2, 7)), DMA((2,)), DMA((count, PARTS)), DMA((count + 1, PARTS)),
            DMA((groups - 1,)), DMA((groups - 1,)), DMA((groups - 1,)), DMA((groups - 1,)),
            DMA((groups - 1,)), DMA((groups - 1,)), DMA((groups - 1,)), DMA((groups - 1,)),
            DMA((levels,)), DMA((levels,)),
        ],
        compiler_params=pltpu.CompilerParams(vmem_limit_bytes=VMEM_LIMIT, collective_id=3, has_side_effects=True),
        cost_estimate=pl.CostEstimate(flops=8 * total * columns * channels, bytes_accessed=60 * total * channels,
                                      transcendentals=4 * total * channels),
    )(tokens, gain, middle_grad, masks, vec, rate, inlet, value_proj, gate_proj, normed_all, dm, vp, gp, state, conv,
      forget, inp)


def spans(total):
    size = 512 if total % 512 == 0 else 256
    return [slice(at, at + size) for at in range(0, total, size)]


def dense_kernel(count, groups, middle_ref, gain_ref, cot_hbm, gate_hbm, value_hbm, down_hbm,
                 middle_grad_ref, gain_grad_ref, dense_part_hbm, gate_out, value_out, down_out,
                 normed, cot, gate_w, value_w, down_w, hidden, gate_g, value_g, dense_part, held, slots, stage,
                 load_sem, cot_sem, part_sem, stage_sem, ag_send, ag_recv, rs_send, rs_recv):
    me = lax.axis_index("mp")
    rows, columns = middle_ref.shape
    units = gate_w.shape[1]
    width = columns // PARTS
    loads = [pltpu.make_async_copy(gate_hbm, gate_w, load_sem.at[0]),
             pltpu.make_async_copy(value_hbm, value_w, load_sem.at[1]),
             pltpu.make_async_copy(down_hbm, down_w, load_sem.at[2])]
    for load in loads:
        load.start()

    def cot_copy(block):
        return pltpu.make_async_copy(cot_hbm.at[block],
                                     cot.at[block], cot_sem.at[block])

    for block in range(count):
        cot_copy(block).start()
    greet(count)
    gather = Gather(count, normed, ag_send, ag_recv)
    scatter = Scatter(count, held, slots, rs_send, rs_recv)
    norm_rows(middle_ref, gain_ref, normed.at[me])
    gather.start()
    for load in loads:
        load.wait()
    pieces = 3
    piece = units // pieces

    def part_copy(block, slot):
        return pltpu.make_async_copy(dense_part.at[slot], dense_part_hbm.at[block], part_sem.at[slot])

    def compute(block, slot, reuse):
        cot_copy(block).wait()
        rows_in = normed[block]
        rows_cot = cot[block]
        for index in range(pieces):
            span = slice(index * piece, (index + 1) * piece)
            gate_linear = dot_nn(rows_in, gate_w[:, span])
            value_linear = dot_nn(rows_in, value_w[:, span])
            hidden_grad = dot_nt(rows_cot, down_w[span, :])
            act, slope = gelu_both(gate_linear)
            hidden[block, :, span] = (act * value_linear).astype(BF)
            gate_g[block, :, span] = (hidden_grad * value_linear * slope).astype(BF)
            value_g[block, :, span] = (hidden_grad * act).astype(BF)
        for part in range(PARTS):
            span = slice(part * width, (part + 1) * width)
            held[block, part] = (dot_nt(gate_g[block], gate_w[span, :])
                                 + dot_nt(value_g[block], value_w[span, :])).astype(BF)
            scatter.first(block, part)
        pl.when(reuse)(lambda: part_copy(block, slot).wait())
        for part in range(PARTS):
            span = slice(part * width, (part + 1) * width)
            dense_part[slot, part] = dot_nn(hidden[block], down_w[:, span]).astype(BF)
        part_copy(block, slot).start()

    def arrive(distance, unused):
        pl.when(distance > 0)(lambda: gather.take(distance))

        def side(which, inner):
            block = me - distance + 2 * distance * which
            pl.when((block >= 0) & (block < count) & ((distance > 0) | (which == 0)))(
                lambda: compute(block, which, (distance > 1) | ((distance == 1) & (which == 0))))
            return inner

        return lax.fori_loop(0, 2, side, unused)

    lax.fori_loop(0, count, arrive, 0)

    total_rows = count * rows
    left_rows = columns // 4
    unit_rows = units // 4
    group_width = columns // groups

    def stage_copy(kind, index, slot):
        if kind == 2:
            half = columns // 2
            return pltpu.make_async_copy(
                stage.at[slot, pl.ds(0, unit_rows), pl.ds(0, half)],
                down_out.at[pl.ds(index // 2 * unit_rows, unit_rows), pl.ds(index % 2 * half, half)],
                stage_sem.at[slot])
        target = gate_out if kind == 0 else value_out
        return pltpu.make_async_copy(
            stage.at[slot, pl.ds(0, left_rows), pl.ds(0, units)],
            target.at[pl.ds(index * left_rows, left_rows)], stage_sem.at[slot])

    def grads(kind, index, slot):
        if kind == 2:
            low = index // 2 * unit_rows
            left = hidden[:, :, low:low + unit_rows].reshape(total_rows, unit_rows)
            for span in spans(columns // 2):
                at = index % 2 * (columns // 2) + span.start
                size = span.stop - span.start
                right = cot[:, :, at:at + size].reshape(total_rows, size)
                stage[slot, 0:unit_rows, span] = dot_tn(left, right).astype(BF)
        else:
            left = normed[:, :, index * left_rows:(index + 1) * left_rows].reshape(total_rows, left_rows)
            source = gate_g if kind == 0 else value_g
            for span in spans(units):
                right = source[:, :, span].reshape(total_rows, span.stop - span.start)
                stage[slot, 0:left_rows, span] = dot_tn(left, right).astype(BF)

    work = [(kind, index) for kind in (0, 1, 2) for index in range((4, 4, 8)[kind])]
    started = []
    times = scatter.times()
    per_step = -(-len(work) // (len(times) + 1))
    for step in range(len(times) + 1):
        if step > 0:
            scatter.pass_on(step, True, True)
        for kind, index in work[step * per_step:(step + 1) * per_step]:
            slot = len(started) % 2
            if len(started) >= 2:
                stage_copy(*started[-2], slot).wait()
            grads(kind, index, slot)
            stage_copy(kind, index, slot).start()
            started.append((kind, index))
    for back in (2, 1):
        stage_copy(*started[-back], (len(started) - back) % 2).wait()

    def write(span, change):
        middle_grad_ref[:, span] = cot[me, :, span].astype(F32) + change

    norm_back(middle_ref, gain_ref, scatter, gain_grad_ref, write)
    part_copy(0, 0).wait()
    pl.when(me < count - 1)(part_copy(0, 1).wait)
    gather.drain()
    scatter.drain()


def call_dense(count, groups, middle, gain, cot_all, dense_gate, dense_value, dense_down):
    rows, columns = middle.shape
    units = dense_gate.shape[1]
    width = columns // PARTS
    any_spec = pl.BlockSpec(memory_space=pl.ANY)
    vmem = pl.BlockSpec(memory_space=pltpu.VMEM)
    dma = pltpu.SemaphoreType.DMA
    return pl.pallas_call(
        functools.partial(dense_kernel, count, groups),
        out_shape=(
            jax.ShapeDtypeStruct((rows, columns), F32),
            jax.ShapeDtypeStruct((1, columns), F32),
            jax.ShapeDtypeStruct((count, PARTS, rows, width), BF),
            jax.ShapeDtypeStruct((columns, units), BF),
            jax.ShapeDtypeStruct((columns, units), BF),
            jax.ShapeDtypeStruct((units, columns), BF),
        ),
        in_specs=[vmem, vmem, any_spec, any_spec, any_spec, any_spec],
        out_specs=(vmem, vmem, any_spec, any_spec, any_spec, any_spec),
        scratch_shapes=[
            pltpu.VMEM((count, rows, columns), BF),
            pltpu.VMEM((count, rows, columns), BF),
            pltpu.VMEM((columns, units), BF),
            pltpu.VMEM((columns, units), BF),
            pltpu.VMEM((units, columns), BF),
            pltpu.VMEM((count, rows, units), BF),
            pltpu.VMEM((count, rows, units), BF),
            pltpu.VMEM((count, rows, units), BF),
            pltpu.VMEM((2, PARTS, rows, width), BF),
            pltpu.VMEM((count, PARTS, rows, width), BF),
            pltpu.VMEM((count + 1, PARTS, rows, width), BF),
            pltpu.VMEM((2, columns // 4, max(units, columns // 2)), BF),
            dma((3,)), dma((count,)), dma((2,)), dma((2,)),
            dma((2, count)), dma((count,)), dma((count, PARTS)), dma((count + 1, PARTS)),
        ],
        compiler_params=pltpu.CompilerParams(
            vmem_limit_bytes=VMEM_LIMIT, collective_id=0, has_side_effects=True),
        cost_estimate=pl.CostEstimate(flops=18 * count * rows * columns * units,
                                      bytes_accessed=12 * columns * units, transcendentals=count * rows * units),
    )(middle, gain, cot_all, dense_gate, dense_value, dense_down)


def block_diagonal(heads):
    count, width, unused = heads.shape
    spread = heads[:, :, None, :] * jnp.eye(count, dtype=heads.dtype)[:, None, :, None]
    return spread.reshape(count * width, count * width)


def scatter_dp(values, dimension):
    return lax.psum_scatter(values, "dp", scatter_dimension=dimension, tiled=True).astype(F32)


def local(groups, tokens, cotangent, lengths, live_mask, mixer_gain, value_proj, gate_proj, conv_taps, conv_bias,
          rate_weight, rate_bias, inlet_weight, inlet_bias, decay_param, mixer_out, dense_gain,
          dense_gate, dense_value, dense_down):
    columns = tokens.shape[1]
    head_count, head_width = rate_weight.shape[:2]
    channels = head_count * head_width
    count = lax.axis_size("mp")
    rows_total = count * tokens.shape[0]
    offsets = doc_offsets(lengths[0], rows_total)
    taps_here = jnp.arange(8, dtype=jnp.int32)
    masks = (offsets[:, None] >= taps_here[None, :]).astype(F32)
    masks = jnp.concatenate([masks, jnp.zeros((8, 8), F32)], axis=0)
    vec = jnp.concatenate([
        conv_taps,
        jnp.stack([conv_bias, rate_bias, inlet_bias, -8.0 * jax.nn.softplus(-decay_param)]),
    ], axis=0)
    rate_square = block_diagonal(rate_weight).astype(BF)
    inlet_square = block_diagonal(inlet_weight).astype(BF)
    weights_live = live_mask.astype(F32)
    live_column = weights_live[:, None]
    middle, mixer_stat, normed_all, cot_all, mixed, vp, gp, state, conv, forget, inp = call_mixer(
        count, tokens, mixer_gain[None, :], live_column, masks, vec, rate_square, inlet_square,
        cotangent, value_proj, gate_proj, mixer_out)
    middle_grad, dense_gain_grad, dense_terms, gate_weights, value_weights, down_weights = call_dense(
        count, groups, middle, dense_gain[None, :], cot_all, dense_gate, dense_value, dense_down)
    layer_out, dense_stat, mixer_out_sum, dm = call_middle(
        count, groups, middle_grad, middle, live_column, dense_terms, mixer_out, mixed)
    input_grad, mixer_gain_grad, value_proj_sum, gate_proj_sum, small, vec_sum = call_input(
        count, groups, head_count, tokens, mixer_gain[None, :], middle_grad, masks, vec, rate_square, inlet_square,
        value_proj, gate_proj, normed_all, dm, vp, gp, state, conv, forget, inp)
    residual = tokens.astype(F32)
    squares = jnp.stack([
        jnp.sum(weights_live * jnp.sum(residual * residual, axis=1)), mixer_stat[0, 0], dense_stat[0, 0]])
    mixer_gain_sum, dense_gain_sum, squares, live_count = lax.psum(
        (mixer_gain_grad[0], dense_gain_grad[0], squares, jnp.sum(weights_live)), ("dp", "mp"))
    branch_rms = jnp.sqrt(squares / (live_count * columns))
    decay_scale = 8.0 * jax.nn.sigmoid(-decay_param)
    return (
        layer_out,
        input_grad,
        mixer_gain_sum,
        value_proj_sum,
        gate_proj_sum,
        vec_sum[0:4],
        vec_sum[4],
        small[:channels].reshape(rate_weight.shape),
        vec_sum[V_RATE],
        small[channels:].reshape(rate_weight.shape),
        vec_sum[V_INLET],
        vec_sum[V_DECAY] * decay_scale,
        mixer_out_sum,
        dense_gain_sum,
        scatter_dp(gate_weights, 0),
        scatter_dp(value_weights, 0),
        scatter_dp(down_weights, 1),
        branch_rms,
    )


def solution(mesh):
    rows = P(("dp", "mp"), None)
    return jax.shard_map(
        functools.partial(local, mesh.shape["dp"]),
        mesh=mesh,
        in_specs=(
            rows, rows, P("dp", None), P(("dp", "mp")), P(),
            P(None, "mp"), P(None, "mp"), P(None, "mp"), P("mp"),
            P("mp", None, None), P("mp"), P("mp", None, None), P("mp"), P("mp"),
            P("mp", None), P(), P(None, "mp"), P(None, "mp"), P("mp", None),
        ),
        out_specs=(
            rows, rows, P(), P("dp", "mp"), P("dp", "mp"),
            P(None, "mp"), P("mp"), P("mp", None, None), P("mp"), P("mp", None, None), P("mp"), P("mp"),
            P("mp", "dp"), P(), P("dp", "mp"), P("dp", "mp"), P("mp", "dp"), P(),
        ),
        check_vma=False,
    )
```

```python
import functools

import jax
import jax.numpy as jnp
from jax import lax
from jax.experimental import pallas as pl
from jax.experimental.pallas import tpu as pltpu
from jax.sharding import PartitionSpec as P

EPS = 1e-06
BF = jnp.bfloat16
F32 = jnp.float32
GELU_C = 0.7978845608028654
GELU_A = 0.044715
CHUNK = 16
VMEM_LIMIT = 60 * 1024 * 1024


def dot_nn(left, right):
    return jnp.dot(left, right, preferred_element_type=F32)


def dot_nt(left, right):
    return lax.dot_general(left, right, (((1,), (1,)), ((), ())), preferred_element_type=F32)


def dot_tn(left, right):
    return lax.dot_general(left, right, (((0,), (0,)), ((), ())), preferred_element_type=F32)


def gelu(x):
    return 0.5 * x * (1.0 + jnp.tanh(GELU_C * (x + GELU_A * x * x * x)))


def gelu_both(x):
    square = x * x
    tanh_in = jnp.tanh(GELU_C * x * (1.0 + GELU_A * square))
    half = 0.5 * (1.0 + tanh_in)
    slope = half + 0.5 * x * (1.0 - tanh_in * tanh_in) * (GELU_C * (1.0 + 3.0 * GELU_A * square))
    return half * x, slope


def sigmoid(x):
    return 1.0 / (1.0 + jnp.exp(-x))


def one_minus_square(log_decay, carried):
    y = 2.0 * log_decay
    series = 1.0 + y * (1.0 / 7.0)
    for k in (6.0, 5.0, 4.0, 3.0, 2.0):
        series = 1.0 + y * (1.0 / k) * series
    return jnp.where(y > -0.5, -y * series, 1.0 - carried * carried)


def row_in_tile(shape):
    return lax.broadcasted_iota(jnp.int32, shape, 0) % 8


def scan_tile_down(mult, add):
    row = row_in_tile(mult.shape)
    for step in (1, 2, 4):
        keep = row >= step
        add_up = jnp.where(keep, pltpu.roll(add, step, 0), 0.0)
        mult_up = jnp.where(keep, pltpu.roll(mult, step, 0), 1.0)
        add = add + mult * add_up
        mult = mult * mult_up
    return mult, add


def scan_tile_up(mult, add):
    row = row_in_tile(mult.shape)
    for step in (1, 2, 4):
        keep = row < 8 - step
        add_dn = jnp.where(keep, pltpu.roll(add, 8 - step, 0), 0.0)
        mult_dn = jnp.where(keep, pltpu.roll(mult, 8 - step, 0), 1.0)
        add = add + mult * add_dn
        mult = mult * mult_dn
    return mult, add


V_BIAS, V_RATE, V_INLET, V_DECAY = 4, 5, 6, 7


def fold(values, columns):
    return jnp.sum(values.reshape(values.shape[0] // 8, 8, columns), axis=0)


def rec_forward(base, rows, vp_ref, gp_ref, mask_ref, vec_ref, rate_ref, inlet_ref,
                mixed_ref, state_ref, conv_ref, forget_ref, input_ref, low_ref, carry_ref):
    bias = vec_ref[V_BIAS:V_BIAS + 1, :]

    def conv_step(index, unused):
        at = pl.multiple_of(base + index * CHUNK, CHUNK)
        ext = vp_ref[pl.ds(at, CHUNK + 8), :]
        masks = mask_ref[pl.ds(at, CHUNK), :]
        total = bias + vec_ref[0:1, :] * ext[8:8 + CHUNK, :]
        for tap in (1, 2, 3):
            total = total + (masks[:, tap:tap + 1] * ext[8 - tap:8 - tap + CHUNK, :]) * vec_ref[tap:tap + 1, :]
        conv_ref[pl.ds(at, CHUNK), :] = total
        low_ref[pl.ds(pl.multiple_of(index * CHUNK, CHUNK), CHUNK), :] = total.astype(BF)
        return unused

    lax.fori_loop(0, rows // CHUNK, conv_step, 0)
    block = pl.ds(pl.multiple_of(base, rows), rows)
    forget_ref[block, :] = dot_nn(low_ref[...], rate_ref[...])
    input_ref[block, :] = dot_nn(low_ref[...], inlet_ref[...])
    rate_bias = vec_ref[V_RATE:V_RATE + 1, :]
    inlet_bias = vec_ref[V_INLET:V_INLET + 1, :]
    decay = vec_ref[V_DECAY:V_DECAY + 1, :]

    def scan_step(index, carry):
        at = pl.multiple_of(base + index * CHUNK, CHUNK)
        window = pl.ds(at, CHUNK)
        forget = sigmoid(forget_ref[window, :] + rate_bias)
        inlet = sigmoid(input_ref[window, :] + inlet_bias)
        log_decay = decay * forget
        carried = jnp.exp(log_decay)
        normalizer = jnp.sqrt(one_minus_square(log_decay, carried))
        forget_ref[window, :] = forget
        input_ref[window, :] = inlet
        add = normalizer * inlet * conv_ref[window, :]
        mult = carried * mask_ref[window, 1:2]
        pieces = []
        for tile in range(CHUNK // 8):
            m, a = scan_tile_down(mult[8 * tile:8 * tile + 8], add[8 * tile:8 * tile + 8])
            states = a + m * carry
            carry = states[7:8, :]
            pieces.append(states)
        states = jnp.concatenate(pieces, axis=0)
        state_ref[pl.ds(at + 8, CHUNK), :] = states
        mixed_ref[window, :] = (states * gelu(gp_ref[window, :])).astype(BF)
        return carry

    carry_ref[0:1, :] = lax.fori_loop(0, rows // CHUNK, scan_step, carry_ref[0:1, :])


def rec_backward(base, rows, dm_ref, vp_ref, gp_ref, mask_ref, vec_ref, rate_ref, inlet_ref,
                 state_ref, conv_ref, forget_ref, input_ref,
                 vlow_ref, glow_ref, dzf_ref, dzi_ref, dconv_ref, clow_ref, sums_ref, carry_ref):
    columns = conv_ref.shape[1]
    decay = vec_ref[V_DECAY:V_DECAY + 1, :]
    chunks = rows // CHUNK

    def scan_step(step, carry):
        grad_next, mult_next, rate_sum, inlet_sum, decay_sum = carry
        low = pl.multiple_of((chunks - 1 - step) * CHUNK, CHUNK)
        here = pl.ds(low, CHUNK)
        window = pl.ds(pl.multiple_of(base + low, CHUNK), CHUNK)
        mixed_grad = dm_ref[here, :]
        act, slope = gelu_both(gp_ref[here, :])
        ext = state_ref[pl.ds(low, CHUNK + 8), :]
        states = ext[8:, :]
        before = ext[7:7 + CHUNK, :]
        glow_ref[window, :] = (mixed_grad * states * slope).astype(BF)
        add = mixed_grad * act
        forget = forget_ref[here, :]
        inlet = input_ref[here, :]
        conv = conv_ref[here, :]
        clow_ref[window, :] = conv.astype(BF)
        log_decay = decay * forget
        carried = jnp.exp(log_decay)
        square = one_minus_square(log_decay, carried)
        inverse = lax.rsqrt(jnp.maximum(square, 1e-30))
        normalizer = square * inverse
        mult = carried * mask_ref[window, 1:2]
        pieces = []
        for tile in reversed(range(CHUNK // 8)):
            lo = 8 * tile
            after = mult[lo + 8:lo + 9, :] if lo + 8 < CHUNK else mult_next
            shifted = jnp.concatenate([mult[lo + 1:lo + 8, :], after], axis=0)
            m, a = scan_tile_up(shifted, add[lo:lo + 8])
            grads = a + m * grad_next
            grad_next = grads[0:1, :]
            pieces.append(grads)
        grads = jnp.concatenate(pieces[::-1], axis=0)
        gated = grads * inlet
        d_log = grads * before * mult - gated * conv * ((1.0 - square) * inverse)
        dzf = d_log * decay * forget * (1.0 - forget)
        dzi = grads * normalizer * conv * inlet * (1.0 - inlet)
        dzf_ref[window, :] = dzf.astype(BF)
        dzi_ref[window, :] = dzi.astype(BF)
        dconv_ref[here, :] = gated * normalizer
        return (grad_next, mult[0:1, :], rate_sum + fold(dzf, columns), inlet_sum + fold(dzi, columns),
                decay_sum + fold(d_log * forget, columns))

    grad_next, mult_next, rate_sum, inlet_sum, decay_sum = lax.fori_loop(
        0, chunks, scan_step,
        (carry_ref[0:1, :], carry_ref[1:2, :], sums_ref[V_RATE], sums_ref[V_INLET], sums_ref[V_DECAY]))
    carry_ref[0:1, :] = grad_next
    carry_ref[1:2, :] = mult_next
    sums_ref[V_RATE] = rate_sum
    sums_ref[V_INLET] = inlet_sum
    sums_ref[V_DECAY] = decay_sum
    block = pl.ds(pl.multiple_of(base, rows), rows)
    dconv_ref[0:rows, :] += dot_nt(dzf_ref[block, :], rate_ref[...]) + dot_nt(dzi_ref[block, :], inlet_ref[...])

    def conv_step(index, carry):
        low = pl.multiple_of(index * CHUNK, CHUNK)
        at = pl.multiple_of(base + low, CHUNK)
        ext = dconv_ref[pl.ds(low, CHUNK + 8), :]
        masks = mask_ref[pl.ds(at, CHUNK + 8), :]
        values = vp_ref[pl.ds(low, CHUNK + 8), :]
        here = ext[:CHUNK, :]
        total = vec_ref[0:1, :] * here
        sums = [carry[0] + fold(here * values[8:, :], columns)]
        for tap in (1, 2, 3):
            gated = ext * masks[:, tap:tap + 1]
            total = total + vec_ref[tap:tap + 1, :] * gated[tap:tap + CHUNK, :]
            sums.append(carry[tap] + fold(gated[:CHUNK, :] * values[8 - tap:8 - tap + CHUNK, :], columns))
        sums.append(carry[4] + fold(here, columns))
        vlow_ref[pl.ds(at, CHUNK), :] = total.astype(BF)
        return tuple(sums)

    sums = lax.fori_loop(0, chunks, conv_step, tuple(sums_ref[row] for row in range(5)))
    for row in range(5):
        sums_ref[row] = sums[row]
    dconv_ref[rows:rows + 8, :] = dconv_ref[0:8, :]


MESH = pl.DeviceIdType.MESH
PARTS = 4


IN_VMEM = pl.BlockSpec(memory_space=pltpu.VMEM)
ANYWHERE = pl.BlockSpec(memory_space=pl.ANY)
DMA = pltpu.SemaphoreType.DMA


def greet(count, groups=1, far=False):
    me = lax.axis_index("mp")
    barrier = pltpu.get_barrier_semaphore()

    @pl.when(me > 0)
    def _():
        pl.semaphore_signal(barrier, inc=1, device_id={"mp": me - 1}, device_id_type=MESH)

    @pl.when(me < count - 1)
    def _():
        pl.semaphore_signal(barrier, inc=1, device_id={"mp": me + 1}, device_id_type=MESH)

    peers = [("dp", bit) for bit in range(groups.bit_length() - 1)]
    if far:
        peers += [("mp", bit) for bit in range(1, count.bit_length() - 1)]
    for axis, bit in peers:
        pl.semaphore_signal(barrier, inc=1, device_id={axis: partner_of(bit, axis)}, device_id_type=MESH)
    inner = (me > 0) & (me < count - 1)

    @pl.when(inner)
    def _():
        pl.semaphore_wait(barrier, 2 + len(peers))

    @pl.when(jnp.logical_not(inner))
    def _():
        pl.semaphore_wait(barrier, 1 + len(peers))


def bit_of(value, bit):
    return (value // (1 << bit)) % 2


def partner_of(bit, axis="dp"):
    me = lax.axis_index(axis)
    return me + (1 << bit) * (1 - 2 * bit_of(me, bit))


class Cube:
    def __init__(self, count, order, held, slots, send, recv):
        self.count, self.order, self.held, self.slots, self.send, self.recv = count, order, held, slots, send, recv
        self.me = lax.axis_index("dp")

    def places(self, level):
        total = self.count >> (level + 1)
        start = self.count - (self.count >> level)
        return [(index, start + index) for index in range(total)]

    def chunk(self, level, index, mine):
        at = 0
        for rank, bit in enumerate(self.order):
            own = bit_of(self.me, bit)
            if rank < level:
                at = at + own * (1 << bit)
            elif rank == level:
                at = at + (own if mine else 1 - own) * (1 << bit)
            else:
                at = at + ((index >> (rank - level - 1)) & 1) * (1 << bit)
        return at

    def copy(self, level, index, slot):
        return pltpu.make_async_remote_copy(
            src_ref=self.held.at[self.chunk(level, index, False)],
            dst_ref=self.slots.at[slot],
            send_sem=self.send.at[slot],
            recv_sem=self.recv.at[slot],
            device_id={"dp": partner_of(self.order[level])},
            device_id_type=MESH,
        )

    def start(self, level):
        for index, slot in self.places(level):
            self.copy(level, index, slot).start()

    def finish(self, level):
        for index, slot in self.places(level):
            self.copy(level, index, slot).wait()
            if level < len(self.order) - 1:
                self.add(self.chunk(level, index, True), slot, self.held.at[self.chunk(level, index, True)])

    def add(self, chunk, slot, target):
        size = self.held.shape[1]
        rows = 64 if size % 64 == 0 else size

        def step(index, unused):
            window = pl.ds(index * rows, rows)
            target[window, :] = (self.held[chunk, window, :].astype(F32)
                                 + self.slots[slot, window, :].astype(F32)).astype(target.dtype)
            return unused

        lax.fori_loop(0, size // rows, step, 0)

    def result(self, target):
        self.add(self.me, self.count - 2, target)


class Spread:
    def __init__(self, cube, full, send, recv):
        self.cube, self.full, self.send, self.recv = cube, full, send, recv

    def copy(self, level, index, slot, mine=True):
        chunk = self.cube.chunk(level, index, mine)
        return pltpu.make_async_remote_copy(
            src_ref=self.full.at[chunk],
            dst_ref=self.full.at[chunk],
            send_sem=self.send.at[slot],
            recv_sem=self.recv.at[slot],
            device_id={"dp": partner_of(self.cube.order[level])},
            device_id_type=MESH,
        )

    def start(self, level):
        for index, slot in self.cube.places(level):
            self.copy(level, index, slot).start()

    def finish(self, level):
        for index, slot in self.cube.places(level):
            self.copy(level, index, slot).wait_send()
            self.copy(level, index, slot, False).wait_recv()


def orders(groups):
    bits = list(range(groups.bit_length() - 1))
    return bits, bits[:1] + bits[:0:-1]


class Gather:
    def __init__(self, count, buf, send, recv):
        self.count, self.buf, self.send, self.recv = count, buf, send, recv
        self.me = lax.axis_index("mp")

    def copy(self, block, way):
        return pltpu.make_async_remote_copy(
            src_ref=self.buf.at[block],
            dst_ref=self.buf.at[block],
            send_sem=self.send.at[0 if way < 0 else 1, block],
            recv_sem=self.recv.at[block],
            device_id={"mp": self.me + way},
            device_id_type=MESH,
        )

    def hand_on(self, block, way):
        pl.when(self.me < self.count - 1 if way > 0 else self.me > 0)(self.copy(block, way).start)

    def start(self):
        self.hand_on(self.me, 1)
        self.hand_on(self.me, -1)

    def take(self, distance):
        low, high = self.me - distance, self.me + distance

        @pl.when(low >= 0)
        def _():
            self.copy(low, -1).wait_recv()
            self.hand_on(low, 1)

        @pl.when(high < self.count)
        def _():
            self.copy(high, 1).wait_recv()
            self.hand_on(high, -1)

    def drain(self):
        def step(block, unused):
            pl.when((block <= self.me) & (self.me < self.count - 1))(self.copy(block, 1).wait_send)
            pl.when((block >= self.me) & (self.me > 0))(self.copy(block, -1).wait_send)
            return unused

        lax.fori_loop(0, self.count, step, 0)


class Scatter:
    def __init__(self, count, held, slots, send, recv):
        self.count, self.held, self.slots, self.send, self.recv = count, held, slots, send, recv
        self.me = lax.axis_index("mp")

    def copy(self, block, part, way):
        slot = block + 1 if way > 0 else block
        return pltpu.make_async_remote_copy(
            src_ref=self.held.at[block, part],
            dst_ref=self.slots.at[slot, part],
            send_sem=self.send.at[block, part],
            recv_sem=self.recv.at[slot, part],
            device_id={"mp": self.me + way},
            device_id_type=MESH,
        )

    def times(self):
        return range(1, 2 * self.count - 3)

    def first(self, block, part):
        pl.when((self.me == 0) & (block > 0))(self.copy(block, part, 1).start)
        pl.when((self.me == self.count - 1) & (block < self.count - 1))(self.copy(block, part, -1).start)

    def pass_part(self, block, part, way):
        self.arrived(block, part, way)
        slot = block + 1 if way > 0 else block
        self.held[block, part] = (
            self.held[block, part].astype(F32) + self.slots[slot, part].astype(F32)).astype(BF)
        self.copy(block, part, way).start()

    def arrived(self, block, part, way):
        slot = block + 1 if way > 0 else block
        pltpu.make_async_remote_copy(
            src_ref=self.held.at[block, part],
            dst_ref=self.slots.at[slot, part],
            send_sem=self.send.at[block, part],
            recv_sem=self.recv.at[slot, part],
            device_id={"mp": self.me - way},
            device_id_type=MESH,
        ).wait_recv()

    def pass_on(self, time, up_near, down_near):
        last = self.count - 1
        up = time + 1 - self.me if up_near else last + self.me - time
        down = 2 * last - 1 - self.me - time if down_near else time - last + self.me
        up_here = (self.me > 0) & (up > self.me) & (up <= last)
        down_here = (self.me < last) & (down < self.me) & (down >= 0)

        def step(part, unused):
            pl.when(up_here)(lambda: self.pass_part(up, part, 1))
            pl.when(down_here)(lambda: self.pass_part(down, part, -1))
            return unused

        lax.fori_loop(0, PARTS, step, 0)

    def wait_total(self, part):
        pl.when(self.me > 0)(lambda: self.arrived(self.me, part, 1))
        pl.when(self.me < self.count - 1)(lambda: self.arrived(self.me, part, -1))

    def total(self, part):
        below = jnp.where(self.me > 0, self.slots[self.me + 1, part].astype(F32), 0.0)
        above = jnp.where(self.me < self.count - 1, self.slots[self.me, part].astype(F32), 0.0)
        return self.held[self.me, part].astype(F32) + below + above

    def drain(self):
        def step(block, unused):
            for part in range(PARTS):
                pl.when(block > self.me)(self.copy(block, part, 1).wait_send)
                pl.when(block < self.me)(self.copy(block, part, -1).wait_send)
            return unused

        lax.fori_loop(0, self.count, step, 0)


def norm_rows(source_ref, gain_ref, target_ref):
    step_rows = 64

    def step(index, unused):
        window = pl.ds(pl.multiple_of(index * step_rows, step_rows), step_rows)
        values = source_ref[window, :].astype(F32)
        scale = lax.rsqrt(jnp.mean(values * values, axis=1, keepdims=True) + EPS)
        target_ref[window, :] = (values * scale * gain_ref[...]).astype(BF)
        return unused

    lax.fori_loop(0, source_ref.shape[0] // step_rows, step, 0)


def norm_back(values_ref, gain_ref, scatter, gain_grad_ref, write):
    rows, columns = values_ref.shape
    width = columns // PARTS
    dot_sum = jnp.zeros((rows, 1), F32)
    square_sum = jnp.zeros((rows, 1), F32)
    for part in range(PARTS):
        span = slice(part * width, (part + 1) * width)
        scatter.wait_total(part)
        grad = scatter.total(part)
        values = values_ref[:, span].astype(F32)
        dot_sum = dot_sum + jnp.sum(grad * gain_ref[:, span] * values, axis=1, keepdims=True)
        square_sum = square_sum + jnp.sum(values * values, axis=1, keepdims=True)
    scale = lax.rsqrt(square_sum * (1.0 / columns) + EPS)
    pull = scale * scale * scale * (dot_sum * (1.0 / columns))
    for part in range(PARTS):
        span = slice(part * width, (part + 1) * width)
        grad = scatter.total(part)
        values = values_ref[:, span].astype(F32)
        if gain_grad_ref is not None:
            gain_grad_ref[:, span] = jnp.sum(grad * values * scale, axis=0, keepdims=True)
        write(span, scale * (grad * gain_ref[:, span]) - values * pull)


def live_total(live_ref, row_sums):
    size = live_ref.shape[1]
    same = lax.broadcasted_iota(jnp.int32, (size, size), 0) == lax.broadcasted_iota(jnp.int32, (size, size), 1)
    column = jnp.sum(jnp.where(same, live_ref[...].astype(F32), 0.0), axis=1, keepdims=True)
    return jnp.sum(column * row_sums, axis=0, keepdims=True)


def fill_masks(lengths_ref, rows, mask_ref):
    row = lax.broadcasted_iota(jnp.int32, mask_ref.shape, 0)
    offset = row
    end = 0
    for index in range(lengths_ref.shape[1] - 1):
        end = end + lengths_ref[0, index]
        offset = jnp.where(row >= end, row - end, offset)
    taps = lax.broadcasted_iota(jnp.int32, mask_ref.shape, 1)
    mask_ref[...] = jnp.where((offset >= taps) & (row < rows), 1.0, 0.0)


def fill_square(heads_ref, square_ref):
    square_ref[...] = jnp.zeros(square_ref.shape, BF)
    width = heads_ref.shape[1]
    for head in range(heads_ref.shape[0]):
        span = slice(head * width, (head + 1) * width)
        square_ref[span, span] = heads_ref[head].astype(BF)


def mixer_kernel(count, lengths_ref, tokens_ref, gain_ref, live_ref, taps_ref, small_ref, rate_heads_ref, inlet_heads_ref,
                 cot_hbm, value_hbm, gate_hbm, out_hbm,
                 middle_ref, stat_ref, mask_ref, vec_ref, rate_ref, inlet_ref,
                 normed_all, cot_all, mixed_out, vp_out, gp_out, state_out, conv_out, forget_out, input_out,
                 normed, value_w, gate_w, out_w, vp, gp, mixed, state, conv, forget, inlet_gate, low, carry, held,
                 slots, load_sem, own_sem, out_sem, block_sem, ag_send, ag_recv, cot_send, cot_recv, rs_send, rs_recv):
    me = lax.axis_index("mp")
    rows, columns = tokens_ref.shape
    channels = value_w.shape[1]
    width = columns // PARTS
    own_copy = pltpu.make_async_copy(cot_hbm, cot_all.at[me], own_sem)
    own_copy.start()
    loads = [pltpu.make_async_copy(source, target, load_sem.at[index]) for index, (source, target) in enumerate(
        ((value_hbm, value_w), (gate_hbm, gate_w), (out_hbm, out_w)))]
    for load in loads:
        load.start()
    norm_rows(tokens_ref, gain_ref, normed.at[me])
    greet(count)
    gather = Gather(count, normed, ag_send, ag_recv)
    cots = Gather(count, cot_all, cot_send, cot_recv)
    scatter = Scatter(count, held, slots, rs_send, rs_recv)
    gather.start()
    zeros = jnp.zeros((8, channels), F32)
    vp[0:8, :] = zeros
    state[0:8, :] = zeros
    carry[...] = zeros
    fill_masks(lengths_ref, count * rows, mask_ref)
    fill_square(rate_heads_ref, rate_ref)
    fill_square(inlet_heads_ref, inlet_ref)
    vec_ref[0:4, :] = taps_ref[...]
    vec_ref[V_BIAS:V_DECAY, :] = small_ref[0:3, :]
    vec_ref[V_DECAY:V_DECAY + 1, :] = -8.0 * jnp.log1p(jnp.exp(-small_ref[3:4, :]))
    own_copy.wait()
    for load in loads:
        load.wait()

    def block_copy(block):
        return pltpu.make_async_copy(normed.at[block], normed_all.at[block], block_sem.at[block])

    def project(block):
        block_copy(block).start()
        rows_in = normed[block]
        vp[pl.ds(pl.multiple_of(block * rows + 8, 8), rows), :] = dot_nn(rows_in, value_w[...])
        gp[pl.ds(pl.multiple_of(block * rows, rows), rows), :] = dot_nn(rows_in, gate_w[...])

    def mix(block):
        base = block * rows
        rec_forward(base, rows, vp, gp, mask_ref, vec_ref, rate_ref, inlet_ref,
                    mixed, state, conv, forget, inlet_gate, low, carry)
        rows_in = mixed[pl.ds(pl.multiple_of(base, rows), rows), :]
        for part in range(PARTS):
            held[block, part] = dot_nn(rows_in, out_w[:, part * width:(part + 1) * width]).astype(BF)
            scatter.first(block, part)

    def mixed_by(block, distance):
        return (distance >= count - 1) | ((distance >= me) & (block <= me + distance)
                                          & (block < 2 * (distance - me + 1)))

    def arrive(distance, unused):
        pl.when(distance > 0)(lambda: gather.take(distance))
        pl.when((distance == me + 1) & (me < count - 1))(cots.copy(me, 1).start)
        pl.when((distance == count - me) & (me > 0))(cots.copy(me, -1).start)

        def side(which, inner):
            block = me - distance + 2 * distance * which
            pl.when((block >= 0) & (block < count) & ((distance > 0) | (which == 0)))(lambda: project(block))
            return inner

        lax.fori_loop(0, 2, side, unused)

        def turn(block, inner):
            before = (distance > 0) & mixed_by(block, distance - 1)
            pl.when(mixed_by(block, distance) & jnp.logical_not(before))(lambda: mix(block))
            return inner

        return lax.fori_loop(0, count, turn, unused)

    lax.fori_loop(0, count, arrive, 0)
    saves = [pltpu.make_async_copy(source, target, out_sem.at[index]) for index, (source, target) in enumerate(
        ((mixed, mixed_out), (vp, vp_out), (gp, gp_out), (state, state_out), (conv, conv_out),
         (forget, forget_out), (inlet_gate, input_out)))]
    for save in saves:
        save.start()
    taken = 1
    for time in scatter.times():
        if taken < count and time >= 2 * taken - 1:
            cots.take(taken)
            taken += 1
        scatter.pass_on(time, True, False)
    for distance in range(taken, count):
        cots.take(distance)
    row_sums = jnp.zeros((rows, 1), F32)
    token_sums = jnp.zeros((rows, 1), F32)
    for part in range(PARTS):
        span = slice(part * width, (part + 1) * width)
        scatter.wait_total(part)
        total = scatter.total(part)
        tokens = tokens_ref[:, span].astype(F32)
        row_sums = row_sums + jnp.sum(total * total, axis=1, keepdims=True)
        token_sums = token_sums + jnp.sum(tokens * tokens, axis=1, keepdims=True)
        middle_ref[:, span] = tokens + total
    stat_ref[...] = jnp.zeros(stat_ref.shape, F32)
    stat_ref[0:1, :] += live_total(live_ref, token_sums)
    stat_ref[1:2, :] += live_total(live_ref, row_sums)
    stat_ref[2:3, :] += live_total(live_ref, jnp.ones((rows, 1), F32))
    for save in saves:
        save.wait()
    for block in range(count):
        block_copy(block).wait()
    gather.drain()
    cots.drain()
    scatter.drain()


def call_mixer(count, lengths, tokens, gain, live, taps, small, rate_heads, inlet_heads, cotangent, value_proj, gate_proj, mixer_out):
    rows, columns = tokens.shape
    channels = value_proj.shape[1]
    total = count * rows
    wide = jax.ShapeDtypeStruct((total, channels), F32)
    ahead = jax.ShapeDtypeStruct((total + 8, channels), F32)
    blocks = jax.ShapeDtypeStruct((count, rows, columns), BF)
    square = jax.ShapeDtypeStruct((channels, channels), BF)
    return pl.pallas_call(
        functools.partial(mixer_kernel, count),
        out_shape=(
            jax.ShapeDtypeStruct((rows, columns), F32), jax.ShapeDtypeStruct((8, 128), F32),
            jax.ShapeDtypeStruct((total + 8, 8), F32), jax.ShapeDtypeStruct((8, channels), F32), square, square,
            blocks, blocks, jax.ShapeDtypeStruct((total, channels), BF), ahead, wide, ahead, wide, wide, wide,
        ),
        in_specs=[pl.BlockSpec(memory_space=pltpu.SMEM)] + [IN_VMEM] * 7 + [ANYWHERE] * 4,
        out_specs=(IN_VMEM,) * 6 + (ANYWHERE,) * 9,
        scratch_shapes=[
            pltpu.VMEM((count, rows, columns), BF),
            pltpu.VMEM((columns, channels), BF),
            pltpu.VMEM((columns, channels), BF),
            pltpu.VMEM((channels, columns), BF),
            pltpu.VMEM((total + 8, channels), F32),
            pltpu.VMEM((total, channels), F32),
            pltpu.VMEM((total, channels), BF),
            pltpu.VMEM((total + 8, channels), F32),
            pltpu.VMEM((total, channels), F32),
            pltpu.VMEM((total, channels), F32),
            pltpu.VMEM((total, channels), F32),
            pltpu.VMEM((rows, channels), BF),
            pltpu.VMEM((8, channels), F32),
            pltpu.VMEM((count, PARTS, rows, columns // PARTS), BF),
            pltpu.VMEM((count + 1, PARTS, rows, columns // PARTS), BF),
            DMA((3,)), DMA, DMA((7,)), DMA((count,)),
            DMA((2, count)), DMA((count,)), DMA((2, count)), DMA((count,)),
            DMA((count, PARTS)), DMA((count + 1, PARTS)),
        ],
        compiler_params=pltpu.CompilerParams(vmem_limit_bytes=VMEM_LIMIT, collective_id=1, has_side_effects=True),
        cost_estimate=pl.CostEstimate(flops=6 * total * columns * channels, bytes_accessed=40 * total * channels,
                                      transcendentals=6 * total * channels),
    )(lengths, tokens, gain, live, taps, small, rate_heads, inlet_heads, cotangent,
      value_proj, gate_proj, mixer_out)


def middle_kernel(count, groups, middle_grad_ref, middle_ref, live_ref, terms_hbm, out_hbm, mixed_hbm,
                  layer_ref, stat_ref, out_grad_ref, dm_hbm,
                  low, out_w, mixed, dm, held, slots, cube_a, slots_a, cube_b, slots_b,
                  load_sem, dm_sem, ag_send, ag_recv, rs_send, rs_recv, a_send, a_recv, b_send, b_recv):
    me = lax.axis_index("mp")
    rows, columns = middle_ref.shape
    channels = out_w.shape[0]
    width = columns // PARTS
    chunk = columns // groups
    half = channels // 2
    loads = [pltpu.make_async_copy(source, target, load_sem.at[index]) for index, (source, target) in enumerate(
        ((out_hbm, out_w), (mixed_hbm, mixed), (terms_hbm, held)))]
    for load in loads:
        load.start()
    low[me] = middle_grad_ref[...].astype(BF)
    greet(count, groups)
    gather = Gather(count, low, ag_send, ag_recv)
    scatter = Scatter(count, held, slots, rs_send, rs_recv)
    order_a, order_b = orders(groups)
    cubes = (Cube(groups, order_a, cube_a, slots_a, a_send, a_recv),
             Cube(groups, order_b, cube_b, slots_b, b_send, b_recv))
    gather.start()
    for load in loads:
        load.wait()

    def dm_copy(block):
        return pltpu.make_async_copy(dm.at[block], dm_hbm.at[pl.ds(pl.multiple_of(block * rows, rows), rows)],
                                     dm_sem.at[block])

    def back(block):
        dm[block] = dot_nt(low[block], out_w[...])
        dm_copy(block).start()

    back(me)
    for distance in range(1, count):
        gather.take(distance)
        if distance == 1:
            for step in range(count - 1):
                for part in range(PARTS):
                    pl.when(me == 0)(scatter.copy(count - 1 - step, part, 1).start)
                    pl.when(me == count - 1)(scatter.copy(step, part, -1).start)
        pl.when(me - distance >= 0)(lambda: back(me - distance))
        pl.when(me + distance < count)(lambda: back(me + distance))

    def out_grad(index, unused):
        right = low[:, :, pl.ds(pl.multiple_of(index * chunk, chunk), chunk)].reshape(count * rows, chunk)
        both = dot_tn(mixed[...], right).astype(BF)
        cube_a[index] = both[:half]
        cube_b[index] = both[half:]
        return unused

    lax.fori_loop(0, groups, out_grad, 0)
    levels = len(order_a)
    for cube in cubes:
        cube.start(0)
    level = 0
    for time in scatter.times():
        scatter.pass_on(time, False, False)
        if level < levels and time > 1:
            for cube in cubes:
                cube.finish(level)
                if level + 1 < levels:
                    cube.start(level + 1)
            level += 1
    for rest in range(level, levels):
        for cube in cubes:
            cube.finish(rest)
            if rest + 1 < levels:
                cube.start(rest + 1)
    cubes[0].result(out_grad_ref.at[0:half])
    cubes[1].result(out_grad_ref.at[half:channels])
    row_sums = jnp.zeros((rows, 1), F32)
    for part in range(PARTS):
        span = slice(part * width, (part + 1) * width)
        scatter.wait_total(part)
        total = scatter.total(part)
        row_sums = row_sums + jnp.sum(total * total, axis=1, keepdims=True)
        layer_ref[:, span] = (middle_ref[:, span] + total).astype(BF)
    stat_ref[...] = jnp.zeros(stat_ref.shape, F32) + live_total(live_ref, row_sums)
    for block in range(count):
        dm_copy(block).wait()
    gather.drain()
    scatter.drain()


def call_middle(count, groups, middle_grad, middle, live, terms, mixer_out, mixed):
    rows, columns = middle.shape
    channels = mixer_out.shape[0]
    total = count * rows
    chunk = columns // groups
    return pl.pallas_call(
        functools.partial(middle_kernel, count, groups),
        out_shape=(
            jax.ShapeDtypeStruct((rows, columns), BF), jax.ShapeDtypeStruct((8, 128), F32),
            jax.ShapeDtypeStruct((channels, chunk), F32), jax.ShapeDtypeStruct((total, channels), F32),
        ),
        in_specs=[IN_VMEM] * 3 + [ANYWHERE] * 3,
        out_specs=(IN_VMEM, IN_VMEM, IN_VMEM, ANYWHERE),
        scratch_shapes=[
            pltpu.VMEM((count, rows, columns), BF),
            pltpu.VMEM((channels, columns), BF),
            pltpu.VMEM((total, channels), BF),
            pltpu.VMEM((count, rows, channels), F32),
            pltpu.VMEM((count, PARTS, rows, columns // PARTS), BF),
            pltpu.VMEM((count + 1, PARTS, rows, columns // PARTS), BF),
            pltpu.VMEM((groups, channels // 2, chunk), BF),
            pltpu.VMEM((groups - 1, channels // 2, chunk), BF),
            pltpu.VMEM((groups, channels // 2, chunk), BF),
            pltpu.VMEM((groups - 1, channels // 2, chunk), BF),
            DMA((3,)), DMA((count,)), DMA((2, count)), DMA((count,)), DMA((count, PARTS)), DMA((count + 1, PARTS)),
            DMA((groups - 1,)), DMA((groups - 1,)), DMA((groups - 1,)), DMA((groups - 1,)),
        ],
        compiler_params=pltpu.CompilerParams(vmem_limit_bytes=VMEM_LIMIT, collective_id=2, has_side_effects=True),
        cost_estimate=pl.CostEstimate(flops=4 * total * columns * channels, bytes_accessed=40 * total * channels,
                                      transcendentals=0),
    )(middle_grad, middle, live, terms, mixer_out, mixed)


def input_kernel(count, groups, heads, tokens_ref, gain_ref, middle_grad_ref, mask_ref, vec_ref, rate_ref, inlet_ref,
                 dense_gain_ref, stat_ref, dense_stat_ref, value_hbm, gate_hbm, normed_hbm, dm_hbm, vp_hbm, gp_hbm, state_hbm, conv_hbm, forget_hbm, input_hbm,
                 input_grad_ref, flat_ref, value_grad_ref, gate_grad_ref, full, vec_grad_ref,
                 value_w, gate_w, dm, vp, gp, state, conv, forget, inlet_gate, normed, vlow, glow, dzf, dzi, dconv,
                 clow, sums, carry, held, slots, cube_a, slots_a, cube_b, slots_b, cube_c, slots_c,
                 vec_held, vec_slots, flat_held, flat_slots,
                 load_sem, block_sem, normed_sem, rs_send, rs_recv, a_send, a_recv, b_send, b_recv, c_send, c_recv,
                 f_send, f_recv, v_send, v_recv, flat_send, flat_recv):
    me = lax.axis_index("mp")
    rows, columns = tokens_ref.shape
    channels = value_w.shape[1]
    width = columns // PARTS
    chunk = columns // groups
    total_rows = count * rows
    head = channels // heads
    loads = [pltpu.make_async_copy(value_hbm, value_w, load_sem.at[0]),
             pltpu.make_async_copy(gate_hbm, gate_w, load_sem.at[1])]
    for load in loads:
        load.start()

    def block_loads(block, slot):
        at = pl.multiple_of(block * rows, rows)
        plain = pl.ds(at, rows)
        ahead = pl.ds(at, rows + 8)
        return [pltpu.make_async_copy(source.at[window], target.at[slot], block_sem.at[slot, index])
                for index, (source, window, target) in enumerate((
                    (dm_hbm, plain, dm), (vp_hbm, ahead, vp), (gp_hbm, plain, gp), (state_hbm, ahead, state),
                    (conv_hbm, plain, conv), (forget_hbm, plain, forget), (input_hbm, plain, inlet_gate)))]

    for load in block_loads(count - 1, 0):
        load.start()
    zeros = jnp.zeros((8, channels), F32)
    dconv[rows:rows + 8, :] = zeros
    carry[...] = zeros
    for row in range(8):
        sums[row] = zeros
    greet(count, groups, True)
    scatter = Scatter(count, held, slots, rs_send, rs_recv)
    order_a, order_b = orders(groups)
    cubes = (Cube(groups, order_a, cube_a, slots_a, a_send, a_recv),
             Cube(groups, order_b, cube_b, slots_b, b_send, b_recv),
             Cube(groups, order_b, cube_c, slots_c, c_send, c_recv))
    spread = Spread(cubes[2], full, f_send, f_recv)
    for load in loads:
        load.wait()

    def back(step, unused):
        block = count - 1 - step
        slot = step % 2
        for load in block_loads(block, slot):
            load.wait()

        @pl.when(step + 1 < count)
        def _():
            for load in block_loads(block - 1, 1 - slot):
                load.start()

        base = block * rows
        rec_backward(base, rows, dm.at[slot], vp.at[slot], gp.at[slot], mask_ref, vec_ref, rate_ref, inlet_ref,
                     state.at[slot], conv.at[slot], forget.at[slot], inlet_gate.at[slot],
                     vlow, glow, dzf, dzi, dconv, clow, sums, carry)
        window = pl.ds(pl.multiple_of(base, rows), rows)
        for part in range(PARTS):
            span = slice(part * width, (part + 1) * width)
            held[block, part] = (dot_nt(vlow[window, :], value_w[span, :])
                                 + dot_nt(glow[window, :], gate_w[span, :])).astype(BF)
            scatter.first(block, part)
        return unused

    def normed_copy(index, slot):
        return pltpu.make_async_copy(
            normed_hbm.at[:, :, pl.ds(pl.multiple_of(index * chunk, chunk), chunk)], normed.at[slot],
            normed_sem.at[slot])

    normed_copy(0, 0).start()
    lax.fori_loop(0, count, back, 0)

    def weights(index, unused):
        slot = index % 2
        normed_copy(index, slot).wait()
        pl.when(index + 1 < groups)(lambda: normed_copy(index + 1, 1 - slot).start())
        left = normed[slot].reshape(total_rows, chunk)
        cube_a[index] = dot_tn(left, vlow[...]).astype(BF)
        cube_b[index] = dot_tn(left, glow[...]).astype(BF)
        part = index * chunk // width
        inside = pl.ds(pl.multiple_of(index * chunk % width, chunk), chunk)
        gain_row = jnp.zeros((1, chunk), F32)
        for block in range(count):
            gain_row = gain_row + jnp.sum(
                normed[slot, block].astype(F32) * held[block, part, :, inside].astype(F32), axis=0, keepdims=True)
        flat_held[0:1, pl.ds(pl.multiple_of(index * chunk, chunk), chunk)] = gain_row
        return unused

    flat_held[...] = jnp.zeros(flat_held.shape, F32)
    lax.fori_loop(0, groups, weights, 0)
    flat_held[0:1, :] = flat_held[0:1, :] / gain_ref[...]
    flat_held[1:2, :] = dense_gain_ref[...]
    for index, value in enumerate((stat_ref[0:1], stat_ref[1:2], dense_stat_ref[0:1], stat_ref[2:3])):
        flat_held[2:3, index * 128:(index + 1) * 128] = value
    peers = [("dp", bit) for bit in range(groups.bit_length() - 1)]
    peers += [("mp", bit) for bit in range(count.bit_length() - 1)]

    def flat_copy(index):
        axis, bit = peers[index]
        return pltpu.make_async_remote_copy(
            src_ref=flat_held, dst_ref=flat_slots.at[index], send_sem=flat_send.at[index],
            recv_sem=flat_recv.at[index], device_id={axis: partner_of(bit, axis)}, device_id_type=MESH)

    flat_copy(0).start()
    cubes[0].start(0)
    cubes[1].start(0)
    slab = 2 * channels // groups
    for which, source in enumerate((dzf, dzi)):
        for index in range(heads):
            span = slice(index * head, (index + 1) * head)
            square = dot_tn(clow[:, span], source[:, span])
            first = (which * channels + index * head) // slab
            for piece in range(head // slab):
                cube_c[first + piece] = square[piece * slab:(piece + 1) * slab]
    cubes[2].start(0)
    for row in range(8):
        vec_held[0, row:row + 1, :] = jnp.sum(sums[row], axis=0, keepdims=True)

    def vec_copy(level):
        return pltpu.make_async_remote_copy(
            src_ref=vec_held.at[level], dst_ref=vec_slots.at[level], send_sem=v_send.at[level],
            recv_sem=v_recv.at[level], device_id={"dp": partner_of(level)}, device_id_type=MESH)

    levels = len(order_a)
    vec_copy(0).start()

    def advance(level):
        if level < len(peers):
            flat_copy(level).wait()
            flat_held[...] += flat_slots[level]
            if level + 1 < len(peers):
                flat_copy(level + 1).start()
        if level < levels:
            for cube in cubes:
                cube.finish(level)
                if level + 1 < levels:
                    cube.start(level + 1)
            vec_copy(level).wait()
            if level + 1 < levels:
                vec_held[level + 1] = vec_held[level] + vec_slots[level]
                vec_copy(level + 1).start()
            else:
                vec_grad_ref[...] = vec_held[level] + vec_slots[level]
                cubes[0].result(value_grad_ref)
                cubes[1].result(gate_grad_ref)
                cubes[2].result(full.at[lax.axis_index("dp")])
                spread.start(levels - 1)
        elif level < 2 * levels:
            back_level = 2 * levels - 1 - level
            spread.finish(back_level)
            if back_level > 0:
                spread.start(back_level - 1)

    level = 0
    for time in scatter.times():
        scatter.pass_on(time, False, True)
        if time > 1:
            advance(level)
            level += 1
    for rest in range(level, max(2 * levels, len(peers))):
        advance(rest)
    flat_ref[...] = flat_held[...]
    def write(span, change):
        input_grad_ref[:, span] = (middle_grad_ref[:, span] + change).astype(BF)

    norm_back(tokens_ref, gain_ref, scatter, None, write)
    scatter.drain()


def call_input(count, groups, heads, tokens, gain, middle_grad, masks, vec, rate, inlet, dense_gain_grad, stat,
               dense_stat, value_proj, gate_proj, normed_all, dm, vp, gp, state, conv, forget, inp):
    rows, columns = tokens.shape
    channels = value_proj.shape[1]
    total = count * rows
    chunk = columns // groups
    head = channels // heads
    slab = 2 * channels // groups
    plain = pltpu.VMEM((2, rows, channels), F32)
    ahead = pltpu.VMEM((2, rows + 8, channels), F32)
    low = pltpu.VMEM((total, channels), BF)
    levels = groups.bit_length() - 1
    flats = levels + count.bit_length() - 1
    return pl.pallas_call(
        functools.partial(input_kernel, count, groups, heads),
        out_shape=(
            jax.ShapeDtypeStruct((rows, columns), BF), jax.ShapeDtypeStruct((8, columns), F32),
            jax.ShapeDtypeStruct((chunk, channels), F32), jax.ShapeDtypeStruct((chunk, channels), F32),
            jax.ShapeDtypeStruct((groups, slab, head), F32), jax.ShapeDtypeStruct((8, channels), F32),
        ),
        in_specs=[IN_VMEM] * 10 + [ANYWHERE] * 10,
        out_specs=(IN_VMEM,) * 6,
        scratch_shapes=[
            pltpu.VMEM((columns, channels), BF),
            pltpu.VMEM((columns, channels), BF),
            plain, ahead, plain, ahead, plain, plain, plain,
            pltpu.VMEM((2, count, rows, chunk), BF),
            low, low, low, low,
            pltpu.VMEM((rows + 8, channels), F32),
            low,
            pltpu.VMEM((8, 8, channels), F32),
            pltpu.VMEM((8, channels), F32),
            pltpu.VMEM((count, PARTS, rows, columns // PARTS), BF),
            pltpu.VMEM((count + 1, PARTS, rows, columns // PARTS), BF),
            pltpu.VMEM((groups, chunk, channels), BF), pltpu.VMEM((groups - 1, chunk, channels), BF),
            pltpu.VMEM((groups, chunk, channels), BF), pltpu.VMEM((groups - 1, chunk, channels), BF),
            pltpu.VMEM((groups, slab, head), F32), pltpu.VMEM((groups - 1, slab, head), F32),
            pltpu.VMEM((levels, 8, channels), F32), pltpu.VMEM((levels, 8, channels), F32),
            pltpu.VMEM((8, columns), F32), pltpu.VMEM((flats, 8, columns), F32),
            DMA((2,)), DMA((2, 7)), DMA((2,)), DMA((count, PARTS)), DMA((count + 1, PARTS)),
            DMA((groups - 1,)), DMA((groups - 1,)), DMA((groups - 1,)), DMA((groups - 1,)),
            DMA((groups - 1,)), DMA((groups - 1,)), DMA((groups - 1,)), DMA((groups - 1,)),
            DMA((levels,)), DMA((levels,)), DMA((flats,)), DMA((flats,)),
        ],
        compiler_params=pltpu.CompilerParams(vmem_limit_bytes=VMEM_LIMIT, collective_id=3, has_side_effects=True),
        cost_estimate=pl.CostEstimate(flops=8 * total * columns * channels, bytes_accessed=60 * total * channels,
                                      transcendentals=4 * total * channels),
    )(tokens, gain, middle_grad, masks, vec, rate, inlet, dense_gain_grad, stat, dense_stat, value_proj, gate_proj,
      normed_all, dm, vp, gp, state, conv, forget, inp)


def spans(total):
    size = 512 if total % 512 == 0 else 256
    return [slice(at, at + size) for at in range(0, total, size)]


def dense_kernel(count, groups, middle_ref, gain_ref, cot_hbm, gate_hbm, value_hbm, down_hbm,
                 middle_grad_ref, gain_grad_ref, dense_part_hbm, gate_out, value_out, down_out,
                 normed, cot, gate_w, value_w, down_w, hidden, gate_g, value_g, dense_part, held, slots, stage,
                 load_sem, cot_sem, part_sem, stage_sem, ag_send, ag_recv, rs_send, rs_recv):
    me = lax.axis_index("mp")
    rows, columns = middle_ref.shape
    units = gate_w.shape[1]
    width = columns // PARTS
    loads = [pltpu.make_async_copy(gate_hbm, gate_w, load_sem.at[0]),
             pltpu.make_async_copy(value_hbm, value_w, load_sem.at[1]),
             pltpu.make_async_copy(down_hbm, down_w, load_sem.at[2])]
    for load in loads:
        load.start()

    def cot_copy(block):
        return pltpu.make_async_copy(cot_hbm.at[block],
                                     cot.at[block], cot_sem.at[block])

    for block in range(count):
        cot_copy(block).start()
    greet(count)
    gather = Gather(count, normed, ag_send, ag_recv)
    scatter = Scatter(count, held, slots, rs_send, rs_recv)
    norm_rows(middle_ref, gain_ref, normed.at[me])
    gather.start()
    for load in loads:
        load.wait()
    pieces = 3
    piece = units // pieces

    def part_copy(block, slot):
        return pltpu.make_async_copy(dense_part.at[slot], dense_part_hbm.at[block], part_sem.at[slot])

    def compute(block, slot, reuse):
        cot_copy(block).wait()
        rows_in = normed[block]
        rows_cot = cot[block]
        for index in range(pieces):
            span = slice(index * piece, (index + 1) * piece)
            gate_linear = dot_nn(rows_in, gate_w[:, span])
            value_linear = dot_nn(rows_in, value_w[:, span])
            hidden_grad = dot_nt(rows_cot, down_w[span, :])
            act, slope = gelu_both(gate_linear)
            hidden[block, :, span] = (act * value_linear).astype(BF)
            gate_g[block, :, span] = (hidden_grad * value_linear * slope).astype(BF)
            value_g[block, :, span] = (hidden_grad * act).astype(BF)
        for part in range(PARTS):
            span = slice(part * width, (part + 1) * width)
            held[block, part] = (dot_nt(gate_g[block], gate_w[span, :])
                                 + dot_nt(value_g[block], value_w[span, :])).astype(BF)
            scatter.first(block, part)
        pl.when(reuse)(lambda: part_copy(block, slot).wait())
        for part in range(PARTS):
            span = slice(part * width, (part + 1) * width)
            dense_part[slot, part] = dot_nn(hidden[block], down_w[:, span]).astype(BF)
        part_copy(block, slot).start()

    def arrive(distance, unused):
        pl.when(distance > 0)(lambda: gather.take(distance))

        def side(which, inner):
            block = me - distance + 2 * distance * which
            pl.when((block >= 0) & (block < count) & ((distance > 0) | (which == 0)))(
                lambda: compute(block, which, (distance > 1) | ((distance == 1) & (which == 0))))
            return inner

        return lax.fori_loop(0, 2, side, unused)

    lax.fori_loop(0, count, arrive, 0)

    total_rows = count * rows
    left_rows = columns // 4
    unit_rows = units // 4
    group_width = columns // groups

    def stage_copy(kind, index, slot):
        if kind == 2:
            half = columns // 2
            return pltpu.make_async_copy(
                stage.at[slot, pl.ds(0, unit_rows), pl.ds(0, half)],
                down_out.at[pl.ds(index // 2 * unit_rows, unit_rows), pl.ds(index % 2 * half, half)],
                stage_sem.at[slot])
        target = gate_out if kind == 0 else value_out
        return pltpu.make_async_copy(
            stage.at[slot, pl.ds(0, left_rows), pl.ds(0, units)],
            target.at[pl.ds(index * left_rows, left_rows)], stage_sem.at[slot])

    def grads(kind, index, slot):
        if kind == 2:
            low = index // 2 * unit_rows
            left = hidden[:, :, low:low + unit_rows].reshape(total_rows, unit_rows)
            for span in spans(columns // 2):
                at = index % 2 * (columns // 2) + span.start
                size = span.stop - span.start
                right = cot[:, :, at:at + size].reshape(total_rows, size)
                stage[slot, 0:unit_rows, span] = dot_tn(left, right).astype(BF)
        else:
            left = normed[:, :, index * left_rows:(index + 1) * left_rows].reshape(total_rows, left_rows)
            source = gate_g if kind == 0 else value_g
            for span in spans(units):
                right = source[:, :, span].reshape(total_rows, span.stop - span.start)
                stage[slot, 0:left_rows, span] = dot_tn(left, right).astype(BF)

    work = [(kind, index) for kind in (0, 1, 2) for index in range((4, 4, 8)[kind])]
    started = []
    times = scatter.times()
    per_step = -(-len(work) // (len(times) + 1))
    for step in range(len(times) + 1):
        if step > 0:
            scatter.pass_on(step, True, True)
        for kind, index in work[step * per_step:(step + 1) * per_step]:
            slot = len(started) % 2
            if len(started) >= 2:
                stage_copy(*started[-2], slot).wait()
            grads(kind, index, slot)
            stage_copy(kind, index, slot).start()
            started.append((kind, index))
    for back in (2, 1):
        stage_copy(*started[-back], (len(started) - back) % 2).wait()

    def write(span, change):
        middle_grad_ref[:, span] = cot[me, :, span].astype(F32) + change

    norm_back(middle_ref, gain_ref, scatter, gain_grad_ref, write)
    part_copy(0, 0).wait()
    pl.when(me < count - 1)(part_copy(0, 1).wait)
    gather.drain()
    scatter.drain()


def call_dense(count, groups, middle, gain, cot_all, dense_gate, dense_value, dense_down):
    rows, columns = middle.shape
    units = dense_gate.shape[1]
    width = columns // PARTS
    any_spec = pl.BlockSpec(memory_space=pl.ANY)
    vmem = pl.BlockSpec(memory_space=pltpu.VMEM)
    dma = pltpu.SemaphoreType.DMA
    return pl.pallas_call(
        functools.partial(dense_kernel, count, groups),
        out_shape=(
            jax.ShapeDtypeStruct((rows, columns), F32),
            jax.ShapeDtypeStruct((1, columns), F32),
            jax.ShapeDtypeStruct((count, PARTS, rows, width), BF),
            jax.ShapeDtypeStruct((columns, units), BF),
            jax.ShapeDtypeStruct((columns, units), BF),
            jax.ShapeDtypeStruct((units, columns), BF),
        ),
        in_specs=[vmem, vmem, any_spec, any_spec, any_spec, any_spec],
        out_specs=(vmem, vmem, any_spec, any_spec, any_spec, any_spec),
        scratch_shapes=[
            pltpu.VMEM((count, rows, columns), BF),
            pltpu.VMEM((count, rows, columns), BF),
            pltpu.VMEM((columns, units), BF),
            pltpu.VMEM((columns, units), BF),
            pltpu.VMEM((units, columns), BF),
            pltpu.VMEM((count, rows, units), BF),
            pltpu.VMEM((count, rows, units), BF),
            pltpu.VMEM((count, rows, units), BF),
            pltpu.VMEM((2, PARTS, rows, width), BF),
            pltpu.VMEM((count, PARTS, rows, width), BF),
            pltpu.VMEM((count + 1, PARTS, rows, width), BF),
            pltpu.VMEM((2, columns // 4, max(units, columns // 2)), BF),
            dma((3,)), dma((count,)), dma((2,)), dma((2,)),
            dma((2, count)), dma((count,)), dma((count, PARTS)), dma((count + 1, PARTS)),
        ],
        compiler_params=pltpu.CompilerParams(
            vmem_limit_bytes=VMEM_LIMIT, collective_id=0, has_side_effects=True),
        cost_estimate=pl.CostEstimate(flops=18 * count * rows * columns * units,
                                      bytes_accessed=12 * columns * units, transcendentals=count * rows * units),
    )(middle, gain, cot_all, dense_gate, dense_value, dense_down)


def scatter_dp(values, dimension):
    return lax.psum_scatter(values, "dp", scatter_dimension=dimension, tiled=True).astype(F32)


def local(groups, tokens, cotangent, lengths, live_mask, mixer_gain, value_proj, gate_proj, conv_taps, conv_bias,
          rate_weight, rate_bias, inlet_weight, inlet_bias, decay_param, mixer_out, dense_gain,
          dense_gate, dense_value, dense_down):
    columns = tokens.shape[1]
    head_count, head_width = rate_weight.shape[:2]
    channels = head_count * head_width
    count = lax.axis_size("mp")
    live = live_mask[None, :]
    middle, stat, masks, vec, rate_square, inlet_square, normed_all, cot_all, mixed, *saved = call_mixer(
        count, lengths, tokens, mixer_gain[None, :], live, conv_taps,
        jnp.stack([conv_bias, rate_bias, inlet_bias, decay_param]), rate_weight, inlet_weight, cotangent,
        value_proj, gate_proj, mixer_out)
    middle_grad, dense_gain_grad, dense_terms, gate_weights, value_weights, down_weights = call_dense(
        count, groups, middle, dense_gain[None, :], cot_all, dense_gate, dense_value, dense_down)
    layer_out, dense_stat, mixer_out_sum, dm = call_middle(
        count, groups, middle_grad, middle, live, dense_terms, mixer_out, mixed)
    input_grad, flat, value_proj_sum, gate_proj_sum, small, vec_sum = call_input(
        count, groups, head_count, tokens, mixer_gain[None, :], middle_grad, masks, vec, rate_square, inlet_square,
        dense_gain_grad, stat, dense_stat, value_proj, gate_proj, normed_all, dm, *saved)
    branch_rms = jnp.sqrt(flat[2, 0:384:128] / (flat[2, 384] * columns))
    decay_scale = 8.0 * jax.nn.sigmoid(-decay_param)
    return (
        layer_out,
        input_grad,
        flat[0],
        value_proj_sum,
        gate_proj_sum,
        vec_sum[0:4],
        vec_sum[4],
        small[:groups // 2].reshape(rate_weight.shape),
        vec_sum[V_RATE],
        small[groups // 2:].reshape(rate_weight.shape),
        vec_sum[V_INLET],
        vec_sum[V_DECAY] * decay_scale,
        mixer_out_sum,
        flat[1],
        scatter_dp(gate_weights, 0),
        scatter_dp(value_weights, 0),
        scatter_dp(down_weights, 1),
        branch_rms,
    )


def solution(mesh):
    rows = P(("dp", "mp"), None)
    return jax.shard_map(
        functools.partial(local, mesh.shape["dp"]),
        mesh=mesh,
        in_specs=(
            rows, rows, P("dp", None), P(("dp", "mp")), P(),
            P(None, "mp"), P(None, "mp"), P(None, "mp"), P("mp"),
            P("mp", None, None), P("mp"), P("mp", None, None), P("mp"), P("mp"),
            P("mp", None), P(), P(None, "mp"), P(None, "mp"), P("mp", None),
        ),
        out_specs=(
            rows, rows, P(), P("dp", "mp"), P("dp", "mp"),
            P(None, "mp"), P("mp"), P("mp", None, None), P("mp"), P("mp", None, None), P("mp"), P("mp"),
            P("mp", "dp"), P(), P("dp", "mp"), P("dp", "mp"), P("mp", "dp"), P(),
        ),
        check_vma=False,
    )
```

```python
import functools

import jax
import jax.numpy as jnp
from jax import lax
from jax.experimental import pallas as pl
from jax.experimental.pallas import tpu as pltpu
from jax.sharding import PartitionSpec as P

EPS = 1e-06
BF = jnp.bfloat16
F32 = jnp.float32
GELU_C = 0.7978845608028654
GELU_A = 0.044715
CHUNK = 16
VMEM_LIMIT = 60 * 1024 * 1024


def dot_nn(left, right):
    return jnp.dot(left, right, preferred_element_type=F32)


def dot_nt(left, right):
    return lax.dot_general(left, right, (((1,), (1,)), ((), ())), preferred_element_type=F32)


def dot_tn(left, right):
    return lax.dot_general(left, right, (((0,), (0,)), ((), ())), preferred_element_type=F32)


def gelu(x):
    return 0.5 * x * (1.0 + jnp.tanh(GELU_C * (x + GELU_A * x * x * x)))


def gelu_both(x):
    square = x * x
    tanh_in = jnp.tanh(GELU_C * x * (1.0 + GELU_A * square))
    half = 0.5 * (1.0 + tanh_in)
    slope = half + 0.5 * x * (1.0 - tanh_in * tanh_in) * (GELU_C * (1.0 + 3.0 * GELU_A * square))
    return half * x, slope


def sigmoid(x):
    return 1.0 / (1.0 + jnp.exp(-x))


def one_minus_square(log_decay, carried):
    y = 2.0 * log_decay
    series = 1.0 + y * (1.0 / 7.0)
    for k in (6.0, 5.0, 4.0, 3.0, 2.0):
        series = 1.0 + y * (1.0 / k) * series
    return jnp.where(y > -0.5, -y * series, 1.0 - carried * carried)


def row_in_tile(shape):
    return lax.broadcasted_iota(jnp.int32, shape, 0) % 8


def scan_tile_down(mult, add):
    row = row_in_tile(mult.shape)
    for step in (1, 2, 4):
        keep = row >= step
        add_up = jnp.where(keep, pltpu.roll(add, step, 0), 0.0)
        mult_up = jnp.where(keep, pltpu.roll(mult, step, 0), 1.0)
        add = add + mult * add_up
        mult = mult * mult_up
    return mult, add


def scan_tile_up(mult, add):
    row = row_in_tile(mult.shape)
    for step in (1, 2, 4):
        keep = row < 8 - step
        add_dn = jnp.where(keep, pltpu.roll(add, 8 - step, 0), 0.0)
        mult_dn = jnp.where(keep, pltpu.roll(mult, 8 - step, 0), 1.0)
        add = add + mult * add_dn
        mult = mult * mult_dn
    return mult, add


V_BIAS, V_RATE, V_INLET, V_DECAY = 4, 5, 6, 7


def fold(values, columns):
    return jnp.sum(values.reshape(values.shape[0] // 8, 8, columns), axis=0)


def rec_forward(base, rows, vp_ref, gp_ref, mask_ref, vec_ref, rate_ref, inlet_ref,
                mixed_ref, state_ref, conv_ref, forget_ref, input_ref, low_ref, carry_ref):
    bias = vec_ref[V_BIAS:V_BIAS + 1, :]

    def conv_step(index, unused):
        at = pl.multiple_of(base + index * CHUNK, CHUNK)
        ext = vp_ref[pl.ds(at, CHUNK + 8), :]
        masks = mask_ref[pl.ds(at, CHUNK), :]
        total = bias + vec_ref[0:1, :] * ext[8:8 + CHUNK, :]
        for tap in (1, 2, 3):
            total = total + (masks[:, tap:tap + 1] * ext[8 - tap:8 - tap + CHUNK, :]) * vec_ref[tap:tap + 1, :]
        conv_ref[pl.ds(at, CHUNK), :] = total
        low_ref[pl.ds(pl.multiple_of(index * CHUNK, CHUNK), CHUNK), :] = total.astype(BF)
        return unused

    lax.fori_loop(0, rows // CHUNK, conv_step, 0)
    block = pl.ds(pl.multiple_of(base, rows), rows)
    forget_ref[block, :] = dot_nn(low_ref[...], rate_ref[...])
    input_ref[block, :] = dot_nn(low_ref[...], inlet_ref[...])
    rate_bias = vec_ref[V_RATE:V_RATE + 1, :]
    inlet_bias = vec_ref[V_INLET:V_INLET + 1, :]
    decay = vec_ref[V_DECAY:V_DECAY + 1, :]

    def scan_step(index, carry):
        at = pl.multiple_of(base + index * CHUNK, CHUNK)
        window = pl.ds(at, CHUNK)
        forget = sigmoid(forget_ref[window, :] + rate_bias)
        inlet = sigmoid(input_ref[window, :] + inlet_bias)
        log_decay = decay * forget
        carried = jnp.exp(log_decay)
        normalizer = jnp.sqrt(one_minus_square(log_decay, carried))
        forget_ref[window, :] = forget
        input_ref[window, :] = inlet
        add = normalizer * inlet * conv_ref[window, :]
        mult = carried * mask_ref[window, 1:2]
        pieces = []
        for tile in range(CHUNK // 8):
            m, a = scan_tile_down(mult[8 * tile:8 * tile + 8], add[8 * tile:8 * tile + 8])
            states = a + m * carry
            carry = states[7:8, :]
            pieces.append(states)
        states = jnp.concatenate(pieces, axis=0)
        state_ref[pl.ds(at + 8, CHUNK), :] = states
        mixed_ref[window, :] = (states * gelu(gp_ref[window, :])).astype(BF)
        return carry

    carry_ref[0:1, :] = lax.fori_loop(0, rows // CHUNK, scan_step, carry_ref[0:1, :])


def rec_backward(base, rows, dm_ref, vp_ref, gp_ref, mask_ref, vec_ref, rate_ref, inlet_ref,
                 state_ref, conv_ref, forget_ref, input_ref,
                 vlow_ref, glow_ref, dzf_ref, dzi_ref, dconv_ref, clow_ref, sums_ref, carry_ref):
    columns = conv_ref.shape[1]
    decay = vec_ref[V_DECAY:V_DECAY + 1, :]
    chunks = rows // CHUNK

    def scan_step(step, carry):
        grad_next, mult_next, rate_sum, inlet_sum, decay_sum = carry
        low = pl.multiple_of((chunks - 1 - step) * CHUNK, CHUNK)
        here = pl.ds(low, CHUNK)
        window = pl.ds(pl.multiple_of(base + low, CHUNK), CHUNK)
        mixed_grad = dm_ref[here, :]
        act, slope = gelu_both(gp_ref[here, :])
        ext = state_ref[pl.ds(low, CHUNK + 8), :]
        states = ext[8:, :]
        before = ext[7:7 + CHUNK, :]
        glow_ref[window, :] = (mixed_grad * states * slope).astype(BF)
        add = mixed_grad * act
        forget = forget_ref[here, :]
        inlet = input_ref[here, :]
        conv = conv_ref[here, :]
        clow_ref[window, :] = conv.astype(BF)
        log_decay = decay * forget
        carried = jnp.exp(log_decay)
        square = one_minus_square(log_decay, carried)
        inverse = lax.rsqrt(jnp.maximum(square, 1e-30))
        normalizer = square * inverse
        mult = carried * mask_ref[window, 1:2]
        pieces = []
        for tile in reversed(range(CHUNK // 8)):
            lo = 8 * tile
            after = mult[lo + 8:lo + 9, :] if lo + 8 < CHUNK else mult_next
            shifted = jnp.concatenate([mult[lo + 1:lo + 8, :], after], axis=0)
            m, a = scan_tile_up(shifted, add[lo:lo + 8])
            grads = a + m * grad_next
            grad_next = grads[0:1, :]
            pieces.append(grads)
        grads = jnp.concatenate(pieces[::-1], axis=0)
        gated = grads * inlet
        d_log = grads * before * mult - gated * conv * ((1.0 - square) * inverse)
        dzf = d_log * decay * forget * (1.0 - forget)
        dzi = grads * normalizer * conv * inlet * (1.0 - inlet)
        dzf_ref[window, :] = dzf.astype(BF)
        dzi_ref[window, :] = dzi.astype(BF)
        dconv_ref[here, :] = gated * normalizer
        return (grad_next, mult[0:1, :], rate_sum + fold(dzf, columns), inlet_sum + fold(dzi, columns),
                decay_sum + fold(d_log * forget, columns))

    grad_next, mult_next, rate_sum, inlet_sum, decay_sum = lax.fori_loop(
        0, chunks, scan_step,
        (carry_ref[0:1, :], carry_ref[1:2, :], sums_ref[V_RATE], sums_ref[V_INLET], sums_ref[V_DECAY]))
    carry_ref[0:1, :] = grad_next
    carry_ref[1:2, :] = mult_next
    sums_ref[V_RATE] = rate_sum
    sums_ref[V_INLET] = inlet_sum
    sums_ref[V_DECAY] = decay_sum
    block = pl.ds(pl.multiple_of(base, rows), rows)
    dconv_ref[0:rows, :] += dot_nt(dzf_ref[block, :], rate_ref[...]) + dot_nt(dzi_ref[block, :], inlet_ref[...])

    def conv_step(index, carry):
        low = pl.multiple_of(index * CHUNK, CHUNK)
        at = pl.multiple_of(base + low, CHUNK)
        ext = dconv_ref[pl.ds(low, CHUNK + 8), :]
        masks = mask_ref[pl.ds(at, CHUNK + 8), :]
        values = vp_ref[pl.ds(low, CHUNK + 8), :]
        here = ext[:CHUNK, :]
        total = vec_ref[0:1, :] * here
        sums = [carry[0] + fold(here * values[8:, :], columns)]
        for tap in (1, 2, 3):
            gated = ext * masks[:, tap:tap + 1]
            total = total + vec_ref[tap:tap + 1, :] * gated[tap:tap + CHUNK, :]
            sums.append(carry[tap] + fold(gated[:CHUNK, :] * values[8 - tap:8 - tap + CHUNK, :], columns))
        sums.append(carry[4] + fold(here, columns))
        vlow_ref[pl.ds(at, CHUNK), :] = total.astype(BF)
        return tuple(sums)

    sums = lax.fori_loop(0, chunks, conv_step, tuple(sums_ref[row] for row in range(5)))
    for row in range(5):
        sums_ref[row] = sums[row]
    dconv_ref[rows:rows + 8, :] = dconv_ref[0:8, :]


MESH = pl.DeviceIdType.MESH
PARTS = 4


IN_VMEM = pl.BlockSpec(memory_space=pltpu.VMEM)
ANYWHERE = pl.BlockSpec(memory_space=pl.ANY)
DMA = pltpu.SemaphoreType.DMA


def greet(count, groups=1, far=False):
    me = lax.axis_index("mp")
    barrier = pltpu.get_barrier_semaphore()

    @pl.when(me > 0)
    def _():
        pl.semaphore_signal(barrier, inc=1, device_id={"mp": me - 1}, device_id_type=MESH)

    @pl.when(me < count - 1)
    def _():
        pl.semaphore_signal(barrier, inc=1, device_id={"mp": me + 1}, device_id_type=MESH)

    peers = [("dp", bit) for bit in range(groups.bit_length() - 1)]
    if far:
        peers += [("mp", bit) for bit in range(1, count.bit_length() - 1)]
    for axis, bit in peers:
        pl.semaphore_signal(barrier, inc=1, device_id={axis: partner_of(bit, axis)}, device_id_type=MESH)
    inner = (me > 0) & (me < count - 1)

    @pl.when(inner)
    def _():
        pl.semaphore_wait(barrier, 2 + len(peers))

    @pl.when(jnp.logical_not(inner))
    def _():
        pl.semaphore_wait(barrier, 1 + len(peers))


def bit_of(value, bit):
    return (value // (1 << bit)) % 2


def partner_of(bit, axis="dp"):
    me = lax.axis_index(axis)
    return me + (1 << bit) * (1 - 2 * bit_of(me, bit))


class Cube:
    def __init__(self, count, order, held, slots, send, recv):
        self.count, self.order, self.held, self.slots, self.send, self.recv = count, order, held, slots, send, recv
        self.me = lax.axis_index("dp")

    def places(self, level):
        total = self.count >> (level + 1)
        start = self.count - (self.count >> level)
        return [(index, start + index) for index in range(total)]

    def chunk(self, level, index, mine):
        at = 0
        for rank, bit in enumerate(self.order):
            own = bit_of(self.me, bit)
            if rank < level:
                at = at + own * (1 << bit)
            elif rank == level:
                at = at + (own if mine else 1 - own) * (1 << bit)
            else:
                at = at + ((index >> (rank - level - 1)) & 1) * (1 << bit)
        return at

    def copy(self, level, index, slot):
        return pltpu.make_async_remote_copy(
            src_ref=self.held.at[self.chunk(level, index, False)],
            dst_ref=self.slots.at[slot],
            send_sem=self.send.at[slot],
            recv_sem=self.recv.at[slot],
            device_id={"dp": partner_of(self.order[level])},
            device_id_type=MESH,
        )

    def start(self, level):
        for index, slot in self.places(level):
            self.copy(level, index, slot).start()

    def finish(self, level):
        for index, slot in self.places(level):
            self.copy(level, index, slot).wait()
            if level < len(self.order) - 1:
                self.add(self.chunk(level, index, True), slot, self.held.at[self.chunk(level, index, True)])

    def add(self, chunk, slot, target):
        size = self.held.shape[1]
        rows = 64 if size % 64 == 0 else size

        def step(index, unused):
            window = pl.ds(index * rows, rows)
            target[window, :] = (self.held[chunk, window, :].astype(F32)
                                 + self.slots[slot, window, :].astype(F32)).astype(target.dtype)
            return unused

        lax.fori_loop(0, size // rows, step, 0)

    def result(self, target):
        self.add(self.me, self.count - 2, target)


class Spread:
    def __init__(self, cube, full, send, recv):
        self.cube, self.full, self.send, self.recv = cube, full, send, recv

    def copy(self, level, index, slot, mine=True):
        chunk = self.cube.chunk(level, index, mine)
        return pltpu.make_async_remote_copy(
            src_ref=self.full.at[chunk],
            dst_ref=self.full.at[chunk],
            send_sem=self.send.at[slot],
            recv_sem=self.recv.at[slot],
            device_id={"dp": partner_of(self.cube.order[level])},
            device_id_type=MESH,
        )

    def start(self, level):
        for index, slot in self.cube.places(level):
            self.copy(level, index, slot).start()

    def finish(self, level):
        for index, slot in self.cube.places(level):
            self.copy(level, index, slot).wait_send()
            self.copy(level, index, slot, False).wait_recv()


def orders(groups):
    bits = list(range(groups.bit_length() - 1))
    return bits, bits[:1] + bits[:0:-1]


class Gather:
    def __init__(self, count, buf, send, recv):
        self.count, self.buf, self.send, self.recv = count, buf, send, recv
        self.me = lax.axis_index("mp")

    def copy(self, block, way):
        return pltpu.make_async_remote_copy(
            src_ref=self.buf.at[block],
            dst_ref=self.buf.at[block],
            send_sem=self.send.at[0 if way < 0 else 1, block],
            recv_sem=self.recv.at[block],
            device_id={"mp": self.me + way},
            device_id_type=MESH,
        )

    def hand_on(self, block, way):
        pl.when(self.me < self.count - 1 if way > 0 else self.me > 0)(self.copy(block, way).start)

    def start(self):
        self.hand_on(self.me, 1)
        self.hand_on(self.me, -1)

    def take(self, distance):
        low, high = self.me - distance, self.me + distance

        @pl.when(low >= 0)
        def _():
            self.copy(low, -1).wait_recv()
            self.hand_on(low, 1)

        @pl.when(high < self.count)
        def _():
            self.copy(high, 1).wait_recv()
            self.hand_on(high, -1)

    def drain(self):
        def step(block, unused):
            pl.when((block <= self.me) & (self.me < self.count - 1))(self.copy(block, 1).wait_send)
            pl.when((block >= self.me) & (self.me > 0))(self.copy(block, -1).wait_send)
            return unused

        lax.fori_loop(0, self.count, step, 0)


class Scatter:
    def __init__(self, count, held, slots, send, recv):
        self.count, self.held, self.slots, self.send, self.recv = count, held, slots, send, recv
        self.me = lax.axis_index("mp")

    def copy(self, block, part, way):
        slot = block + 1 if way > 0 else block
        return pltpu.make_async_remote_copy(
            src_ref=self.held.at[block, part],
            dst_ref=self.slots.at[slot, part],
            send_sem=self.send.at[block, part],
            recv_sem=self.recv.at[slot, part],
            device_id={"mp": self.me + way},
            device_id_type=MESH,
        )

    def times(self):
        return range(1, 2 * self.count - 3)

    def first(self, block, part):
        pl.when((self.me == 0) & (block > 0))(self.copy(block, part, 1).start)
        pl.when((self.me == self.count - 1) & (block < self.count - 1))(self.copy(block, part, -1).start)

    def pass_part(self, block, part, way):
        self.arrived(block, part, way)
        slot = block + 1 if way > 0 else block
        self.held[block, part] = (
            self.held[block, part].astype(F32) + self.slots[slot, part].astype(F32)).astype(BF)
        self.copy(block, part, way).start()

    def arrived(self, block, part, way):
        slot = block + 1 if way > 0 else block
        pltpu.make_async_remote_copy(
            src_ref=self.held.at[block, part],
            dst_ref=self.slots.at[slot, part],
            send_sem=self.send.at[block, part],
            recv_sem=self.recv.at[slot, part],
            device_id={"mp": self.me - way},
            device_id_type=MESH,
        ).wait_recv()

    def passing(self, time, up_near, down_near):
        last = self.count - 1
        up = time + 1 - self.me if up_near else last + self.me - time
        down = 2 * last - 1 - self.me - time if down_near else time - last + self.me
        up_here = (self.me > 0) & (up > self.me) & (up <= last)
        down_here = (self.me < last) & (down < self.me) & (down >= 0)
        return up, up_here, down, down_here

    def pass_one(self, time, part, up_near, down_near):
        up, up_here, down, down_here = self.passing(time, up_near, down_near)
        pl.when(up_here)(lambda: self.pass_part(up, part, 1))
        pl.when(down_here)(lambda: self.pass_part(down, part, -1))

    def pass_on(self, time, up_near, down_near):
        def step(part, unused):
            self.pass_one(time, part, up_near, down_near)
            return unused

        lax.fori_loop(0, PARTS, step, 0)

    def wait_total(self, part):
        pl.when(self.me > 0)(lambda: self.arrived(self.me, part, 1))
        pl.when(self.me < self.count - 1)(lambda: self.arrived(self.me, part, -1))

    def total(self, part):
        below = jnp.where(self.me > 0, self.slots[self.me + 1, part].astype(F32), 0.0)
        above = jnp.where(self.me < self.count - 1, self.slots[self.me, part].astype(F32), 0.0)
        return self.held[self.me, part].astype(F32) + below + above

    def drain(self):
        def step(block, unused):
            for part in range(PARTS):
                pl.when(block > self.me)(self.copy(block, part, 1).wait_send)
                pl.when(block < self.me)(self.copy(block, part, -1).wait_send)
            return unused

        lax.fori_loop(0, self.count, step, 0)


def norm_rows(source_ref, gain_ref, target_ref):
    step_rows = 64

    def step(index, unused):
        window = pl.ds(pl.multiple_of(index * step_rows, step_rows), step_rows)
        values = source_ref[window, :].astype(F32)
        scale = lax.rsqrt(jnp.mean(values * values, axis=1, keepdims=True) + EPS)
        target_ref[window, :] = (values * scale * gain_ref[...]).astype(BF)
        return unused

    lax.fori_loop(0, source_ref.shape[0] // step_rows, step, 0)


def norm_back(values_ref, gain_ref, scatter, gain_grad_ref, write):
    rows, columns = values_ref.shape
    width = columns // PARTS
    dot_sum = jnp.zeros((rows, 1), F32)
    square_sum = jnp.zeros((rows, 1), F32)
    for part in range(PARTS):
        span = slice(part * width, (part + 1) * width)
        scatter.wait_total(part)
        grad = scatter.total(part)
        values = values_ref[:, span].astype(F32)
        dot_sum = dot_sum + jnp.sum(grad * gain_ref[:, span] * values, axis=1, keepdims=True)
        square_sum = square_sum + jnp.sum(values * values, axis=1, keepdims=True)
    scale = lax.rsqrt(square_sum * (1.0 / columns) + EPS)
    pull = scale * scale * scale * (dot_sum * (1.0 / columns))
    for part in range(PARTS):
        span = slice(part * width, (part + 1) * width)
        grad = scatter.total(part)
        values = values_ref[:, span].astype(F32)
        if gain_grad_ref is not None:
            gain_grad_ref[:, span] = jnp.sum(grad * values * scale, axis=0, keepdims=True)
        write(span, scale * (grad * gain_ref[:, span]) - values * pull)


def live_total(live_ref, row_sums):
    size = live_ref.shape[1]
    same = lax.broadcasted_iota(jnp.int32, (size, size), 0) == lax.broadcasted_iota(jnp.int32, (size, size), 1)
    column = jnp.sum(jnp.where(same, live_ref[...].astype(F32), 0.0), axis=1, keepdims=True)
    return jnp.sum(column * row_sums, axis=0, keepdims=True)


def fill_masks(lengths_ref, rows, mask_ref):
    row = lax.broadcasted_iota(jnp.int32, mask_ref.shape, 0)
    offset = row
    end = 0
    for index in range(lengths_ref.shape[1] - 1):
        end = end + lengths_ref[0, index]
        offset = jnp.where(row >= end, row - end, offset)
    taps = lax.broadcasted_iota(jnp.int32, mask_ref.shape, 1)
    mask_ref[...] = jnp.where((offset >= taps) & (row < rows), 1.0, 0.0)


def fill_square(heads_ref, square_ref):
    square_ref[...] = jnp.zeros(square_ref.shape, BF)
    width = heads_ref.shape[1]
    for head in range(heads_ref.shape[0]):
        span = slice(head * width, (head + 1) * width)
        square_ref[span, span] = heads_ref[head].astype(BF)


def mixer_kernel(count, lengths_ref, tokens_ref, gain_ref, live_ref, taps_ref, shift_ref, rate_bias_ref,
                 inlet_bias_ref, decay_ref, rate_heads_ref, inlet_heads_ref,
                 cot_hbm, value_hbm, gate_hbm, out_hbm,
                 middle_ref, stat_ref, mask_ref, vec_ref, rate_ref, inlet_ref,
                 normed_all, cot_all, mixed_out, vp_out, gp_out, state_out, conv_out, forget_out, input_out,
                 normed, value_w, gate_w, out_w, vp, gp, mixed, state, conv, forget, inlet_gate, low, carry, held,
                 slots, load_sem, own_sem, out_sem, block_sem, ag_send, ag_recv, cot_send, cot_recv, rs_send, rs_recv):
    me = lax.axis_index("mp")
    rows, columns = tokens_ref.shape
    channels = value_w.shape[1]
    width = columns // PARTS
    own_copy = pltpu.make_async_copy(cot_hbm, cot_all.at[me], own_sem)
    own_copy.start()
    loads = [pltpu.make_async_copy(source, target, load_sem.at[index]) for index, (source, target) in enumerate(
        ((value_hbm, value_w), (gate_hbm, gate_w), (out_hbm, out_w)))]
    for load in loads:
        load.start()
    norm_rows(tokens_ref, gain_ref, normed.at[me])
    greet(count)
    gather = Gather(count, normed, ag_send, ag_recv)
    cots = Gather(count, cot_all, cot_send, cot_recv)
    scatter = Scatter(count, held, slots, rs_send, rs_recv)
    gather.start()
    zeros = jnp.zeros((8, channels), F32)
    vp[0:8, :] = zeros
    state[0:8, :] = zeros
    carry[...] = zeros
    fill_masks(lengths_ref, count * rows, mask_ref)
    fill_square(rate_heads_ref, rate_ref)
    fill_square(inlet_heads_ref, inlet_ref)
    vec_ref[0:4, :] = taps_ref[...]
    vec_ref[V_BIAS:V_BIAS + 1, :] = shift_ref[...].reshape(1, channels)
    vec_ref[V_RATE:V_RATE + 1, :] = rate_bias_ref[...].reshape(1, channels)
    vec_ref[V_INLET:V_INLET + 1, :] = inlet_bias_ref[...].reshape(1, channels)
    vec_ref[V_DECAY:V_DECAY + 1, :] = -8.0 * jnp.log1p(jnp.exp(-decay_ref[...].reshape(1, channels)))
    own_copy.wait()
    for load in loads:
        load.wait()

    def block_copy(block):
        return pltpu.make_async_copy(normed.at[block], normed_all.at[block], block_sem.at[block])

    def project(block):
        block_copy(block).start()
        rows_in = normed[block]
        vp[pl.ds(pl.multiple_of(block * rows + 8, 8), rows), :] = dot_nn(rows_in, value_w[...])
        gp[pl.ds(pl.multiple_of(block * rows, rows), rows), :] = dot_nn(rows_in, gate_w[...])

    def mix(block):
        base = block * rows
        rec_forward(base, rows, vp, gp, mask_ref, vec_ref, rate_ref, inlet_ref,
                    mixed, state, conv, forget, inlet_gate, low, carry)
        rows_in = mixed[pl.ds(pl.multiple_of(base, rows), rows), :]
        for part in range(PARTS):
            held[block, part] = dot_nn(rows_in, out_w[:, part * width:(part + 1) * width]).astype(BF)
            scatter.first(block, part)

    def mixed_by(block, distance):
        return (distance >= count - 1) | ((distance >= me) & (block <= me + distance)
                                          & (block < 2 * (distance - me + 1)))

    def arrive(distance, unused):
        pl.when(distance > 0)(lambda: gather.take(distance))
        pl.when((distance == me + 1) & (me < count - 1))(cots.copy(me, 1).start)
        pl.when((distance == count - me) & (me > 0))(cots.copy(me, -1).start)

        def side(which, inner):
            block = me - distance + 2 * distance * which
            pl.when((block >= 0) & (block < count) & ((distance > 0) | (which == 0)))(lambda: project(block))
            return inner

        lax.fori_loop(0, 2, side, unused)

        def turn(block, inner):
            before = (distance > 0) & mixed_by(block, distance - 1)
            pl.when(mixed_by(block, distance) & jnp.logical_not(before))(lambda: mix(block))
            return inner

        return lax.fori_loop(0, count, turn, unused)

    lax.fori_loop(0, count, arrive, 0)
    saves = [pltpu.make_async_copy(source, target, out_sem.at[index]) for index, (source, target) in enumerate(
        ((mixed, mixed_out), (vp, vp_out), (gp, gp_out), (state, state_out), (conv, conv_out),
         (forget, forget_out), (inlet_gate, input_out)))]
    for save in saves:
        save.start()
    taken = 1
    for time in scatter.times():
        if taken < count and time >= 2 * taken - 1:
            cots.take(taken)
            taken += 1
        scatter.pass_on(time, True, False)
    for distance in range(taken, count):
        cots.take(distance)
    row_sums = jnp.zeros((rows, 1), F32)
    token_sums = jnp.zeros((rows, 1), F32)
    for part in range(PARTS):
        span = slice(part * width, (part + 1) * width)
        scatter.wait_total(part)
        total = scatter.total(part)
        tokens = tokens_ref[:, span].astype(F32)
        row_sums = row_sums + jnp.sum(total * total, axis=1, keepdims=True)
        token_sums = token_sums + jnp.sum(tokens * tokens, axis=1, keepdims=True)
        middle_ref[:, span] = tokens + total
    stat_ref[...] = jnp.zeros(stat_ref.shape, F32)
    stat_ref[0:1, :] += live_total(live_ref, token_sums)
    stat_ref[1:2, :] += live_total(live_ref, row_sums)
    stat_ref[2:3, :] += live_total(live_ref, jnp.ones((rows, 1), F32))
    for save in saves:
        save.wait()
    for block in range(count):
        block_copy(block).wait()
    gather.drain()
    cots.drain()
    scatter.drain()


def call_mixer(count, lengths, tokens, gain, live, taps, vectors, rate_heads, inlet_heads, cotangent, value_proj, gate_proj, mixer_out):
    rows, columns = tokens.shape
    channels = value_proj.shape[1]
    total = count * rows
    wide = jax.ShapeDtypeStruct((total, channels), F32)
    ahead = jax.ShapeDtypeStruct((total + 8, channels), F32)
    blocks = jax.ShapeDtypeStruct((count, rows, columns), BF)
    square = jax.ShapeDtypeStruct((channels, channels), BF)
    return pl.pallas_call(
        functools.partial(mixer_kernel, count),
        out_shape=(
            jax.ShapeDtypeStruct((rows, columns), F32), jax.ShapeDtypeStruct((8, 128), F32),
            jax.ShapeDtypeStruct((total + 8, 8), F32), jax.ShapeDtypeStruct((8, channels), F32), square, square,
            blocks, blocks, jax.ShapeDtypeStruct((total, channels), BF), ahead, wide, ahead, wide, wide, wide,
        ),
        in_specs=[pl.BlockSpec(memory_space=pltpu.SMEM)] + [IN_VMEM] * 10 + [ANYWHERE] * 4,
        out_specs=(IN_VMEM,) * 6 + (ANYWHERE,) * 9,
        scratch_shapes=[
            pltpu.VMEM((count, rows, columns), BF),
            pltpu.VMEM((columns, channels), BF),
            pltpu.VMEM((columns, channels), BF),
            pltpu.VMEM((channels, columns), BF),
            pltpu.VMEM((total + 8, channels), F32),
            pltpu.VMEM((total, channels), F32),
            pltpu.VMEM((total, channels), BF),
            pltpu.VMEM((total + 8, channels), F32),
            pltpu.VMEM((total, channels), F32),
            pltpu.VMEM((total, channels), F32),
            pltpu.VMEM((total, channels), F32),
            pltpu.VMEM((rows, channels), BF),
            pltpu.VMEM((8, channels), F32),
            pltpu.VMEM((count, PARTS, rows, columns // PARTS), BF),
            pltpu.VMEM((count + 1, PARTS, rows, columns // PARTS), BF),
            DMA((3,)), DMA, DMA((7,)), DMA((count,)),
            DMA((2, count)), DMA((count,)), DMA((2, count)), DMA((count,)),
            DMA((count, PARTS)), DMA((count + 1, PARTS)),
        ],
        compiler_params=pltpu.CompilerParams(vmem_limit_bytes=VMEM_LIMIT, collective_id=1, has_side_effects=True),
        cost_estimate=pl.CostEstimate(flops=6 * total * columns * channels, bytes_accessed=40 * total * channels,
                                      transcendentals=6 * total * channels),
    )(lengths, tokens, gain, live, taps, *vectors, rate_heads, inlet_heads, cotangent,
      value_proj, gate_proj, mixer_out)


def middle_kernel(count, groups, middle_grad_ref, middle_ref, live_ref, terms_hbm, out_hbm, mixed_hbm,
                  gate_hbm, value_hbm, layer_ref, stat_ref, out_grad_ref, gate_sum_ref, value_sum_ref, dm_hbm,
                  low, out_w, mixed, dm, held, slots, cube_a, slots_a, cube_b, slots_b, gate_held, gate_slots, value_held, value_slots,
                  load_sem, dm_sem, ag_send, ag_recv, rs_send, rs_recv, a_send, a_recv, b_send, b_recv,
                  gate_send, gate_recv, value_send, value_recv):
    me = lax.axis_index("mp")
    rows, columns = middle_ref.shape
    channels = out_w.shape[0]
    width = columns // PARTS
    chunk = columns // groups
    half = channels // 2
    loads = [pltpu.make_async_copy(source, target, load_sem.at[index]) for index, (source, target) in enumerate(
        ((gate_hbm, gate_held), (value_hbm, value_held), (out_hbm, out_w), (mixed_hbm, mixed), (terms_hbm, held)))]
    for load in loads:
        load.start()
    low[me] = middle_grad_ref[...].astype(BF)
    greet(count, groups)
    gather = Gather(count, low, ag_send, ag_recv)
    scatter = Scatter(count, held, slots, rs_send, rs_recv)
    order_a, order_b = orders(groups)
    cubes = (Cube(groups, order_a, cube_a, slots_a, a_send, a_recv),
             Cube(groups, order_b, cube_b, slots_b, b_send, b_recv))
    dense_cubes = (Cube(groups, order_a, gate_held, gate_slots, gate_send, gate_recv),
                   Cube(groups, order_b, value_held, value_slots, value_send, value_recv))
    levels = len(order_a)
    gather.start()
    for load in loads:
        load.wait()
    for cube in dense_cubes:
        cube.start(0)

    def dense_advance(level):
        for cube in dense_cubes:
            cube.finish(level)
            if level + 1 < levels:
                cube.start(level + 1)

    def dm_copy(block):
        return pltpu.make_async_copy(dm.at[block], dm_hbm.at[pl.ds(pl.multiple_of(block * rows, rows), rows)],
                                     dm_sem.at[block])

    def back(block):
        dm[block] = dot_nt(low[block], out_w[...])
        dm_copy(block).start()

    back(me)
    dense_advance(0)
    for distance in range(1, count):
        gather.take(distance)
        if distance == 1:
            for step in range(count - 1):
                for part in range(PARTS):
                    pl.when(me == 0)(scatter.copy(count - 1 - step, part, 1).start)
                    pl.when(me == count - 1)(scatter.copy(step, part, -1).start)
        pl.when(me - distance >= 0)(lambda: back(me - distance))
        pl.when(me + distance < count)(lambda: back(me + distance))
        if distance == count - 2:
            scatter.pass_on(1, False, False)
            dense_advance(1)

    def out_grad(index, unused):
        right = low[:, :, pl.ds(pl.multiple_of(index * chunk, chunk), chunk)].reshape(count * rows, chunk)
        both = dot_tn(mixed[...], right).astype(BF)
        cube_a[index] = both[:half]
        cube_b[index] = both[half:]
        return unused

    lax.fori_loop(0, groups, out_grad, 0)
    for cube in cubes:
        cube.start(0)
    level = 0
    for time in list(scatter.times())[1:]:
        scatter.pass_on(time, False, False)
        if time == 2:
            for rest in range(2, levels):
                dense_advance(rest)
            dense_cubes[0].result(gate_sum_ref)
            dense_cubes[1].result(value_sum_ref)
        if level < levels:
            for cube in cubes:
                cube.finish(level)
                if level + 1 < levels:
                    cube.start(level + 1)
            level += 1
    for rest in range(level, levels):
        for cube in cubes:
            cube.finish(rest)
            if rest + 1 < levels:
                cube.start(rest + 1)
    cubes[0].result(out_grad_ref.at[0:half])
    cubes[1].result(out_grad_ref.at[half:channels])
    row_sums = jnp.zeros((rows, 1), F32)
    for part in range(PARTS):
        span = slice(part * width, (part + 1) * width)
        scatter.wait_total(part)
        total = scatter.total(part)
        row_sums = row_sums + jnp.sum(total * total, axis=1, keepdims=True)
        layer_ref[:, span] = (middle_ref[:, span] + total).astype(BF)
    stat_ref[...] = jnp.zeros(stat_ref.shape, F32) + live_total(live_ref, row_sums)
    for block in range(count):
        dm_copy(block).wait()
    gather.drain()
    scatter.drain()


def call_middle(count, groups, middle_grad, middle, live, terms, mixer_out, mixed, gate_weights, value_weights):
    rows, columns = middle.shape
    channels = mixer_out.shape[0]
    total = count * rows
    chunk = columns // groups
    units = gate_weights.shape[1]
    split = (groups, chunk, units)
    return pl.pallas_call(
        functools.partial(middle_kernel, count, groups),
        out_shape=(
            jax.ShapeDtypeStruct((rows, columns), BF), jax.ShapeDtypeStruct((8, 128), F32),
            jax.ShapeDtypeStruct((channels, chunk), F32), jax.ShapeDtypeStruct((chunk, units), F32),
            jax.ShapeDtypeStruct((chunk, units), F32), jax.ShapeDtypeStruct((total, channels), F32),
        ),
        in_specs=[IN_VMEM] * 3 + [ANYWHERE] * 5,
        out_specs=(IN_VMEM,) * 5 + (ANYWHERE,),
        scratch_shapes=[
            pltpu.VMEM((count, rows, columns), BF),
            pltpu.VMEM((channels, columns), BF),
            pltpu.VMEM((total, channels), BF),
            pltpu.VMEM((count, rows, channels), F32),
            pltpu.VMEM((count, PARTS, rows, columns // PARTS), BF),
            pltpu.VMEM((count + 1, PARTS, rows, columns // PARTS), BF),
            pltpu.VMEM((groups, channels // 2, chunk), BF),
            pltpu.VMEM((groups - 1, channels // 2, chunk), BF),
            pltpu.VMEM((groups, channels // 2, chunk), BF),
            pltpu.VMEM((groups - 1, channels // 2, chunk), BF),
            pltpu.VMEM(split, BF), pltpu.VMEM((groups - 1, chunk, units), BF),
            pltpu.VMEM(split, BF), pltpu.VMEM((groups - 1, chunk, units), BF),
            DMA((5,)), DMA((count,)), DMA((2, count)), DMA((count,)), DMA((count, PARTS)), DMA((count + 1, PARTS)),
            DMA((groups - 1,)), DMA((groups - 1,)), DMA((groups - 1,)), DMA((groups - 1,)),
            DMA((groups - 1,)), DMA((groups - 1,)), DMA((groups - 1,)), DMA((groups - 1,)),
        ],
        compiler_params=pltpu.CompilerParams(vmem_limit_bytes=VMEM_LIMIT, collective_id=2, has_side_effects=True),
        cost_estimate=pl.CostEstimate(flops=4 * total * columns * channels, bytes_accessed=40 * total * channels,
                                      transcendentals=0),
    )(middle_grad, middle, live, terms, mixer_out, mixed, gate_weights.reshape(split), value_weights.reshape(split))


def input_kernel(count, groups, heads, tokens_ref, gain_ref, middle_grad_ref, mask_ref, vec_ref, rate_ref, inlet_ref,
                 dense_gain_ref, stat_ref, dense_stat_ref, value_hbm, gate_hbm, normed_hbm, dm_hbm, vp_hbm, gp_hbm, state_hbm, conv_hbm, forget_hbm, input_hbm,
                 input_grad_ref, flat_ref, value_grad_ref, gate_grad_ref, full, vec_grad_ref,
                 value_w, gate_w, dm, vp, gp, state, conv, forget, inlet_gate, normed, vlow, glow, dzf, dzi, dconv,
                 clow, sums, carry, held, slots, cube_a, slots_a, cube_b, slots_b, cube_c, slots_c,
                 vec_held, vec_slots, flat_held, flat_slots,
                 load_sem, block_sem, normed_sem, rs_send, rs_recv, a_send, a_recv, b_send, b_recv, c_send, c_recv,
                 f_send, f_recv, v_send, v_recv, flat_send, flat_recv):
    me = lax.axis_index("mp")
    rows, columns = tokens_ref.shape
    channels = value_w.shape[1]
    width = columns // PARTS
    chunk = columns // groups
    total_rows = count * rows
    head = channels // heads
    loads = [pltpu.make_async_copy(value_hbm, value_w, load_sem.at[0]),
             pltpu.make_async_copy(gate_hbm, gate_w, load_sem.at[1])]
    for load in loads:
        load.start()

    def block_loads(block, slot):
        at = pl.multiple_of(block * rows, rows)
        plain = pl.ds(at, rows)
        ahead = pl.ds(at, rows + 8)
        return [pltpu.make_async_copy(source.at[window], target.at[slot], block_sem.at[slot, index])
                for index, (source, window, target) in enumerate((
                    (dm_hbm, plain, dm), (vp_hbm, ahead, vp), (gp_hbm, plain, gp), (state_hbm, ahead, state),
                    (conv_hbm, plain, conv), (forget_hbm, plain, forget), (input_hbm, plain, inlet_gate)))]

    for load in block_loads(count - 1, 0):
        load.start()
    zeros = jnp.zeros((8, channels), F32)
    dconv[rows:rows + 8, :] = zeros
    carry[...] = zeros
    for row in range(8):
        sums[row] = zeros
    greet(count, groups, True)
    scatter = Scatter(count, held, slots, rs_send, rs_recv)
    order_a, order_b = orders(groups)
    cubes = (Cube(groups, order_a, cube_a, slots_a, a_send, a_recv),
             Cube(groups, order_b, cube_b, slots_b, b_send, b_recv),
             Cube(groups, order_b, cube_c, slots_c, c_send, c_recv))
    spread = Spread(cubes[2], full, f_send, f_recv)
    for load in loads:
        load.wait()

    def back(step, unused):
        block = count - 1 - step
        slot = step % 2
        for load in block_loads(block, slot):
            load.wait()

        @pl.when(step + 1 < count)
        def _():
            for load in block_loads(block - 1, 1 - slot):
                load.start()

        base = block * rows
        rec_backward(base, rows, dm.at[slot], vp.at[slot], gp.at[slot], mask_ref, vec_ref, rate_ref, inlet_ref,
                     state.at[slot], conv.at[slot], forget.at[slot], inlet_gate.at[slot],
                     vlow, glow, dzf, dzi, dconv, clow, sums, carry)
        window = pl.ds(pl.multiple_of(base, rows), rows)
        for part in range(PARTS):
            span = slice(part * width, (part + 1) * width)
            held[block, part] = (dot_nt(vlow[window, :], value_w[span, :])
                                 + dot_nt(glow[window, :], gate_w[span, :])).astype(BF)
            scatter.first(block, part)
        return unused

    def normed_copy(index, slot):
        return pltpu.make_async_copy(
            normed_hbm.at[:, :, pl.ds(pl.multiple_of(index * chunk, chunk), chunk)], normed.at[slot],
            normed_sem.at[slot])

    normed_copy(0, 0).start()
    lax.fori_loop(0, count, back, 0)

    def weights(index, unused):
        slot = index % 2
        normed_copy(index, slot).wait()
        pl.when(index + 1 < groups)(lambda: normed_copy(index + 1, 1 - slot).start())
        left = normed[slot].reshape(total_rows, chunk)
        cube_a[index] = dot_tn(left, vlow[...]).astype(BF)
        cube_b[index] = dot_tn(left, glow[...]).astype(BF)
        part = index * chunk // width
        inside = pl.ds(pl.multiple_of(index * chunk % width, chunk), chunk)
        gain_row = jnp.zeros((1, chunk), F32)
        for block in range(count):
            gain_row = gain_row + jnp.sum(
                normed[slot, block].astype(F32) * held[block, part, :, inside].astype(F32), axis=0, keepdims=True)
        flat_held[0:1, pl.ds(pl.multiple_of(index * chunk, chunk), chunk)] = gain_row
        return unused

    flat_held[...] = jnp.zeros(flat_held.shape, F32)
    lax.fori_loop(0, groups, weights, 0)
    flat_held[0:1, :] = flat_held[0:1, :] / gain_ref[...]
    flat_held[1:2, :] = dense_gain_ref[...]
    for index, value in enumerate((stat_ref[0:1], stat_ref[1:2], dense_stat_ref[0:1], stat_ref[2:3])):
        flat_held[2:3, index * 128:(index + 1) * 128] = value
    peers = [("dp", bit) for bit in range(groups.bit_length() - 1)]
    peers += [("mp", bit) for bit in range(count.bit_length() - 1)]

    def flat_copy(index):
        axis, bit = peers[index]
        return pltpu.make_async_remote_copy(
            src_ref=flat_held, dst_ref=flat_slots.at[index], send_sem=flat_send.at[index],
            recv_sem=flat_recv.at[index], device_id={axis: partner_of(bit, axis)}, device_id_type=MESH)

    flat_copy(0).start()
    cubes[0].start(0)
    cubes[1].start(0)
    slab = 2 * channels // groups
    for which, source in enumerate((dzf, dzi)):
        for index in range(heads):
            span = slice(index * head, (index + 1) * head)
            square = dot_tn(clow[:, span], source[:, span])
            first = (which * channels + index * head) // slab
            for piece in range(head // slab):
                cube_c[first + piece] = square[piece * slab:(piece + 1) * slab]
    cubes[2].start(0)
    for row in range(8):
        vec_held[0, row:row + 1, :] = jnp.sum(sums[row], axis=0, keepdims=True)

    def vec_copy(level):
        return pltpu.make_async_remote_copy(
            src_ref=vec_held.at[level], dst_ref=vec_slots.at[level], send_sem=v_send.at[level],
            recv_sem=v_recv.at[level], device_id={"dp": partner_of(level)}, device_id_type=MESH)

    levels = len(order_a)
    vec_copy(0).start()

    def advance(level):
        if level < len(peers):
            flat_copy(level).wait()
            flat_held[...] += flat_slots[level]
            if level + 1 < len(peers):
                flat_copy(level + 1).start()
        if level < levels:
            for cube in cubes:
                cube.finish(level)
                if level + 1 < levels:
                    cube.start(level + 1)
            vec_copy(level).wait()
            if level + 1 < levels:
                vec_held[level + 1] = vec_held[level] + vec_slots[level]
                vec_copy(level + 1).start()
            else:
                vec_grad_ref[...] = vec_held[level] + vec_slots[level]
                cubes[0].result(value_grad_ref)
                cubes[1].result(gate_grad_ref)
                cubes[2].result(full.at[lax.axis_index("dp")])
                spread.start(levels - 1)
        elif level < 2 * levels:
            back_level = 2 * levels - 1 - level
            spread.finish(back_level)
            if back_level > 0:
                spread.start(back_level - 1)

    stages = max(2 * levels, len(peers))
    slots_all = [(time, part) for time in scatter.times() for part in range(PARTS)]
    early = max(len(slots_all) - 5 - 2 * (stages - 4), 0)
    for time in range(1, early // PARTS + 1):
        scatter.pass_on(time, False, True)
    level = 0
    for index in range(early // PARTS * PARTS, len(slots_all)):
        scatter.pass_one(*slots_all[index], False, True)
        turn = len(slots_all) - index - 1
        if level < stages and (turn <= 4 or turn % 2 == 0) and turn > 0 and stages - level >= min(turn, 4):
            advance(level)
            level += 1
    for rest in range(level, stages):
        advance(rest)
    flat_ref[...] = flat_held[...]
    def write(span, change):
        input_grad_ref[:, span] = (middle_grad_ref[:, span] + change).astype(BF)

    norm_back(tokens_ref, gain_ref, scatter, None, write)
    scatter.drain()


def call_input(count, groups, heads, tokens, gain, middle_grad, masks, vec, rate, inlet, dense_gain_grad, stat,
               dense_stat, value_proj, gate_proj, normed_all, dm, vp, gp, state, conv, forget, inp):
    rows, columns = tokens.shape
    channels = value_proj.shape[1]
    total = count * rows
    chunk = columns // groups
    head = channels // heads
    slab = 2 * channels // groups
    plain = pltpu.VMEM((2, rows, channels), F32)
    ahead = pltpu.VMEM((2, rows + 8, channels), F32)
    low = pltpu.VMEM((total, channels), BF)
    levels = groups.bit_length() - 1
    flats = levels + count.bit_length() - 1
    return pl.pallas_call(
        functools.partial(input_kernel, count, groups, heads),
        out_shape=(
            jax.ShapeDtypeStruct((rows, columns), BF), jax.ShapeDtypeStruct((8, columns), F32),
            jax.ShapeDtypeStruct((chunk, channels), F32), jax.ShapeDtypeStruct((chunk, channels), F32),
            jax.ShapeDtypeStruct((groups, slab, head), F32), jax.ShapeDtypeStruct((8, channels), F32),
        ),
        in_specs=[IN_VMEM] * 10 + [ANYWHERE] * 10,
        out_specs=(IN_VMEM,) * 6,
        scratch_shapes=[
            pltpu.VMEM((columns, channels), BF),
            pltpu.VMEM((columns, channels), BF),
            plain, ahead, plain, ahead, plain, plain, plain,
            pltpu.VMEM((2, count, rows, chunk), BF),
            low, low, low, low,
            pltpu.VMEM((rows + 8, channels), F32),
            low,
            pltpu.VMEM((8, 8, channels), F32),
            pltpu.VMEM((8, channels), F32),
            pltpu.VMEM((count, PARTS, rows, columns // PARTS), BF),
            pltpu.VMEM((count + 1, PARTS, rows, columns // PARTS), BF),
            pltpu.VMEM((groups, chunk, channels), BF), pltpu.VMEM((groups - 1, chunk, channels), BF),
            pltpu.VMEM((groups, chunk, channels), BF), pltpu.VMEM((groups - 1, chunk, channels), BF),
            pltpu.VMEM((groups, slab, head), F32), pltpu.VMEM((groups - 1, slab, head), F32),
            pltpu.VMEM((levels, 8, channels), F32), pltpu.VMEM((levels, 8, channels), F32),
            pltpu.VMEM((8, columns), F32), pltpu.VMEM((flats, 8, columns), F32),
            DMA((2,)), DMA((2, 7)), DMA((2,)), DMA((count, PARTS)), DMA((count + 1, PARTS)),
            DMA((groups - 1,)), DMA((groups - 1,)), DMA((groups - 1,)), DMA((groups - 1,)),
            DMA((groups - 1,)), DMA((groups - 1,)), DMA((groups - 1,)), DMA((groups - 1,)),
            DMA((levels,)), DMA((levels,)), DMA((flats,)), DMA((flats,)),
        ],
        compiler_params=pltpu.CompilerParams(vmem_limit_bytes=VMEM_LIMIT, collective_id=3, has_side_effects=True),
        cost_estimate=pl.CostEstimate(flops=8 * total * columns * channels, bytes_accessed=60 * total * channels,
                                      transcendentals=4 * total * channels),
    )(tokens, gain, middle_grad, masks, vec, rate, inlet, dense_gain_grad, stat, dense_stat, value_proj, gate_proj,
      normed_all, dm, vp, gp, state, conv, forget, inp)


def spans(total):
    size = 512 if total % 512 == 0 else 256
    return [slice(at, at + size) for at in range(0, total, size)]


def dense_kernel(count, groups, middle_ref, gain_ref, cot_hbm, gate_hbm, value_hbm, down_hbm,
                 middle_grad_ref, gain_grad_ref, dense_part_hbm, gate_out, value_out, down_out,
                 normed, cot, gate_w, value_w, down_w, hidden, gate_g, value_g, dense_part, held, slots, stage,
                 load_sem, cot_sem, part_sem, stage_sem, ag_send, ag_recv, rs_send, rs_recv):
    me = lax.axis_index("mp")
    rows, columns = middle_ref.shape
    units = gate_w.shape[1]
    width = columns // PARTS
    loads = [pltpu.make_async_copy(gate_hbm, gate_w, load_sem.at[0]),
             pltpu.make_async_copy(value_hbm, value_w, load_sem.at[1]),
             pltpu.make_async_copy(down_hbm, down_w, load_sem.at[2])]
    for load in loads:
        load.start()

    def cot_copy(block):
        return pltpu.make_async_copy(cot_hbm.at[block],
                                     cot.at[block], cot_sem.at[block])

    for block in range(count):
        cot_copy(block).start()
    greet(count)
    gather = Gather(count, normed, ag_send, ag_recv)
    scatter = Scatter(count, held, slots, rs_send, rs_recv)
    norm_rows(middle_ref, gain_ref, normed.at[me])
    gather.start()
    for load in loads:
        load.wait()
    pieces = 3
    piece = units // pieces

    def part_copy(block, slot):
        return pltpu.make_async_copy(dense_part.at[slot], dense_part_hbm.at[block], part_sem.at[slot])

    def compute(block, slot, reuse):
        cot_copy(block).wait()
        rows_in = normed[block]
        rows_cot = cot[block]
        for index in range(pieces):
            span = slice(index * piece, (index + 1) * piece)
            gate_linear = dot_nn(rows_in, gate_w[:, span])
            value_linear = dot_nn(rows_in, value_w[:, span])
            hidden_grad = dot_nt(rows_cot, down_w[span, :])
            act, slope = gelu_both(gate_linear)
            hidden[block, :, span] = (act * value_linear).astype(BF)
            gate_g[block, :, span] = (hidden_grad * value_linear * slope).astype(BF)
            value_g[block, :, span] = (hidden_grad * act).astype(BF)
        for part in range(PARTS):
            span = slice(part * width, (part + 1) * width)
            held[block, part] = (dot_nt(gate_g[block], gate_w[span, :])
                                 + dot_nt(value_g[block], value_w[span, :])).astype(BF)
            scatter.first(block, part)
        pl.when(reuse)(lambda: part_copy(block, slot).wait())
        for part in range(PARTS):
            span = slice(part * width, (part + 1) * width)
            dense_part[slot, part] = dot_nn(hidden[block], down_w[:, span]).astype(BF)
        part_copy(block, slot).start()

    def arrive(distance, unused):
        pl.when(distance > 0)(lambda: gather.take(distance))

        def side(which, inner):
            block = me - distance + 2 * distance * which
            pl.when((block >= 0) & (block < count) & ((distance > 0) | (which == 0)))(
                lambda: compute(block, which, (distance > 1) | ((distance == 1) & (which == 0))))
            return inner

        return lax.fori_loop(0, 2, side, unused)

    lax.fori_loop(0, count, arrive, 0)

    total_rows = count * rows
    left_rows = columns // 4
    unit_rows = units // 4
    group_width = columns // groups

    def stage_copy(kind, index, slot):
        if kind == 2:
            half = columns // 2
            return pltpu.make_async_copy(
                stage.at[slot, pl.ds(0, unit_rows), pl.ds(0, half)],
                down_out.at[pl.ds(index // 2 * unit_rows, unit_rows), pl.ds(index % 2 * half, half)],
                stage_sem.at[slot])
        target = gate_out if kind == 0 else value_out
        return pltpu.make_async_copy(
            stage.at[slot, pl.ds(0, left_rows), pl.ds(0, units)],
            target.at[pl.ds(index * left_rows, left_rows)], stage_sem.at[slot])

    def grads(kind, index, slot):
        if kind == 2:
            low = index // 2 * unit_rows
            left = hidden[:, :, low:low + unit_rows].reshape(total_rows, unit_rows)
            for span in spans(columns // 2):
                at = index % 2 * (columns // 2) + span.start
                size = span.stop - span.start
                right = cot[:, :, at:at + size].reshape(total_rows, size)
                stage[slot, 0:unit_rows, span] = dot_tn(left, right).astype(BF)
        else:
            left = normed[:, :, index * left_rows:(index + 1) * left_rows].reshape(total_rows, left_rows)
            source = gate_g if kind == 0 else value_g
            for span in spans(units):
                right = source[:, :, span].reshape(total_rows, span.stop - span.start)
                stage[slot, 0:left_rows, span] = dot_tn(left, right).astype(BF)

    work = [(kind, index) for kind in (0, 1, 2) for index in range((4, 4, 8)[kind])]
    started = []
    times = scatter.times()
    per_step = -(-len(work) // (len(times) + 1))
    for step in range(len(times) + 1):
        if step > 0:
            scatter.pass_on(step, True, True)
        for kind, index in work[step * per_step:(step + 1) * per_step]:
            slot = len(started) % 2
            if len(started) >= 2:
                stage_copy(*started[-2], slot).wait()
            grads(kind, index, slot)
            stage_copy(kind, index, slot).start()
            started.append((kind, index))
    for back in (2, 1):
        stage_copy(*started[-back], (len(started) - back) % 2).wait()

    def write(span, change):
        middle_grad_ref[:, span] = cot[me, :, span].astype(F32) + change

    norm_back(middle_ref, gain_ref, scatter, gain_grad_ref, write)
    part_copy(0, 0).wait()
    pl.when(me < count - 1)(part_copy(0, 1).wait)
    gather.drain()
    scatter.drain()


def call_dense(count, groups, middle, gain, cot_all, dense_gate, dense_value, dense_down):
    rows, columns = middle.shape
    units = dense_gate.shape[1]
    width = columns // PARTS
    any_spec = pl.BlockSpec(memory_space=pl.ANY)
    vmem = pl.BlockSpec(memory_space=pltpu.VMEM)
    dma = pltpu.SemaphoreType.DMA
    return pl.pallas_call(
        functools.partial(dense_kernel, count, groups),
        out_shape=(
            jax.ShapeDtypeStruct((rows, columns), F32),
            jax.ShapeDtypeStruct((1, columns), F32),
            jax.ShapeDtypeStruct((count, PARTS, rows, width), BF),
            jax.ShapeDtypeStruct((columns, units), BF),
            jax.ShapeDtypeStruct((columns, units), BF),
            jax.ShapeDtypeStruct((units, columns), BF),
        ),
        in_specs=[vmem, vmem, any_spec, any_spec, any_spec, any_spec],
        out_specs=(vmem, vmem, any_spec, any_spec, any_spec, any_spec),
        scratch_shapes=[
            pltpu.VMEM((count, rows, columns), BF),
            pltpu.VMEM((count, rows, columns), BF),
            pltpu.VMEM((columns, units), BF),
            pltpu.VMEM((columns, units), BF),
            pltpu.VMEM((units, columns), BF),
            pltpu.VMEM((count, rows, units), BF),
            pltpu.VMEM((count, rows, units), BF),
            pltpu.VMEM((count, rows, units), BF),
            pltpu.VMEM((2, PARTS, rows, width), BF),
            pltpu.VMEM((count, PARTS, rows, width), BF),
            pltpu.VMEM((count + 1, PARTS, rows, width), BF),
            pltpu.VMEM((2, columns // 4, max(units, columns // 2)), BF),
            dma((3,)), dma((count,)), dma((2,)), dma((2,)),
            dma((2, count)), dma((count,)), dma((count, PARTS)), dma((count + 1, PARTS)),
        ],
        compiler_params=pltpu.CompilerParams(
            vmem_limit_bytes=VMEM_LIMIT, collective_id=0, has_side_effects=True),
        cost_estimate=pl.CostEstimate(flops=18 * count * rows * columns * units,
                                      bytes_accessed=12 * columns * units, transcendentals=count * rows * units),
    )(middle, gain, cot_all, dense_gate, dense_value, dense_down)


def scatter_dp(values, dimension):
    return lax.psum_scatter(values, "dp", scatter_dimension=dimension, tiled=True).astype(F32)


def local(groups, tokens, cotangent, lengths, live_mask, mixer_gain, value_proj, gate_proj, conv_taps, conv_bias,
          rate_weight, rate_bias, inlet_weight, inlet_bias, decay_param, mixer_out, dense_gain,
          dense_gate, dense_value, dense_down):
    columns = tokens.shape[1]
    head_count, head_width = rate_weight.shape[:2]
    channels = head_count * head_width
    count = lax.axis_size("mp")
    live = live_mask[None, :]
    middle, stat, masks, vec, rate_square, inlet_square, normed_all, cot_all, mixed, *saved = call_mixer(
        count, lengths, tokens, mixer_gain[None, :], live, conv_taps,
        (conv_bias, rate_bias, inlet_bias, decay_param), rate_weight, inlet_weight, cotangent,
        value_proj, gate_proj, mixer_out)
    middle_grad, dense_gain_grad, dense_terms, gate_weights, value_weights, down_weights = call_dense(
        count, groups, middle, dense_gain[None, :], cot_all, dense_gate, dense_value, dense_down)
    layer_out, dense_stat, mixer_out_sum, gate_sum, value_sum, dm = call_middle(
        count, groups, middle_grad, middle, live, dense_terms, mixer_out, mixed, gate_weights, value_weights)
    dm, down_weights = lax.optimization_barrier((dm, down_weights))
    input_grad, flat, value_proj_sum, gate_proj_sum, small, vec_sum = call_input(
        count, groups, head_count, tokens, mixer_gain[None, :], middle_grad, masks, vec, rate_square, inlet_square,
        dense_gain_grad, stat, dense_stat, value_proj, gate_proj, normed_all, dm, *saved)
    branch_rms = jnp.sqrt(flat[2, 0:384:128] / (flat[2, 384] * columns))
    decay_scale = 8.0 * jax.nn.sigmoid(-decay_param)
    return (
        layer_out,
        input_grad,
        flat[0],
        value_proj_sum,
        gate_proj_sum,
        vec_sum[0:4],
        vec_sum[4],
        small[:groups // 2].reshape(rate_weight.shape),
        vec_sum[V_RATE],
        small[groups // 2:].reshape(rate_weight.shape),
        vec_sum[V_INLET],
        vec_sum[V_DECAY] * decay_scale,
        mixer_out_sum,
        flat[1],
        gate_sum,
        value_sum,
        scatter_dp(down_weights, 1),
        branch_rms,
    )


def solution(mesh):
    rows = P(("dp", "mp"), None)
    return jax.shard_map(
        functools.partial(local, mesh.shape["dp"]),
        mesh=mesh,
        in_specs=(
            rows, rows, P("dp", None), P(("dp", "mp")), P(),
            P(None, "mp"), P(None, "mp"), P(None, "mp"), P("mp"),
            P("mp", None, None), P("mp"), P("mp", None, None), P("mp"), P("mp"),
            P("mp", None), P(), P(None, "mp"), P(None, "mp"), P("mp", None),
        ),
        out_specs=(
            rows, rows, P(), P("dp", "mp"), P("dp", "mp"),
            P(None, "mp"), P("mp"), P("mp", None, None), P("mp"), P("mp", None, None), P("mp"), P("mp"),
            P("mp", "dp"), P(), P("dp", "mp"), P("dp", "mp"), P("mp", "dp"), P(),
        ),
        check_vma=False,
    )
```

```python
import functools

import jax
import jax.numpy as jnp
from jax import lax
from jax.experimental import pallas as pl
from jax.experimental.pallas import tpu as pltpu
from jax.sharding import PartitionSpec as P

EPS = 1e-06
BF = jnp.bfloat16
F32 = jnp.float32
GELU_C = 0.7978845608028654
GELU_A = 0.044715
CHUNK = 16
VMEM_LIMIT = 60 * 1024 * 1024


def dot_nn(left, right):
    return jnp.dot(left, right, preferred_element_type=F32)


def dot_nt(left, right):
    return lax.dot_general(left, right, (((1,), (1,)), ((), ())), preferred_element_type=F32)


def dot_tn(left, right):
    return lax.dot_general(left, right, (((0,), (0,)), ((), ())), preferred_element_type=F32)


def gelu(x):
    return 0.5 * x * (1.0 + jnp.tanh(GELU_C * (x + GELU_A * x * x * x)))


def gelu_both(x):
    square = x * x
    tanh_in = jnp.tanh(GELU_C * x * (1.0 + GELU_A * square))
    half = 0.5 * (1.0 + tanh_in)
    slope = half + 0.5 * x * (1.0 - tanh_in * tanh_in) * (GELU_C * (1.0 + 3.0 * GELU_A * square))
    return half * x, slope


def sigmoid(x):
    return 1.0 / (1.0 + jnp.exp(-x))


def one_minus_square(log_decay, carried):
    y = 2.0 * log_decay
    series = 1.0 + y * (1.0 / 7.0)
    for k in (6.0, 5.0, 4.0, 3.0, 2.0):
        series = 1.0 + y * (1.0 / k) * series
    return jnp.where(y > -0.5, -y * series, 1.0 - carried * carried)


def row_in_tile(shape):
    return lax.broadcasted_iota(jnp.int32, shape, 0) % 8


def scan_tile_down(mult, add):
    row = row_in_tile(mult.shape)
    for step in (1, 2, 4):
        keep = row >= step
        add_up = jnp.where(keep, pltpu.roll(add, step, 0), 0.0)
        mult_up = jnp.where(keep, pltpu.roll(mult, step, 0), 1.0)
        add = add + mult * add_up
        mult = mult * mult_up
    return mult, add


def scan_tile_up(mult, add):
    row = row_in_tile(mult.shape)
    for step in (1, 2, 4):
        keep = row < 8 - step
        add_dn = jnp.where(keep, pltpu.roll(add, 8 - step, 0), 0.0)
        mult_dn = jnp.where(keep, pltpu.roll(mult, 8 - step, 0), 1.0)
        add = add + mult * add_dn
        mult = mult * mult_dn
    return mult, add


V_BIAS, V_RATE, V_INLET, V_DECAY = 4, 5, 6, 7


def fold(values, columns):
    return jnp.sum(values.reshape(values.shape[0] // 8, 8, columns), axis=0)


def rec_forward(base, rows, vp_ref, gp_ref, mask_ref, vec_ref, rate_ref, inlet_ref,
                mixed_ref, state_ref, conv_ref, forget_ref, input_ref, low_ref, carry_ref):
    bias = vec_ref[V_BIAS:V_BIAS + 1, :]

    def conv_step(index, unused):
        at = pl.multiple_of(base + index * CHUNK, CHUNK)
        ext = vp_ref[pl.ds(at, CHUNK + 8), :]
        masks = mask_ref[pl.ds(at, CHUNK), :]
        total = bias + vec_ref[0:1, :] * ext[8:8 + CHUNK, :]
        for tap in (1, 2, 3):
            total = total + (masks[:, tap:tap + 1] * ext[8 - tap:8 - tap + CHUNK, :]) * vec_ref[tap:tap + 1, :]
        conv_ref[pl.ds(at, CHUNK), :] = total
        low_ref[pl.ds(pl.multiple_of(index * CHUNK, CHUNK), CHUNK), :] = total.astype(BF)
        return unused

    lax.fori_loop(0, rows // CHUNK, conv_step, 0)
    block = pl.ds(pl.multiple_of(base, rows), rows)
    forget_ref[block, :] = dot_nn(low_ref[...], rate_ref[...])
    input_ref[block, :] = dot_nn(low_ref[...], inlet_ref[...])
    rate_bias = vec_ref[V_RATE:V_RATE + 1, :]
    inlet_bias = vec_ref[V_INLET:V_INLET + 1, :]
    decay = vec_ref[V_DECAY:V_DECAY + 1, :]

    def scan_step(index, carry):
        at = pl.multiple_of(base + index * CHUNK, CHUNK)
        window = pl.ds(at, CHUNK)
        forget = sigmoid(forget_ref[window, :] + rate_bias)
        inlet = sigmoid(input_ref[window, :] + inlet_bias)
        log_decay = decay * forget
        carried = jnp.exp(log_decay)
        normalizer = jnp.sqrt(one_minus_square(log_decay, carried))
        forget_ref[window, :] = forget
        input_ref[window, :] = inlet
        add = normalizer * inlet * conv_ref[window, :]
        mult = carried * mask_ref[window, 1:2]
        pieces = []
        for tile in range(CHUNK // 8):
            m, a = scan_tile_down(mult[8 * tile:8 * tile + 8], add[8 * tile:8 * tile + 8])
            states = a + m * carry
            carry = states[7:8, :]
            pieces.append(states)
        states = jnp.concatenate(pieces, axis=0)
        state_ref[pl.ds(at + 8, CHUNK), :] = states
        mixed_ref[window, :] = (states * gelu(gp_ref[window, :])).astype(BF)
        return carry

    carry_ref[0:1, :] = lax.fori_loop(0, rows // CHUNK, scan_step, carry_ref[0:1, :])


def rec_backward(base, rows, dm_ref, vp_ref, gp_ref, mask_ref, vec_ref, rate_ref, inlet_ref,
                 state_ref, conv_ref, forget_ref, input_ref,
                 vlow_ref, glow_ref, dzf_ref, dzi_ref, dconv_ref, clow_ref, sums_ref, carry_ref):
    columns = conv_ref.shape[1]
    decay = vec_ref[V_DECAY:V_DECAY + 1, :]
    chunks = rows // CHUNK

    def scan_step(step, carry):
        grad_next, mult_next, rate_sum, inlet_sum, decay_sum = carry
        low = pl.multiple_of((chunks - 1 - step) * CHUNK, CHUNK)
        here = pl.ds(low, CHUNK)
        window = pl.ds(pl.multiple_of(base + low, CHUNK), CHUNK)
        mixed_grad = dm_ref[here, :]
        act, slope = gelu_both(gp_ref[here, :])
        ext = state_ref[pl.ds(low, CHUNK + 8), :]
        states = ext[8:, :]
        before = ext[7:7 + CHUNK, :]
        glow_ref[window, :] = (mixed_grad * states * slope).astype(BF)
        add = mixed_grad * act
        forget = forget_ref[here, :]
        inlet = input_ref[here, :]
        conv = conv_ref[here, :]
        clow_ref[window, :] = conv.astype(BF)
        log_decay = decay * forget
        carried = jnp.exp(log_decay)
        square = one_minus_square(log_decay, carried)
        inverse = lax.rsqrt(jnp.maximum(square, 1e-30))
        normalizer = square * inverse
        mult = carried * mask_ref[window, 1:2]
        pieces = []
        for tile in reversed(range(CHUNK // 8)):
            lo = 8 * tile
            after = mult[lo + 8:lo + 9, :] if lo + 8 < CHUNK else mult_next
            shifted = jnp.concatenate([mult[lo + 1:lo + 8, :], after], axis=0)
            m, a = scan_tile_up(shifted, add[lo:lo + 8])
            grads = a + m * grad_next
            grad_next = grads[0:1, :]
            pieces.append(grads)
        grads = jnp.concatenate(pieces[::-1], axis=0)
        gated = grads * inlet
        d_log = grads * before * mult - gated * conv * ((1.0 - square) * inverse)
        dzf = d_log * decay * forget * (1.0 - forget)
        dzi = grads * normalizer * conv * inlet * (1.0 - inlet)
        dzf_ref[window, :] = dzf.astype(BF)
        dzi_ref[window, :] = dzi.astype(BF)
        dconv_ref[here, :] = gated * normalizer
        return (grad_next, mult[0:1, :], rate_sum + fold(dzf, columns), inlet_sum + fold(dzi, columns),
                decay_sum + fold(d_log * forget, columns))

    grad_next, mult_next, rate_sum, inlet_sum, decay_sum = lax.fori_loop(
        0, chunks, scan_step,
        (carry_ref[0:1, :], carry_ref[1:2, :], sums_ref[V_RATE], sums_ref[V_INLET], sums_ref[V_DECAY]))
    carry_ref[0:1, :] = grad_next
    carry_ref[1:2, :] = mult_next
    sums_ref[V_RATE] = rate_sum
    sums_ref[V_INLET] = inlet_sum
    sums_ref[V_DECAY] = decay_sum
    block = pl.ds(pl.multiple_of(base, rows), rows)
    dconv_ref[0:rows, :] += dot_nt(dzf_ref[block, :], rate_ref[...]) + dot_nt(dzi_ref[block, :], inlet_ref[...])

    def conv_step(index, carry):
        low = pl.multiple_of(index * CHUNK, CHUNK)
        at = pl.multiple_of(base + low, CHUNK)
        ext = dconv_ref[pl.ds(low, CHUNK + 8), :]
        masks = mask_ref[pl.ds(at, CHUNK + 8), :]
        values = vp_ref[pl.ds(low, CHUNK + 8), :]
        here = ext[:CHUNK, :]
        total = vec_ref[0:1, :] * here
        sums = [carry[0] + fold(here * values[8:, :], columns)]
        for tap in (1, 2, 3):
            gated = ext * masks[:, tap:tap + 1]
            total = total + vec_ref[tap:tap + 1, :] * gated[tap:tap + CHUNK, :]
            sums.append(carry[tap] + fold(gated[:CHUNK, :] * values[8 - tap:8 - tap + CHUNK, :], columns))
        sums.append(carry[4] + fold(here, columns))
        vlow_ref[pl.ds(at, CHUNK), :] = total.astype(BF)
        return tuple(sums)

    sums = lax.fori_loop(0, chunks, conv_step, tuple(sums_ref[row] for row in range(5)))
    for row in range(5):
        sums_ref[row] = sums[row]
    dconv_ref[rows:rows + 8, :] = dconv_ref[0:8, :]


MESH = pl.DeviceIdType.MESH
PARTS = 4


IN_VMEM = pl.BlockSpec(memory_space=pltpu.VMEM)
ANYWHERE = pl.BlockSpec(memory_space=pl.ANY)
DMA = pltpu.SemaphoreType.DMA


def greet(count, groups=1, far=False):
    me = lax.axis_index("mp")
    barrier = pltpu.get_barrier_semaphore()

    @pl.when(me > 0)
    def _():
        pl.semaphore_signal(barrier, inc=1, device_id={"mp": me - 1}, device_id_type=MESH)

    @pl.when(me < count - 1)
    def _():
        pl.semaphore_signal(barrier, inc=1, device_id={"mp": me + 1}, device_id_type=MESH)

    peers = [("dp", bit) for bit in range(groups.bit_length() - 1)]
    if far:
        peers += [("mp", bit) for bit in range(1, count.bit_length() - 1)]
    for axis, bit in peers:
        pl.semaphore_signal(barrier, inc=1, device_id={axis: partner_of(bit, axis)}, device_id_type=MESH)
    inner = (me > 0) & (me < count - 1)

    @pl.when(inner)
    def _():
        pl.semaphore_wait(barrier, 2 + len(peers))

    @pl.when(jnp.logical_not(inner))
    def _():
        pl.semaphore_wait(barrier, 1 + len(peers))


def bit_of(value, bit):
    return (value // (1 << bit)) % 2


def partner_of(bit, axis="dp"):
    me = lax.axis_index(axis)
    return me + (1 << bit) * (1 - 2 * bit_of(me, bit))


class Cube:
    def __init__(self, count, order, held, slots, send, recv):
        self.count, self.order, self.held, self.slots, self.send, self.recv = count, order, held, slots, send, recv
        self.me = lax.axis_index("dp")

    def places(self, level):
        total = self.count >> (level + 1)
        start = self.count - (self.count >> level)
        return [(index, start + index) for index in range(total)]

    def chunk(self, level, index, mine):
        at = 0
        for rank, bit in enumerate(self.order):
            own = bit_of(self.me, bit)
            if rank < level:
                at = at + own * (1 << bit)
            elif rank == level:
                at = at + (own if mine else 1 - own) * (1 << bit)
            else:
                at = at + ((index >> (rank - level - 1)) & 1) * (1 << bit)
        return at

    def copy(self, level, index, slot):
        return pltpu.make_async_remote_copy(
            src_ref=self.held.at[self.chunk(level, index, False)],
            dst_ref=self.slots.at[slot],
            send_sem=self.send.at[slot],
            recv_sem=self.recv.at[slot],
            device_id={"dp": partner_of(self.order[level])},
            device_id_type=MESH,
        )

    def start(self, level):
        for index, slot in self.places(level):
            self.copy(level, index, slot).start()

    def finish(self, level):
        for index, slot in self.places(level):
            self.copy(level, index, slot).wait()
            if level < len(self.order) - 1:
                self.add(self.chunk(level, index, True), slot, self.held.at[self.chunk(level, index, True)])

    def add(self, chunk, slot, target):
        size = self.held.shape[1]
        rows = 64 if size % 64 == 0 else size

        def step(index, unused):
            window = pl.ds(index * rows, rows)
            target[window, :] = (self.held[chunk, window, :].astype(F32)
                                 + self.slots[slot, window, :].astype(F32)).astype(target.dtype)
            return unused

        lax.fori_loop(0, size // rows, step, 0)

    def result(self, target):
        self.add(self.me, self.count - 2, target)


class Spread:
    def __init__(self, cube, full, send, recv):
        self.cube, self.full, self.send, self.recv = cube, full, send, recv

    def copy(self, level, index, slot, mine=True):
        chunk = self.cube.chunk(level, index, mine)
        return pltpu.make_async_remote_copy(
            src_ref=self.full.at[chunk],
            dst_ref=self.full.at[chunk],
            send_sem=self.send.at[slot],
            recv_sem=self.recv.at[slot],
            device_id={"dp": partner_of(self.cube.order[level])},
            device_id_type=MESH,
        )

    def start(self, level):
        for index, slot in self.cube.places(level):
            self.copy(level, index, slot).start()

    def finish(self, level):
        for index, slot in self.cube.places(level):
            self.copy(level, index, slot).wait_send()
            self.copy(level, index, slot, False).wait_recv()


def orders(groups):
    bits = list(range(groups.bit_length() - 1))
    return bits, bits[:1] + bits[:0:-1]


class Gather:
    def __init__(self, count, buf, send, recv):
        self.count, self.buf, self.send, self.recv = count, buf, send, recv
        self.me = lax.axis_index("mp")

    def copy(self, block, way):
        return pltpu.make_async_remote_copy(
            src_ref=self.buf.at[block],
            dst_ref=self.buf.at[block],
            send_sem=self.send.at[0 if way < 0 else 1, block],
            recv_sem=self.recv.at[block],
            device_id={"mp": self.me + way},
            device_id_type=MESH,
        )

    def hand_on(self, block, way):
        pl.when(self.me < self.count - 1 if way > 0 else self.me > 0)(self.copy(block, way).start)

    def start(self):
        self.hand_on(self.me, 1)
        self.hand_on(self.me, -1)

    def take_low(self, distance):
        low = self.me - distance

        @pl.when(low >= 0)
        def _():
            self.copy(low, -1).wait_recv()
            self.hand_on(low, 1)

    def take_high(self, distance):
        high = self.me + distance

        @pl.when(high < self.count)
        def _():
            self.copy(high, 1).wait_recv()
            self.hand_on(high, -1)

    def take(self, distance):
        self.take_low(distance)
        self.take_high(distance)

    def drain(self):
        def step(block, unused):
            pl.when((block <= self.me) & (self.me < self.count - 1))(self.copy(block, 1).wait_send)
            pl.when((block >= self.me) & (self.me > 0))(self.copy(block, -1).wait_send)
            return unused

        lax.fori_loop(0, self.count, step, 0)


class Scatter:
    def __init__(self, count, held, slots, send, recv):
        self.count, self.held, self.slots, self.send, self.recv = count, held, slots, send, recv
        self.me = lax.axis_index("mp")

    def copy(self, block, part, way):
        slot = block + 1 if way > 0 else block
        return pltpu.make_async_remote_copy(
            src_ref=self.held.at[block, part],
            dst_ref=self.slots.at[slot, part],
            send_sem=self.send.at[block, part],
            recv_sem=self.recv.at[slot, part],
            device_id={"mp": self.me + way},
            device_id_type=MESH,
        )

    def times(self):
        return range(1, 2 * self.count - 3)

    def first(self, block, part):
        pl.when((self.me == 0) & (block > 0))(self.copy(block, part, 1).start)
        pl.when((self.me == self.count - 1) & (block < self.count - 1))(self.copy(block, part, -1).start)

    def pass_part(self, block, part, way):
        self.arrived(block, part, way)
        slot = block + 1 if way > 0 else block
        self.held[block, part] = (
            self.held[block, part].astype(F32) + self.slots[slot, part].astype(F32)).astype(BF)
        self.copy(block, part, way).start()

    def arrived(self, block, part, way):
        slot = block + 1 if way > 0 else block
        pltpu.make_async_remote_copy(
            src_ref=self.held.at[block, part],
            dst_ref=self.slots.at[slot, part],
            send_sem=self.send.at[block, part],
            recv_sem=self.recv.at[slot, part],
            device_id={"mp": self.me - way},
            device_id_type=MESH,
        ).wait_recv()

    def passing(self, time, up_near, down_near):
        last = self.count - 1
        up = time + 1 - self.me if up_near else last + self.me - time
        down = {True: 2 * last - 1 - self.me - time, False: time - last + self.me, None: time - self.count + self.me}[
            down_near]
        up_here = (self.me > 0) & (up > self.me) & (up <= last)
        down_here = (self.me < last) & (down < self.me) & (down >= 0)
        return up, up_here, down, down_here

    def pass_one(self, time, part, up_near, down_near):
        up, up_here, down, down_here = self.passing(time, up_near, down_near)
        pl.when(up_here)(lambda: self.pass_part(up, part, 1))
        pl.when(down_here)(lambda: self.pass_part(down, part, -1))

    def pass_on(self, time, up_near, down_near):
        def step(part, unused):
            self.pass_one(time, part, up_near, down_near)
            return unused

        lax.fori_loop(0, PARTS, step, 0)

    def wait_total(self, part):
        pl.when(self.me > 0)(lambda: self.arrived(self.me, part, 1))
        pl.when(self.me < self.count - 1)(lambda: self.arrived(self.me, part, -1))

    def total(self, part):
        below = jnp.where(self.me > 0, self.slots[self.me + 1, part].astype(F32), 0.0)
        above = jnp.where(self.me < self.count - 1, self.slots[self.me, part].astype(F32), 0.0)
        return self.held[self.me, part].astype(F32) + below + above

    def drain(self):
        def step(block, unused):
            for part in range(PARTS):
                pl.when(block > self.me)(self.copy(block, part, 1).wait_send)
                pl.when(block < self.me)(self.copy(block, part, -1).wait_send)
            return unused

        lax.fori_loop(0, self.count, step, 0)


def norm_rows(source_ref, gain_ref, target_ref):
    step_rows = 64

    def step(index, unused):
        window = pl.ds(pl.multiple_of(index * step_rows, step_rows), step_rows)
        values = source_ref[window, :].astype(F32)
        scale = lax.rsqrt(jnp.mean(values * values, axis=1, keepdims=True) + EPS)
        target_ref[window, :] = (values * scale * gain_ref[...]).astype(BF)
        return unused

    lax.fori_loop(0, source_ref.shape[0] // step_rows, step, 0)


def norm_back(values_ref, gain_ref, scatter, gain_grad_ref, write):
    rows, columns = values_ref.shape
    width = columns // PARTS
    dot_sum = jnp.zeros((rows, 1), F32)
    square_sum = jnp.zeros((rows, 1), F32)
    for part in range(PARTS):
        span = slice(part * width, (part + 1) * width)
        scatter.wait_total(part)
        grad = scatter.total(part)
        values = values_ref[:, span].astype(F32)
        dot_sum = dot_sum + jnp.sum(grad * gain_ref[:, span] * values, axis=1, keepdims=True)
        square_sum = square_sum + jnp.sum(values * values, axis=1, keepdims=True)
    scale = lax.rsqrt(square_sum * (1.0 / columns) + EPS)
    pull = scale * scale * scale * (dot_sum * (1.0 / columns))
    for part in range(PARTS):
        span = slice(part * width, (part + 1) * width)
        grad = scatter.total(part)
        values = values_ref[:, span].astype(F32)
        if gain_grad_ref is not None:
            gain_grad_ref[:, span] = jnp.sum(grad * values * scale, axis=0, keepdims=True)
        write(span, scale * (grad * gain_ref[:, span]) - values * pull)


def live_total(live_ref, row_sums):
    size = live_ref.shape[1]
    same = lax.broadcasted_iota(jnp.int32, (size, size), 0) == lax.broadcasted_iota(jnp.int32, (size, size), 1)
    column = jnp.sum(jnp.where(same, live_ref[...].astype(F32), 0.0), axis=1, keepdims=True)
    return jnp.sum(column * row_sums, axis=0, keepdims=True)


def fill_masks(lengths_ref, rows, mask_ref):
    row = lax.broadcasted_iota(jnp.int32, mask_ref.shape, 0)
    offset = row
    end = 0
    for index in range(lengths_ref.shape[1] - 1):
        end = end + lengths_ref[0, index]
        offset = jnp.where(row >= end, row - end, offset)
    taps = lax.broadcasted_iota(jnp.int32, mask_ref.shape, 1)
    mask_ref[...] = jnp.where((offset >= taps) & (row < rows), 1.0, 0.0)


def fill_square(heads_ref, square_ref):
    square_ref[...] = jnp.zeros(square_ref.shape, BF)
    width = heads_ref.shape[1]
    for head in range(heads_ref.shape[0]):
        span = slice(head * width, (head + 1) * width)
        square_ref[span, span] = heads_ref[head].astype(BF)


def mixer_kernel(count, lengths_ref, tokens_ref, gain_ref, live_ref, taps_ref, shift_ref, rate_bias_ref,
                 inlet_bias_ref, decay_ref, rate_heads_ref, inlet_heads_ref,
                 cot_hbm, value_hbm, gate_hbm, out_hbm,
                 middle_ref, stat_ref, mask_ref, vec_ref, rate_ref, inlet_ref,
                 normed_all, cot_all, mixed_out, vp_out, gp_out, state_out, conv_out, forget_out, input_out,
                 normed, value_w, gate_w, out_w, vp, gp, mixed, state, conv, forget, inlet_gate, low, carry, held,
                 slots, load_sem, own_sem, out_sem, block_sem, ag_send, ag_recv, cot_send, cot_recv, rs_send, rs_recv):
    me = lax.axis_index("mp")
    rows, columns = tokens_ref.shape
    channels = value_w.shape[1]
    width = columns // PARTS
    own_copy = pltpu.make_async_copy(cot_hbm, cot_all.at[me], own_sem)
    own_copy.start()
    loads = [pltpu.make_async_copy(source, target, load_sem.at[index]) for index, (source, target) in enumerate(
        ((value_hbm, value_w), (gate_hbm, gate_w), (out_hbm, out_w)))]
    for load in loads:
        load.start()
    norm_rows(tokens_ref, gain_ref, normed.at[me])
    greet(count)
    gather = Gather(count, normed, ag_send, ag_recv)
    cots = Gather(count, cot_all, cot_send, cot_recv)
    scatter = Scatter(count, held, slots, rs_send, rs_recv)
    gather.start()
    zeros = jnp.zeros((8, channels), F32)
    vp[0:8, :] = zeros
    state[0:8, :] = zeros
    carry[...] = zeros
    fill_masks(lengths_ref, count * rows, mask_ref)
    fill_square(rate_heads_ref, rate_ref)
    fill_square(inlet_heads_ref, inlet_ref)
    vec_ref[0:4, :] = taps_ref[...]
    vec_ref[V_BIAS:V_BIAS + 1, :] = shift_ref[...].reshape(1, channels)
    vec_ref[V_RATE:V_RATE + 1, :] = rate_bias_ref[...].reshape(1, channels)
    vec_ref[V_INLET:V_INLET + 1, :] = inlet_bias_ref[...].reshape(1, channels)
    vec_ref[V_DECAY:V_DECAY + 1, :] = -8.0 * jnp.log1p(jnp.exp(-decay_ref[...].reshape(1, channels)))
    own_copy.wait()
    for load in loads:
        load.wait()

    def block_copy(block):
        return pltpu.make_async_copy(normed.at[block], normed_all.at[block], block_sem.at[block])

    def project(block):
        block_copy(block).start()
        rows_in = normed[block]
        vp[pl.ds(pl.multiple_of(block * rows + 8, 8), rows), :] = dot_nn(rows_in, value_w[...])
        gp[pl.ds(pl.multiple_of(block * rows, rows), rows), :] = dot_nn(rows_in, gate_w[...])

    def mix(block):
        base = block * rows
        rec_forward(base, rows, vp, gp, mask_ref, vec_ref, rate_ref, inlet_ref,
                    mixed, state, conv, forget, inlet_gate, low, carry)
        rows_in = mixed[pl.ds(pl.multiple_of(base, rows), rows), :]
        for part in range(PARTS):
            held[block, part] = dot_nn(rows_in, out_w[:, part * width:(part + 1) * width]).astype(BF)
            scatter.first(block, part)

    def mixed_by(block, distance):
        return (distance >= count - 1) | ((distance >= me) & (block <= me + distance)
                                          & (block < 2 * (distance - me + 1)))

    def arrive(distance, unused):
        pl.when(distance > 0)(lambda: gather.take(distance))
        pl.when((distance == me + 1) & (me < count - 1))(cots.copy(me, 1).start)
        pl.when((distance == count - me) & (me > 0))(cots.copy(me, -1).start)

        def side(which, inner):
            block = me - distance + 2 * distance * which
            pl.when((block >= 0) & (block < count) & ((distance > 0) | (which == 0)))(lambda: project(block))
            return inner

        lax.fori_loop(0, 2, side, unused)

        def turn(block, inner):
            before = (distance > 0) & mixed_by(block, distance - 1)
            pl.when(mixed_by(block, distance) & jnp.logical_not(before))(lambda: mix(block))
            return inner

        return lax.fori_loop(0, count, turn, unused)

    lax.fori_loop(0, count, arrive, 0)
    saves = [pltpu.make_async_copy(source, target, out_sem.at[index]) for index, (source, target) in enumerate(
        ((mixed, mixed_out), (vp, vp_out), (gp, gp_out), (state, state_out), (conv, conv_out),
         (forget, forget_out), (inlet_gate, input_out)))]
    for save in saves:
        save.start()
    cots.take(1)
    below, above = 2, 2
    for time in scatter.times():
        if below < count and time >= 2 * below - 2:
            cots.take_low(below)
            below += 1
        if above < count and time >= 2 * above - 1:
            cots.take_high(above)
            above += 1
        scatter.pass_on(time, True, False)
    for distance in range(below, count):
        cots.take_low(distance)
    for distance in range(above, count):
        cots.take_high(distance)
    row_sums = jnp.zeros((rows, 1), F32)
    token_sums = jnp.zeros((rows, 1), F32)
    for part in range(PARTS):
        span = slice(part * width, (part + 1) * width)
        scatter.wait_total(part)
        total = scatter.total(part)
        tokens = tokens_ref[:, span].astype(F32)
        row_sums = row_sums + jnp.sum(total * total, axis=1, keepdims=True)
        token_sums = token_sums + jnp.sum(tokens * tokens, axis=1, keepdims=True)
        middle_ref[:, span] = tokens + total
    stat_ref[...] = jnp.zeros(stat_ref.shape, F32)
    stat_ref[0:1, :] += live_total(live_ref, token_sums)
    stat_ref[1:2, :] += live_total(live_ref, row_sums)
    stat_ref[2:3, :] += live_total(live_ref, jnp.ones((rows, 1), F32))
    for save in saves:
        save.wait()
    for block in range(count):
        block_copy(block).wait()
    gather.drain()
    cots.drain()
    scatter.drain()


def call_mixer(count, lengths, tokens, gain, live, taps, vectors, rate_heads, inlet_heads, cotangent, value_proj, gate_proj, mixer_out):
    rows, columns = tokens.shape
    channels = value_proj.shape[1]
    total = count * rows
    wide = jax.ShapeDtypeStruct((total, channels), F32)
    ahead = jax.ShapeDtypeStruct((total + 8, channels), F32)
    blocks = jax.ShapeDtypeStruct((count, rows, columns), BF)
    square = jax.ShapeDtypeStruct((channels, channels), BF)
    return pl.pallas_call(
        functools.partial(mixer_kernel, count),
        out_shape=(
            jax.ShapeDtypeStruct((rows, columns), F32), jax.ShapeDtypeStruct((8, 128), F32),
            jax.ShapeDtypeStruct((total + 8, 8), F32), jax.ShapeDtypeStruct((8, channels), F32), square, square,
            blocks, blocks, jax.ShapeDtypeStruct((total, channels), BF), ahead, wide, ahead, wide, wide, wide,
        ),
        in_specs=[pl.BlockSpec(memory_space=pltpu.SMEM)] + [IN_VMEM] * 10 + [ANYWHERE] * 4,
        out_specs=(IN_VMEM,) * 6 + (ANYWHERE,) * 9,
        scratch_shapes=[
            pltpu.VMEM((count, rows, columns), BF),
            pltpu.VMEM((columns, channels), BF),
            pltpu.VMEM((columns, channels), BF),
            pltpu.VMEM((channels, columns), BF),
            pltpu.VMEM((total + 8, channels), F32),
            pltpu.VMEM((total, channels), F32),
            pltpu.VMEM((total, channels), BF),
            pltpu.VMEM((total + 8, channels), F32),
            pltpu.VMEM((total, channels), F32),
            pltpu.VMEM((total, channels), F32),
            pltpu.VMEM((total, channels), F32),
            pltpu.VMEM((rows, channels), BF),
            pltpu.VMEM((8, channels), F32),
            pltpu.VMEM((count, PARTS, rows, columns // PARTS), BF),
            pltpu.VMEM((count + 1, PARTS, rows, columns // PARTS), BF),
            DMA((3,)), DMA, DMA((7,)), DMA((count,)),
            DMA((2, count)), DMA((count,)), DMA((2, count)), DMA((count,)),
            DMA((count, PARTS)), DMA((count + 1, PARTS)),
        ],
        compiler_params=pltpu.CompilerParams(vmem_limit_bytes=VMEM_LIMIT, collective_id=1, has_side_effects=True),
        cost_estimate=pl.CostEstimate(flops=6 * total * columns * channels, bytes_accessed=40 * total * channels,
                                      transcendentals=6 * total * channels),
    )(lengths, tokens, gain, live, taps, *vectors, rate_heads, inlet_heads, cotangent,
      value_proj, gate_proj, mixer_out)


def middle_kernel(count, groups, middle_grad_ref, middle_ref, live_ref, terms_hbm, out_hbm, mixed_hbm,
                  gate_hbm, value_hbm, layer_ref, stat_ref, out_grad_ref, gate_sum_ref, value_sum_ref, dm_hbm,
                  low, out_w, mixed, dm, held, slots, cube_a, slots_a, cube_b, slots_b, gate_held, gate_slots, value_held, value_slots,
                  load_sem, dm_sem, ag_send, ag_recv, rs_send, rs_recv, a_send, a_recv, b_send, b_recv,
                  gate_send, gate_recv, value_send, value_recv):
    me = lax.axis_index("mp")
    rows, columns = middle_ref.shape
    channels = out_w.shape[0]
    width = columns // PARTS
    chunk = columns // groups
    half = channels // 2
    loads = [pltpu.make_async_copy(source, target, load_sem.at[index]) for index, (source, target) in enumerate(
        ((gate_hbm, gate_held), (value_hbm, value_held), (out_hbm, out_w), (mixed_hbm, mixed), (terms_hbm, held)))]
    for load in loads:
        load.start()
    low[me] = middle_grad_ref[...].astype(BF)
    greet(count, groups)
    gather = Gather(count, low, ag_send, ag_recv)
    scatter = Scatter(count, held, slots, rs_send, rs_recv)
    order_a, order_b = orders(groups)
    cubes = (Cube(groups, order_a, cube_a, slots_a, a_send, a_recv),
             Cube(groups, order_b, cube_b, slots_b, b_send, b_recv))
    dense_cubes = (Cube(groups, order_a, gate_held, gate_slots, gate_send, gate_recv),
                   Cube(groups, order_b, value_held, value_slots, value_send, value_recv))
    levels = len(order_a)
    gather.start()
    for load in loads:
        load.wait()
    for cube in dense_cubes:
        cube.start(0)

    def dense_advance(level):
        for cube in dense_cubes:
            cube.finish(level)
            if level + 1 < levels:
                cube.start(level + 1)

    def dm_copy(block):
        return pltpu.make_async_copy(dm.at[block], dm_hbm.at[pl.ds(pl.multiple_of(block * rows, rows), rows)],
                                     dm_sem.at[block])

    def back(block):
        dm[block] = dot_nt(low[block], out_w[...])
        dm_copy(block).start()

    back(me)
    dense_advance(0)
    for distance in range(1, count):
        gather.take(distance)
        if distance == 1:
            for step in range(count - 1):
                for part in range(PARTS):
                    pl.when(me == 0)(scatter.copy(count - 1 - step, part, 1).start)
                    pl.when(me == count - 1)(scatter.copy(step, part, -1).start)
        pl.when(me - distance >= 0)(lambda: back(me - distance))
        pl.when(me + distance < count)(lambda: back(me + distance))
        if distance == count - 2:
            scatter.pass_on(1, False, False)
            dense_advance(1)

    def out_grad(index, unused):
        right = low[:, :, pl.ds(pl.multiple_of(index * chunk, chunk), chunk)].reshape(count * rows, chunk)
        both = dot_tn(mixed[...], right).astype(BF)
        cube_a[index] = both[:half]
        cube_b[index] = both[half:]
        return unused

    lax.fori_loop(0, groups, out_grad, 0)
    for cube in cubes:
        cube.start(0)
    level = 0
    for time in list(scatter.times())[1:]:
        scatter.pass_on(time, False, False)
        if time == 2:
            for rest in range(2, levels):
                dense_advance(rest)
            dense_cubes[0].result(gate_sum_ref)
            dense_cubes[1].result(value_sum_ref)
        if level < levels:
            for cube in cubes:
                cube.finish(level)
                if level + 1 < levels:
                    cube.start(level + 1)
            level += 1
    for rest in range(level, levels):
        for cube in cubes:
            cube.finish(rest)
            if rest + 1 < levels:
                cube.start(rest + 1)
    cubes[0].result(out_grad_ref.at[0:half])
    cubes[1].result(out_grad_ref.at[half:channels])
    row_sums = jnp.zeros((rows, 1), F32)
    for part in range(PARTS):
        span = slice(part * width, (part + 1) * width)
        scatter.wait_total(part)
        total = scatter.total(part)
        row_sums = row_sums + jnp.sum(total * total, axis=1, keepdims=True)
        layer_ref[:, span] = (middle_ref[:, span] + total).astype(BF)
    stat_ref[...] = jnp.zeros(stat_ref.shape, F32) + live_total(live_ref, row_sums)
    for block in range(count):
        dm_copy(block).wait()
    gather.drain()
    scatter.drain()


def call_middle(count, groups, middle_grad, middle, live, terms, mixer_out, mixed, gate_weights, value_weights):
    rows, columns = middle.shape
    channels = mixer_out.shape[0]
    total = count * rows
    chunk = columns // groups
    units = gate_weights.shape[1]
    split = (groups, chunk, units)
    return pl.pallas_call(
        functools.partial(middle_kernel, count, groups),
        out_shape=(
            jax.ShapeDtypeStruct((rows, columns), BF), jax.ShapeDtypeStruct((8, 128), F32),
            jax.ShapeDtypeStruct((channels, chunk), F32), jax.ShapeDtypeStruct((chunk, units), F32),
            jax.ShapeDtypeStruct((chunk, units), F32), jax.ShapeDtypeStruct((total, channels), F32),
        ),
        in_specs=[IN_VMEM] * 3 + [ANYWHERE] * 5,
        out_specs=(IN_VMEM,) * 5 + (ANYWHERE,),
        scratch_shapes=[
            pltpu.VMEM((count, rows, columns), BF),
            pltpu.VMEM((channels, columns), BF),
            pltpu.VMEM((total, channels), BF),
            pltpu.VMEM((count, rows, channels), F32),
            pltpu.VMEM((count, PARTS, rows, columns // PARTS), BF),
            pltpu.VMEM((count + 1, PARTS, rows, columns // PARTS), BF),
            pltpu.VMEM((groups, channels // 2, chunk), BF),
            pltpu.VMEM((groups - 1, channels // 2, chunk), BF),
            pltpu.VMEM((groups, channels // 2, chunk), BF),
            pltpu.VMEM((groups - 1, channels // 2, chunk), BF),
            pltpu.VMEM(split, BF), pltpu.VMEM((groups - 1, chunk, units), BF),
            pltpu.VMEM(split, BF), pltpu.VMEM((groups - 1, chunk, units), BF),
            DMA((5,)), DMA((count,)), DMA((2, count)), DMA((count,)), DMA((count, PARTS)), DMA((count + 1, PARTS)),
            DMA((groups - 1,)), DMA((groups - 1,)), DMA((groups - 1,)), DMA((groups - 1,)),
            DMA((groups - 1,)), DMA((groups - 1,)), DMA((groups - 1,)), DMA((groups - 1,)),
        ],
        compiler_params=pltpu.CompilerParams(vmem_limit_bytes=VMEM_LIMIT, collective_id=2, has_side_effects=True),
        cost_estimate=pl.CostEstimate(flops=4 * total * columns * channels, bytes_accessed=40 * total * channels,
                                      transcendentals=0),
    )(middle_grad, middle, live, terms, mixer_out, mixed, gate_weights.reshape(split), value_weights.reshape(split))


def input_kernel(count, groups, heads, tokens_ref, gain_ref, middle_grad_ref, mask_ref, vec_ref, rate_ref, inlet_ref,
                 dense_gain_ref, stat_ref, dense_stat_ref, value_hbm, gate_hbm, normed_hbm, dm_hbm, vp_hbm, gp_hbm, state_hbm, conv_hbm, forget_hbm, input_hbm,
                 input_grad_ref, flat_ref, value_grad_ref, gate_grad_ref, full, vec_grad_ref,
                 value_w, gate_w, dm, vp, gp, state, conv, forget, inlet_gate, normed, vlow, glow, dzf, dzi, dconv,
                 clow, sums, carry, held, slots, cube_a, slots_a, cube_b, slots_b, cube_c, slots_c,
                 vec_held, vec_slots, flat_held, flat_slots,
                 load_sem, block_sem, normed_sem, rs_send, rs_recv, a_send, a_recv, b_send, b_recv, c_send, c_recv,
                 f_send, f_recv, v_send, v_recv, flat_send, flat_recv):
    me = lax.axis_index("mp")
    rows, columns = tokens_ref.shape
    channels = value_w.shape[1]
    width = columns // PARTS
    chunk = columns // groups
    total_rows = count * rows
    head = channels // heads
    loads = [pltpu.make_async_copy(value_hbm, value_w, load_sem.at[0]),
             pltpu.make_async_copy(gate_hbm, gate_w, load_sem.at[1])]
    for load in loads:
        load.start()

    def block_loads(block, slot):
        at = pl.multiple_of(block * rows, rows)
        plain = pl.ds(at, rows)
        ahead = pl.ds(at, rows + 8)
        return [pltpu.make_async_copy(source.at[window], target.at[slot], block_sem.at[slot, index])
                for index, (source, window, target) in enumerate((
                    (dm_hbm, plain, dm), (vp_hbm, ahead, vp), (gp_hbm, plain, gp), (state_hbm, ahead, state),
                    (conv_hbm, plain, conv), (forget_hbm, plain, forget), (input_hbm, plain, inlet_gate)))]

    for load in block_loads(count - 1, 0):
        load.start()
    zeros = jnp.zeros((8, channels), F32)
    dconv[rows:rows + 8, :] = zeros
    carry[...] = zeros
    for row in range(8):
        sums[row] = zeros
    greet(count, groups, True)
    scatter = Scatter(count, held, slots, rs_send, rs_recv)
    order_a, order_b = orders(groups)
    cubes = (Cube(groups, order_a, cube_a, slots_a, a_send, a_recv),
             Cube(groups, order_b, cube_b, slots_b, b_send, b_recv),
             Cube(groups, order_b, cube_c, slots_c, c_send, c_recv))
    spread = Spread(cubes[2], full, f_send, f_recv)
    for load in loads:
        load.wait()

    def back(step, unused):
        block = count - 1 - step
        slot = step % 2
        for load in block_loads(block, slot):
            load.wait()

        @pl.when(step + 1 < count)
        def _():
            for load in block_loads(block - 1, 1 - slot):
                load.start()

        base = block * rows
        rec_backward(base, rows, dm.at[slot], vp.at[slot], gp.at[slot], mask_ref, vec_ref, rate_ref, inlet_ref,
                     state.at[slot], conv.at[slot], forget.at[slot], inlet_gate.at[slot],
                     vlow, glow, dzf, dzi, dconv, clow, sums, carry)
        window = pl.ds(pl.multiple_of(base, rows), rows)
        for part in range(PARTS):
            span = slice(part * width, (part + 1) * width)
            held[block, part] = (dot_nt(vlow[window, :], value_w[span, :])
                                 + dot_nt(glow[window, :], gate_w[span, :])).astype(BF)
            pl.when((me == 0) & (block > 0))(scatter.copy(block, part, 1).start)
            pl.when((me == count - 1) & (block == count - 2))(scatter.copy(block, part, -1).start)
        return unused

    def normed_copy(index, slot):
        return pltpu.make_async_copy(
            normed_hbm.at[:, :, pl.ds(pl.multiple_of(index * chunk, chunk), chunk)], normed.at[slot],
            normed_sem.at[slot])

    normed_copy(0, 0).start()
    lax.fori_loop(0, count, back, 0)
    for block in range(count - 2):
        for part in range(PARTS):
            pl.when(me == count - 1)(scatter.copy(block, part, -1).start)

    def weights(index, unused):
        slot = index % 2
        normed_copy(index, slot).wait()
        pl.when(index + 1 < groups)(lambda: normed_copy(index + 1, 1 - slot).start())
        left = normed[slot].reshape(total_rows, chunk)
        cube_a[index] = dot_tn(left, vlow[...]).astype(BF)
        cube_b[index] = dot_tn(left, glow[...]).astype(BF)
        part = index * chunk // width
        inside = pl.ds(pl.multiple_of(index * chunk % width, chunk), chunk)
        gain_row = jnp.zeros((1, chunk), F32)
        for block in range(count):
            gain_row = gain_row + jnp.sum(
                normed[slot, block].astype(F32) * held[block, part, :, inside].astype(F32), axis=0, keepdims=True)
        flat_held[0:1, pl.ds(pl.multiple_of(index * chunk, chunk), chunk)] = gain_row
        return unused

    flat_held[...] = jnp.zeros(flat_held.shape, F32)
    lax.fori_loop(0, groups, weights, 0)
    flat_held[0:1, :] = flat_held[0:1, :] / gain_ref[...]
    flat_held[1:2, :] = dense_gain_ref[...]
    for index, value in enumerate((stat_ref[0:1], stat_ref[1:2], dense_stat_ref[0:1], stat_ref[2:3])):
        flat_held[2:3, index * 128:(index + 1) * 128] = value
    peers = [("dp", bit) for bit in range(groups.bit_length() - 1)]
    peers += [("mp", bit) for bit in range(count.bit_length() - 1)]

    def flat_copy(index):
        axis, bit = peers[index]
        return pltpu.make_async_remote_copy(
            src_ref=flat_held, dst_ref=flat_slots.at[index], send_sem=flat_send.at[index],
            recv_sem=flat_recv.at[index], device_id={axis: partner_of(bit, axis)}, device_id_type=MESH)

    flat_copy(0).start()
    cubes[0].start(0)
    cubes[1].start(0)
    slab = 2 * channels // groups
    for which, source in enumerate((dzf, dzi)):
        for index in range(heads):
            span = slice(index * head, (index + 1) * head)
            square = dot_tn(clow[:, span], source[:, span])
            first = (which * channels + index * head) // slab
            for piece in range(head // slab):
                cube_c[first + piece] = square[piece * slab:(piece + 1) * slab]
    cubes[2].start(0)
    for row in range(8):
        vec_held[0, row:row + 1, :] = jnp.sum(sums[row], axis=0, keepdims=True)

    def vec_copy(level):
        return pltpu.make_async_remote_copy(
            src_ref=vec_held.at[level], dst_ref=vec_slots.at[level], send_sem=v_send.at[level],
            recv_sem=v_recv.at[level], device_id={"dp": partner_of(level)}, device_id_type=MESH)

    levels = len(order_a)
    vec_copy(0).start()

    def advance(level):
        if level < len(peers):
            flat_copy(level).wait()
            flat_held[...] += flat_slots[level]
            if level + 1 < len(peers):
                flat_copy(level + 1).start()
        if level < levels:
            for cube in cubes:
                cube.finish(level)
                if level + 1 < levels:
                    cube.start(level + 1)
            vec_copy(level).wait()
            if level + 1 < levels:
                vec_held[level + 1] = vec_held[level] + vec_slots[level]
                vec_copy(level + 1).start()
            else:
                vec_grad_ref[...] = vec_held[level] + vec_slots[level]
                cubes[0].result(value_grad_ref)
                cubes[1].result(gate_grad_ref)
                cubes[2].result(full.at[lax.axis_index("dp")])
                spread.start(levels - 1)
        elif level < 2 * levels:
            back_level = 2 * levels - 1 - level
            spread.finish(back_level)
            if back_level > 0:
                spread.start(back_level - 1)

    stages = max(2 * levels, len(peers))
    slots_all = [(time, part) for time in scatter.times() for part in range(PARTS)]
    early = max(len(slots_all) - 5 - 2 * (stages - 4), 0)
    for time in range(1, early // PARTS + 1):
        scatter.pass_on(time, False, None)
    level = 0
    for index in range(early // PARTS * PARTS, len(slots_all)):
        scatter.pass_one(*slots_all[index], False, None)
        turn = len(slots_all) - index - 1
        if level < stages and (turn <= 4 or turn % 2 == 0) and turn > 0 and stages - level >= min(turn, 4):
            advance(level)
            level += 1
    for rest in range(level, stages):
        advance(rest)
    flat_ref[...] = flat_held[...]
    def write(span, change):
        input_grad_ref[:, span] = (middle_grad_ref[:, span] + change).astype(BF)

    norm_back(tokens_ref, gain_ref, scatter, None, write)
    scatter.drain()


def call_input(count, groups, heads, tokens, gain, middle_grad, masks, vec, rate, inlet, dense_gain_grad, stat,
               dense_stat, value_proj, gate_proj, normed_all, dm, vp, gp, state, conv, forget, inp):
    rows, columns = tokens.shape
    channels = value_proj.shape[1]
    total = count * rows
    chunk = columns // groups
    head = channels // heads
    slab = 2 * channels // groups
    plain = pltpu.VMEM((2, rows, channels), F32)
    ahead = pltpu.VMEM((2, rows + 8, channels), F32)
    low = pltpu.VMEM((total, channels), BF)
    levels = groups.bit_length() - 1
    flats = levels + count.bit_length() - 1
    return pl.pallas_call(
        functools.partial(input_kernel, count, groups, heads),
        out_shape=(
            jax.ShapeDtypeStruct((rows, columns), BF), jax.ShapeDtypeStruct((8, columns), F32),
            jax.ShapeDtypeStruct((chunk, channels), F32), jax.ShapeDtypeStruct((chunk, channels), F32),
            jax.ShapeDtypeStruct((groups, slab, head), F32), jax.ShapeDtypeStruct((8, channels), F32),
        ),
        in_specs=[IN_VMEM] * 10 + [ANYWHERE] * 10,
        out_specs=(IN_VMEM,) * 6,
        scratch_shapes=[
            pltpu.VMEM((columns, channels), BF),
            pltpu.VMEM((columns, channels), BF),
            plain, ahead, plain, ahead, plain, plain, plain,
            pltpu.VMEM((2, count, rows, chunk), BF),
            low, low, low, low,
            pltpu.VMEM((rows + 8, channels), F32),
            low,
            pltpu.VMEM((8, 8, channels), F32),
            pltpu.VMEM((8, channels), F32),
            pltpu.VMEM((count, PARTS, rows, columns // PARTS), BF),
            pltpu.VMEM((count + 1, PARTS, rows, columns // PARTS), BF),
            pltpu.VMEM((groups, chunk, channels), BF), pltpu.VMEM((groups - 1, chunk, channels), BF),
            pltpu.VMEM((groups, chunk, channels), BF), pltpu.VMEM((groups - 1, chunk, channels), BF),
            pltpu.VMEM((groups, slab, head), F32), pltpu.VMEM((groups - 1, slab, head), F32),
            pltpu.VMEM((levels, 8, channels), F32), pltpu.VMEM((levels, 8, channels), F32),
            pltpu.VMEM((8, columns), F32), pltpu.VMEM((flats, 8, columns), F32),
            DMA((2,)), DMA((2, 7)), DMA((2,)), DMA((count, PARTS)), DMA((count + 1, PARTS)),
            DMA((groups - 1,)), DMA((groups - 1,)), DMA((groups - 1,)), DMA((groups - 1,)),
            DMA((groups - 1,)), DMA((groups - 1,)), DMA((groups - 1,)), DMA((groups - 1,)),
            DMA((levels,)), DMA((levels,)), DMA((flats,)), DMA((flats,)),
        ],
        compiler_params=pltpu.CompilerParams(vmem_limit_bytes=VMEM_LIMIT, collective_id=3, has_side_effects=True),
        cost_estimate=pl.CostEstimate(flops=8 * total * columns * channels, bytes_accessed=60 * total * channels,
                                      transcendentals=4 * total * channels),
    )(tokens, gain, middle_grad, masks, vec, rate, inlet, dense_gain_grad, stat, dense_stat, value_proj, gate_proj,
      normed_all, dm, vp, gp, state, conv, forget, inp)


def spans(total):
    size = 512 if total % 512 == 0 else 256
    return [slice(at, at + size) for at in range(0, total, size)]


def dense_kernel(count, groups, middle_ref, gain_ref, cot_hbm, gate_hbm, value_hbm, down_hbm,
                 middle_grad_ref, gain_grad_ref, dense_part_hbm, gate_out, value_out, down_out,
                 normed, cot, gate_w, value_w, down_w, hidden, gate_g, value_g, dense_part, held, slots, stage,
                 load_sem, cot_sem, part_sem, stage_sem, ag_send, ag_recv, rs_send, rs_recv):
    me = lax.axis_index("mp")
    rows, columns = middle_ref.shape
    units = gate_w.shape[1]
    width = columns // PARTS
    loads = [pltpu.make_async_copy(gate_hbm, gate_w, load_sem.at[0]),
             pltpu.make_async_copy(value_hbm, value_w, load_sem.at[1]),
             pltpu.make_async_copy(down_hbm, down_w, load_sem.at[2])]
    for load in loads:
        load.start()

    def cot_copy(block):
        return pltpu.make_async_copy(cot_hbm.at[block],
                                     cot.at[block], cot_sem.at[block])

    for block in range(count):
        cot_copy(block).start()
    greet(count)
    gather = Gather(count, normed, ag_send, ag_recv)
    scatter = Scatter(count, held, slots, rs_send, rs_recv)
    norm_rows(middle_ref, gain_ref, normed.at[me])
    gather.start()
    for load in loads:
        load.wait()
    pieces = 3
    piece = units // pieces

    def part_copy(block, slot):
        return pltpu.make_async_copy(dense_part.at[slot], dense_part_hbm.at[block], part_sem.at[slot])

    def compute(block, slot, reuse):
        cot_copy(block).wait()
        rows_in = normed[block]
        rows_cot = cot[block]
        for index in range(pieces):
            span = slice(index * piece, (index + 1) * piece)
            gate_linear = dot_nn(rows_in, gate_w[:, span])
            value_linear = dot_nn(rows_in, value_w[:, span])
            hidden_grad = dot_nt(rows_cot, down_w[span, :])
            act, slope = gelu_both(gate_linear)
            hidden[block, :, span] = (act * value_linear).astype(BF)
            gate_g[block, :, span] = (hidden_grad * value_linear * slope).astype(BF)
            value_g[block, :, span] = (hidden_grad * act).astype(BF)
        for part in range(PARTS):
            span = slice(part * width, (part + 1) * width)
            held[block, part] = (dot_nt(gate_g[block], gate_w[span, :])
                                 + dot_nt(value_g[block], value_w[span, :])).astype(BF)
            scatter.first(block, part)
        pl.when(reuse)(lambda: part_copy(block, slot).wait())
        for part in range(PARTS):
            span = slice(part * width, (part + 1) * width)
            dense_part[slot, part] = dot_nn(hidden[block], down_w[:, span]).astype(BF)
        part_copy(block, slot).start()

    def arrive(distance, unused):
        pl.when(distance > 0)(lambda: gather.take(distance))

        def side(which, inner):
            block = me - distance + 2 * distance * which
            pl.when((block >= 0) & (block < count) & ((distance > 0) | (which == 0)))(
                lambda: compute(block, which, (distance > 1) | ((distance == 1) & (which == 0))))
            return inner

        return lax.fori_loop(0, 2, side, unused)

    lax.fori_loop(0, count, arrive, 0)

    total_rows = count * rows
    left_rows = columns // 4
    unit_rows = units // 4
    group_width = columns // groups

    def stage_copy(kind, index, slot):
        if kind == 2:
            half = columns // 2
            return pltpu.make_async_copy(
                stage.at[slot, pl.ds(0, unit_rows), pl.ds(0, half)],
                down_out.at[pl.ds(index // 2 * unit_rows, unit_rows), pl.ds(index % 2 * half, half)],
                stage_sem.at[slot])
        target = gate_out if kind == 0 else value_out
        return pltpu.make_async_copy(
            stage.at[slot, pl.ds(0, left_rows), pl.ds(0, units)],
            target.at[pl.ds(index * left_rows, left_rows)], stage_sem.at[slot])

    def grads(kind, index, slot):
        if kind == 2:
            low = index // 2 * unit_rows
            left = hidden[:, :, low:low + unit_rows].reshape(total_rows, unit_rows)
            for span in spans(columns // 2):
                at = index % 2 * (columns // 2) + span.start
                size = span.stop - span.start
                right = cot[:, :, at:at + size].reshape(total_rows, size)
                stage[slot, 0:unit_rows, span] = dot_tn(left, right).astype(BF)
        else:
            left = normed[:, :, index * left_rows:(index + 1) * left_rows].reshape(total_rows, left_rows)
            source = gate_g if kind == 0 else value_g
            for span in spans(units):
                right = source[:, :, span].reshape(total_rows, span.stop - span.start)
                stage[slot, 0:left_rows, span] = dot_tn(left, right).astype(BF)

    work = [(kind, index) for kind in (0, 1, 2) for index in range((4, 4, 8)[kind])]
    started = []
    times = scatter.times()
    per_step = -(-len(work) // (len(times) + 1))
    for step in range(len(times) + 1):
        if step > 0:
            scatter.pass_on(step, True, True)
        for kind, index in work[step * per_step:(step + 1) * per_step]:
            slot = len(started) % 2
            if len(started) >= 2:
                stage_copy(*started[-2], slot).wait()
            grads(kind, index, slot)
            stage_copy(kind, index, slot).start()
            started.append((kind, index))
    for back in (2, 1):
        stage_copy(*started[-back], (len(started) - back) % 2).wait()

    def write(span, change):
        middle_grad_ref[:, span] = cot[me, :, span].astype(F32) + change

    norm_back(middle_ref, gain_ref, scatter, gain_grad_ref, write)
    part_copy(0, 0).wait()
    pl.when(me < count - 1)(part_copy(0, 1).wait)
    gather.drain()
    scatter.drain()


def call_dense(count, groups, middle, gain, cot_all, dense_gate, dense_value, dense_down):
    rows, columns = middle.shape
    units = dense_gate.shape[1]
    width = columns // PARTS
    any_spec = pl.BlockSpec(memory_space=pl.ANY)
    vmem = pl.BlockSpec(memory_space=pltpu.VMEM)
    dma = pltpu.SemaphoreType.DMA
    return pl.pallas_call(
        functools.partial(dense_kernel, count, groups),
        out_shape=(
            jax.ShapeDtypeStruct((rows, columns), F32),
            jax.ShapeDtypeStruct((1, columns), F32),
            jax.ShapeDtypeStruct((count, PARTS, rows, width), BF),
            jax.ShapeDtypeStruct((columns, units), BF),
            jax.ShapeDtypeStruct((columns, units), BF),
            jax.ShapeDtypeStruct((units, columns), BF),
        ),
        in_specs=[vmem, vmem, any_spec, any_spec, any_spec, any_spec],
        out_specs=(vmem, vmem, any_spec, any_spec, any_spec, any_spec),
        scratch_shapes=[
            pltpu.VMEM((count, rows, columns), BF),
            pltpu.VMEM((count, rows, columns), BF),
            pltpu.VMEM((columns, units), BF),
            pltpu.VMEM((columns, units), BF),
            pltpu.VMEM((units, columns), BF),
            pltpu.VMEM((count, rows, units), BF),
            pltpu.VMEM((count, rows, units), BF),
            pltpu.VMEM((count, rows, units), BF),
            pltpu.VMEM((2, PARTS, rows, width), BF),
            pltpu.VMEM((count, PARTS, rows, width), BF),
            pltpu.VMEM((count + 1, PARTS, rows, width), BF),
            pltpu.VMEM((2, columns // 4, max(units, columns // 2)), BF),
            dma((3,)), dma((count,)), dma((2,)), dma((2,)),
            dma((2, count)), dma((count,)), dma((count, PARTS)), dma((count + 1, PARTS)),
        ],
        compiler_params=pltpu.CompilerParams(
            vmem_limit_bytes=VMEM_LIMIT, collective_id=0, has_side_effects=True),
        cost_estimate=pl.CostEstimate(flops=18 * count * rows * columns * units,
                                      bytes_accessed=12 * columns * units, transcendentals=count * rows * units),
    )(middle, gain, cot_all, dense_gate, dense_value, dense_down)


def scatter_dp(values, dimension):
    return lax.psum_scatter(values, "dp", scatter_dimension=dimension, tiled=True).astype(F32)


def local(groups, tokens, cotangent, lengths, live_mask, mixer_gain, value_proj, gate_proj, conv_taps, conv_bias,
          rate_weight, rate_bias, inlet_weight, inlet_bias, decay_param, mixer_out, dense_gain,
          dense_gate, dense_value, dense_down):
    columns = tokens.shape[1]
    head_count, head_width = rate_weight.shape[:2]
    channels = head_count * head_width
    count = lax.axis_size("mp")
    live = live_mask[None, :]
    middle, stat, masks, vec, rate_square, inlet_square, normed_all, cot_all, mixed, *saved = call_mixer(
        count, lengths, tokens, mixer_gain[None, :], live, conv_taps,
        (conv_bias, rate_bias, inlet_bias, decay_param), rate_weight, inlet_weight, cotangent,
        value_proj, gate_proj, mixer_out)
    middle_grad, dense_gain_grad, dense_terms, gate_weights, value_weights, down_weights = call_dense(
        count, groups, middle, dense_gain[None, :], cot_all, dense_gate, dense_value, dense_down)
    layer_out, dense_stat, mixer_out_sum, gate_sum, value_sum, dm = call_middle(
        count, groups, middle_grad, middle, live, dense_terms, mixer_out, mixed, gate_weights, value_weights)
    dm, down_weights = lax.optimization_barrier((dm, down_weights))
    input_grad, flat, value_proj_sum, gate_proj_sum, small, vec_sum = call_input(
        count, groups, head_count, tokens, mixer_gain[None, :], middle_grad, masks, vec, rate_square, inlet_square,
        dense_gain_grad, stat, dense_stat, value_proj, gate_proj, normed_all, dm, *saved)
    branch_rms = jnp.sqrt(flat[2, 0:384:128] / (flat[2, 384] * columns))
    decay_scale = 8.0 * jax.nn.sigmoid(-decay_param)
    return (
        layer_out,
        input_grad,
        flat[0],
        value_proj_sum,
        gate_proj_sum,
        vec_sum[0:4],
        vec_sum[4],
        small[:groups // 2].reshape(rate_weight.shape),
        vec_sum[V_RATE],
        small[groups // 2:].reshape(rate_weight.shape),
        vec_sum[V_INLET],
        vec_sum[V_DECAY] * decay_scale,
        mixer_out_sum,
        flat[1],
        gate_sum,
        value_sum,
        scatter_dp(down_weights, 1),
        branch_rms,
    )


def solution(mesh):
    rows = P(("dp", "mp"), None)
    return jax.shard_map(
        functools.partial(local, mesh.shape["dp"]),
        mesh=mesh,
        in_specs=(
            rows, rows, P("dp", None), P(("dp", "mp")), P(),
            P(None, "mp"), P(None, "mp"), P(None, "mp"), P("mp"),
            P("mp", None, None), P("mp"), P("mp", None, None), P("mp"), P("mp"),
            P("mp", None), P(), P(None, "mp"), P(None, "mp"), P("mp", None),
        ),
        out_specs=(
            rows, rows, P(), P("dp", "mp"), P("dp", "mp"),
            P(None, "mp"), P("mp"), P("mp", None, None), P("mp"), P("mp", None, None), P("mp"), P("mp"),
            P("mp", "dp"), P(), P("dp", "mp"), P("dp", "mp"), P("mp", "dp"), P(),
        ),
        check_vma=False,
    )
```

```python
import functools

import jax
import jax.numpy as jnp
from jax import lax
from jax.experimental import pallas as pl
from jax.experimental.pallas import tpu as pltpu
from jax.sharding import PartitionSpec as P

EPS = 1e-06
BF = jnp.bfloat16
F32 = jnp.float32
GELU_C = 0.7978845608028654
GELU_A = 0.044715
CHUNK = 16
VMEM_LIMIT = 60 * 1024 * 1024


def dot_nn(left, right):
    return jnp.dot(left, right, preferred_element_type=F32)


def dot_nt(left, right):
    return lax.dot_general(left, right, (((1,), (1,)), ((), ())), preferred_element_type=F32)


def dot_tn(left, right):
    return lax.dot_general(left, right, (((0,), (0,)), ((), ())), preferred_element_type=F32)


def gelu(x):
    return 0.5 * x * (1.0 + jnp.tanh(GELU_C * (x + GELU_A * x * x * x)))


def gelu_both(x):
    square = x * x
    tanh_in = jnp.tanh(GELU_C * x * (1.0 + GELU_A * square))
    half = 0.5 * (1.0 + tanh_in)
    slope = half + 0.5 * x * (1.0 - tanh_in * tanh_in) * (GELU_C * (1.0 + 3.0 * GELU_A * square))
    return half * x, slope


def sigmoid(x):
    return 1.0 / (1.0 + jnp.exp(-x))


def one_minus_square(log_decay, carried):
    y = 2.0 * log_decay
    series = 1.0 + y * (1.0 / 7.0)
    for k in (6.0, 5.0, 4.0, 3.0, 2.0):
        series = 1.0 + y * (1.0 / k) * series
    return jnp.where(y > -0.5, -y * series, 1.0 - carried * carried)


def row_in_tile(shape):
    return lax.broadcasted_iota(jnp.int32, shape, 0) % 8


def scan_tile_down(mult, add):
    row = row_in_tile(mult.shape)
    for step in (1, 2, 4):
        keep = row >= step
        add_up = jnp.where(keep, pltpu.roll(add, step, 0), 0.0)
        mult_up = jnp.where(keep, pltpu.roll(mult, step, 0), 1.0)
        add = add + mult * add_up
        mult = mult * mult_up
    return mult, add


def scan_tile_up(mult, add):
    row = row_in_tile(mult.shape)
    for step in (1, 2, 4):
        keep = row < 8 - step
        add_dn = jnp.where(keep, pltpu.roll(add, 8 - step, 0), 0.0)
        mult_dn = jnp.where(keep, pltpu.roll(mult, 8 - step, 0), 1.0)
        add = add + mult * add_dn
        mult = mult * mult_dn
    return mult, add


V_BIAS, V_RATE, V_INLET, V_DECAY = 4, 5, 6, 7


def fold(values, columns):
    return jnp.sum(values.reshape(values.shape[0] // 8, 8, columns), axis=0)


def rec_forward(base, rows, vp_ref, gp_ref, mask_ref, vec_ref, rate_ref, inlet_ref,
                mixed_ref, state_ref, conv_ref, forget_ref, input_ref, low_ref, carry_ref):
    bias = vec_ref[V_BIAS:V_BIAS + 1, :]

    def conv_step(index, unused):
        at = pl.multiple_of(base + index * CHUNK, CHUNK)
        ext = vp_ref[pl.ds(at, CHUNK + 8), :]
        masks = mask_ref[pl.ds(at, CHUNK), :]
        total = bias + vec_ref[0:1, :] * ext[8:8 + CHUNK, :]
        for tap in (1, 2, 3):
            total = total + (masks[:, tap:tap + 1] * ext[8 - tap:8 - tap + CHUNK, :]) * vec_ref[tap:tap + 1, :]
        conv_ref[pl.ds(at, CHUNK), :] = total
        low_ref[pl.ds(pl.multiple_of(index * CHUNK, CHUNK), CHUNK), :] = total.astype(BF)
        return unused

    lax.fori_loop(0, rows // CHUNK, conv_step, 0)
    block = pl.ds(pl.multiple_of(base, rows), rows)
    forget_ref[block, :] = dot_nn(low_ref[...], rate_ref[...])
    input_ref[block, :] = dot_nn(low_ref[...], inlet_ref[...])
    rate_bias = vec_ref[V_RATE:V_RATE + 1, :]
    inlet_bias = vec_ref[V_INLET:V_INLET + 1, :]
    decay = vec_ref[V_DECAY:V_DECAY + 1, :]

    def scan_step(index, carry):
        at = pl.multiple_of(base + index * CHUNK, CHUNK)
        window = pl.ds(at, CHUNK)
        forget = sigmoid(forget_ref[window, :] + rate_bias)
        inlet = sigmoid(input_ref[window, :] + inlet_bias)
        log_decay = decay * forget
        carried = jnp.exp(log_decay)
        normalizer = jnp.sqrt(one_minus_square(log_decay, carried))
        forget_ref[window, :] = forget
        input_ref[window, :] = inlet
        add = normalizer * inlet * conv_ref[window, :]
        mult = carried * mask_ref[window, 1:2]
        pieces = []
        for tile in range(CHUNK // 8):
            m, a = scan_tile_down(mult[8 * tile:8 * tile + 8], add[8 * tile:8 * tile + 8])
            states = a + m * carry
            carry = states[7:8, :]
            pieces.append(states)
        states = jnp.concatenate(pieces, axis=0)
        state_ref[pl.ds(at + 8, CHUNK), :] = states
        mixed_ref[window, :] = (states * gelu(gp_ref[window, :])).astype(BF)
        return carry

    carry_ref[0:1, :] = lax.fori_loop(0, rows // CHUNK, scan_step, carry_ref[0:1, :])


def rec_backward(base, rows, dm_ref, vp_ref, gp_ref, mask_ref, vec_ref, rate_ref, inlet_ref,
                 state_ref, conv_ref, forget_ref, input_ref,
                 vlow_ref, glow_ref, dzf_ref, dzi_ref, dconv_ref, clow_ref, sums_ref, carry_ref):
    columns = conv_ref.shape[1]
    decay = vec_ref[V_DECAY:V_DECAY + 1, :]
    chunks = rows // CHUNK

    def scan_step(step, carry):
        grad_next, mult_next, rate_sum, inlet_sum, decay_sum = carry
        low = pl.multiple_of((chunks - 1 - step) * CHUNK, CHUNK)
        here = pl.ds(low, CHUNK)
        window = pl.ds(pl.multiple_of(base + low, CHUNK), CHUNK)
        mixed_grad = dm_ref[here, :]
        act, slope = gelu_both(gp_ref[here, :])
        ext = state_ref[pl.ds(low, CHUNK + 8), :]
        states = ext[8:, :]
        before = ext[7:7 + CHUNK, :]
        glow_ref[window, :] = (mixed_grad * states * slope).astype(BF)
        add = mixed_grad * act
        forget = forget_ref[here, :]
        inlet = input_ref[here, :]
        conv = conv_ref[here, :]
        clow_ref[window, :] = conv.astype(BF)
        log_decay = decay * forget
        carried = jnp.exp(log_decay)
        square = one_minus_square(log_decay, carried)
        inverse = lax.rsqrt(jnp.maximum(square, 1e-30))
        normalizer = square * inverse
        mult = carried * mask_ref[window, 1:2]
        pieces = []
        for tile in reversed(range(CHUNK // 8)):
            lo = 8 * tile
            after = mult[lo + 8:lo + 9, :] if lo + 8 < CHUNK else mult_next
            shifted = jnp.concatenate([mult[lo + 1:lo + 8, :], after], axis=0)
            m, a = scan_tile_up(shifted, add[lo:lo + 8])
            grads = a + m * grad_next
            grad_next = grads[0:1, :]
            pieces.append(grads)
        grads = jnp.concatenate(pieces[::-1], axis=0)
        gated = grads * inlet
        d_log = grads * before * mult - gated * conv * ((1.0 - square) * inverse)
        dzf = d_log * decay * forget * (1.0 - forget)
        dzi = grads * normalizer * conv * inlet * (1.0 - inlet)
        dzf_ref[window, :] = dzf.astype(BF)
        dzi_ref[window, :] = dzi.astype(BF)
        dconv_ref[here, :] = gated * normalizer
        return (grad_next, mult[0:1, :], rate_sum + fold(dzf, columns), inlet_sum + fold(dzi, columns),
                decay_sum + fold(d_log * forget, columns))

    grad_next, mult_next, rate_sum, inlet_sum, decay_sum = lax.fori_loop(
        0, chunks, scan_step,
        (carry_ref[0:1, :], carry_ref[1:2, :], sums_ref[V_RATE], sums_ref[V_INLET], sums_ref[V_DECAY]))
    carry_ref[0:1, :] = grad_next
    carry_ref[1:2, :] = mult_next
    sums_ref[V_RATE] = rate_sum
    sums_ref[V_INLET] = inlet_sum
    sums_ref[V_DECAY] = decay_sum
    block = pl.ds(pl.multiple_of(base, rows), rows)
    dconv_ref[0:rows, :] += dot_nt(dzf_ref[block, :], rate_ref[...]) + dot_nt(dzi_ref[block, :], inlet_ref[...])

    def conv_step(index, carry):
        low = pl.multiple_of(index * CHUNK, CHUNK)
        at = pl.multiple_of(base + low, CHUNK)
        ext = dconv_ref[pl.ds(low, CHUNK + 8), :]
        masks = mask_ref[pl.ds(at, CHUNK + 8), :]
        values = vp_ref[pl.ds(low, CHUNK + 8), :]
        here = ext[:CHUNK, :]
        total = vec_ref[0:1, :] * here
        sums = [carry[0] + fold(here * values[8:, :], columns)]
        for tap in (1, 2, 3):
            gated = ext * masks[:, tap:tap + 1]
            total = total + vec_ref[tap:tap + 1, :] * gated[tap:tap + CHUNK, :]
            sums.append(carry[tap] + fold(gated[:CHUNK, :] * values[8 - tap:8 - tap + CHUNK, :], columns))
        sums.append(carry[4] + fold(here, columns))
        vlow_ref[pl.ds(at, CHUNK), :] = total.astype(BF)
        return tuple(sums)

    sums = lax.fori_loop(0, chunks, conv_step, tuple(sums_ref[row] for row in range(5)))
    for row in range(5):
        sums_ref[row] = sums[row]
    dconv_ref[rows:rows + 8, :] = dconv_ref[0:8, :]


MESH = pl.DeviceIdType.MESH
PARTS = 4


IN_VMEM = pl.BlockSpec(memory_space=pltpu.VMEM)
ANYWHERE = pl.BlockSpec(memory_space=pl.ANY)
DMA = pltpu.SemaphoreType.DMA


def greet(count, groups=1, far=False):
    me = lax.axis_index("mp")
    barrier = pltpu.get_barrier_semaphore()

    @pl.when(me > 0)
    def _():
        pl.semaphore_signal(barrier, inc=1, device_id={"mp": me - 1}, device_id_type=MESH)

    @pl.when(me < count - 1)
    def _():
        pl.semaphore_signal(barrier, inc=1, device_id={"mp": me + 1}, device_id_type=MESH)

    peers = [("dp", bit) for bit in range(groups.bit_length() - 1)]
    if far:
        peers += [("mp", bit) for bit in range(1, count.bit_length() - 1)]
    for axis, bit in peers:
        pl.semaphore_signal(barrier, inc=1, device_id={axis: partner_of(bit, axis)}, device_id_type=MESH)
    inner = (me > 0) & (me < count - 1)

    @pl.when(inner)
    def _():
        pl.semaphore_wait(barrier, 2 + len(peers))

    @pl.when(jnp.logical_not(inner))
    def _():
        pl.semaphore_wait(barrier, 1 + len(peers))


def bit_of(value, bit):
    return (value // (1 << bit)) % 2


def partner_of(bit, axis="dp"):
    me = lax.axis_index(axis)
    return me + (1 << bit) * (1 - 2 * bit_of(me, bit))


class Cube:
    def __init__(self, count, order, held, slots, send, recv):
        self.count, self.order, self.held, self.slots, self.send, self.recv = count, order, held, slots, send, recv
        self.me = lax.axis_index("dp")

    def places(self, level):
        total = self.count >> (level + 1)
        start = self.count - (self.count >> level)
        return [(index, start + index) for index in range(total)]

    def chunk(self, level, index, mine):
        at = 0
        for rank, bit in enumerate(self.order):
            own = bit_of(self.me, bit)
            if rank < level:
                at = at + own * (1 << bit)
            elif rank == level:
                at = at + (own if mine else 1 - own) * (1 << bit)
            else:
                at = at + ((index >> (rank - level - 1)) & 1) * (1 << bit)
        return at

    def copy(self, level, index, slot):
        return pltpu.make_async_remote_copy(
            src_ref=self.held.at[self.chunk(level, index, False)],
            dst_ref=self.slots.at[slot],
            send_sem=self.send.at[slot],
            recv_sem=self.recv.at[slot],
            device_id={"dp": partner_of(self.order[level])},
            device_id_type=MESH,
        )

    def start(self, level):
        for index, slot in self.places(level):
            self.copy(level, index, slot).start()

    def finish(self, level):
        for index, slot in self.places(level):
            self.copy(level, index, slot).wait()
            if level < len(self.order) - 1:
                self.add(self.chunk(level, index, True), slot, self.held.at[self.chunk(level, index, True)])

    def add(self, chunk, slot, target):
        size = self.held.shape[1]
        rows = 64 if size % 64 == 0 else size

        def step(index, unused):
            window = pl.ds(index * rows, rows)
            target[window, :] = (self.held[chunk, window, :].astype(F32)
                                 + self.slots[slot, window, :].astype(F32)).astype(target.dtype)
            return unused

        lax.fori_loop(0, size // rows, step, 0)

    def result(self, target):
        self.add(self.me, self.count - 2, target)


class Spread:
    def __init__(self, cube, full, send, recv):
        self.cube, self.full, self.send, self.recv = cube, full, send, recv

    def copy(self, level, index, slot, mine=True):
        chunk = self.cube.chunk(level, index, mine)
        return pltpu.make_async_remote_copy(
            src_ref=self.full.at[chunk],
            dst_ref=self.full.at[chunk],
            send_sem=self.send.at[slot],
            recv_sem=self.recv.at[slot],
            device_id={"dp": partner_of(self.cube.order[level])},
            device_id_type=MESH,
        )

    def start(self, level):
        for index, slot in self.cube.places(level):
            self.copy(level, index, slot).start()

    def finish(self, level):
        for index, slot in self.cube.places(level):
            self.copy(level, index, slot).wait_send()
            self.copy(level, index, slot, False).wait_recv()


def orders(groups):
    bits = list(range(groups.bit_length() - 1))
    return bits, bits[:1] + bits[:0:-1]


class Gather:
    def __init__(self, count, buf, send, recv):
        self.count, self.buf, self.send, self.recv = count, buf, send, recv
        self.me = lax.axis_index("mp")

    def copy(self, block, way):
        return pltpu.make_async_remote_copy(
            src_ref=self.buf.at[block],
            dst_ref=self.buf.at[block],
            send_sem=self.send.at[0 if way < 0 else 1, block],
            recv_sem=self.recv.at[block],
            device_id={"mp": self.me + way},
            device_id_type=MESH,
        )

    def hand_on(self, block, way):
        pl.when(self.me < self.count - 1 if way > 0 else self.me > 0)(self.copy(block, way).start)

    def start(self):
        self.hand_on(self.me, 1)
        self.hand_on(self.me, -1)

    def take_low(self, distance):
        low = self.me - distance

        @pl.when(low >= 0)
        def _():
            self.copy(low, -1).wait_recv()
            self.hand_on(low, 1)

    def take_high(self, distance):
        high = self.me + distance

        @pl.when(high < self.count)
        def _():
            self.copy(high, 1).wait_recv()
            self.hand_on(high, -1)

    def take(self, distance):
        self.take_low(distance)
        self.take_high(distance)

    def drain(self):
        def step(block, unused):
            pl.when((block <= self.me) & (self.me < self.count - 1))(self.copy(block, 1).wait_send)
            pl.when((block >= self.me) & (self.me > 0))(self.copy(block, -1).wait_send)
            return unused

        lax.fori_loop(0, self.count, step, 0)


class Scatter:
    def __init__(self, count, held, slots, send, recv):
        self.count, self.held, self.slots, self.send, self.recv = count, held, slots, send, recv
        self.me = lax.axis_index("mp")

    def copy(self, block, part, way):
        slot = block + 1 if way > 0 else block
        return pltpu.make_async_remote_copy(
            src_ref=self.held.at[block, part],
            dst_ref=self.slots.at[slot, part],
            send_sem=self.send.at[block, part],
            recv_sem=self.recv.at[slot, part],
            device_id={"mp": self.me + way},
            device_id_type=MESH,
        )

    def times(self):
        return range(1, 2 * self.count - 3)

    def first(self, block, part):
        pl.when((self.me == 0) & (block > 0))(self.copy(block, part, 1).start)
        pl.when((self.me == self.count - 1) & (block < self.count - 1))(self.copy(block, part, -1).start)

    def pass_part(self, block, part, way):
        self.arrived(block, part, way)
        slot = block + 1 if way > 0 else block
        self.held[block, part] = (
            self.held[block, part].astype(F32) + self.slots[slot, part].astype(F32)).astype(BF)
        self.copy(block, part, way).start()

    def arrived(self, block, part, way):
        slot = block + 1 if way > 0 else block
        pltpu.make_async_remote_copy(
            src_ref=self.held.at[block, part],
            dst_ref=self.slots.at[slot, part],
            send_sem=self.send.at[block, part],
            recv_sem=self.recv.at[slot, part],
            device_id={"mp": self.me - way},
            device_id_type=MESH,
        ).wait_recv()

    def passing(self, time, up_near, down_near):
        last = self.count - 1
        up = time + 1 - self.me if up_near else last + self.me - time
        down = {True: 2 * last - 1 - self.me - time, False: time - last + self.me, None: time - self.count + self.me}[
            down_near]
        up_here = (self.me > 0) & (up > self.me) & (up <= last)
        down_here = (self.me < last) & (down < self.me) & (down >= 0)
        return up, up_here, down, down_here

    def pass_one(self, time, part, up_near, down_near):
        up, up_here, down, down_here = self.passing(time, up_near, down_near)
        pl.when(up_here)(lambda: self.pass_part(up, part, 1))
        pl.when(down_here)(lambda: self.pass_part(down, part, -1))

    def pass_on(self, time, up_near, down_near):
        def step(part, unused):
            self.pass_one(time, part, up_near, down_near)
            return unused

        lax.fori_loop(0, PARTS, step, 0)

    def wait_total(self, part):
        pl.when(self.me > 0)(lambda: self.arrived(self.me, part, 1))
        pl.when(self.me < self.count - 1)(lambda: self.arrived(self.me, part, -1))

    def total(self, part):
        below = jnp.where(self.me > 0, self.slots[self.me + 1, part].astype(F32), 0.0)
        above = jnp.where(self.me < self.count - 1, self.slots[self.me, part].astype(F32), 0.0)
        return self.held[self.me, part].astype(F32) + below + above

    def drain(self):
        def step(block, unused):
            for part in range(PARTS):
                pl.when(block > self.me)(self.copy(block, part, 1).wait_send)
                pl.when(block < self.me)(self.copy(block, part, -1).wait_send)
            return unused

        lax.fori_loop(0, self.count, step, 0)


def norm_rows(source_ref, gain_ref, target_ref):
    step_rows = 64

    def step(index, unused):
        window = pl.ds(pl.multiple_of(index * step_rows, step_rows), step_rows)
        values = source_ref[window, :].astype(F32)
        scale = lax.rsqrt(jnp.mean(values * values, axis=1, keepdims=True) + EPS)
        target_ref[window, :] = (values * scale * gain_ref[...]).astype(BF)
        return unused

    lax.fori_loop(0, source_ref.shape[0] // step_rows, step, 0)


def norm_back(values_ref, gain_ref, scatter, gain_grad_ref, write):
    rows, columns = values_ref.shape
    width = columns // PARTS
    dot_sum = jnp.zeros((rows, 1), F32)
    square_sum = jnp.zeros((rows, 1), F32)
    for part in range(PARTS):
        span = slice(part * width, (part + 1) * width)
        scatter.wait_total(part)
        grad = scatter.total(part)
        values = values_ref[:, span].astype(F32)
        dot_sum = dot_sum + jnp.sum(grad * gain_ref[:, span] * values, axis=1, keepdims=True)
        square_sum = square_sum + jnp.sum(values * values, axis=1, keepdims=True)
    scale = lax.rsqrt(square_sum * (1.0 / columns) + EPS)
    pull = scale * scale * scale * (dot_sum * (1.0 / columns))
    for part in range(PARTS):
        span = slice(part * width, (part + 1) * width)
        grad = scatter.total(part)
        values = values_ref[:, span].astype(F32)
        if gain_grad_ref is not None:
            gain_grad_ref[:, span] = jnp.sum(grad * values * scale, axis=0, keepdims=True)
        write(span, scale * (grad * gain_ref[:, span]) - values * pull)


def live_total(live_ref, row_sums):
    size = live_ref.shape[1]
    same = lax.broadcasted_iota(jnp.int32, (size, size), 0) == lax.broadcasted_iota(jnp.int32, (size, size), 1)
    column = jnp.sum(jnp.where(same, live_ref[...].astype(F32), 0.0), axis=1, keepdims=True)
    return jnp.sum(column * row_sums, axis=0, keepdims=True)


def fill_masks(lengths_ref, rows, mask_ref):
    row = lax.broadcasted_iota(jnp.int32, mask_ref.shape, 0)
    offset = row
    end = 0
    for index in range(lengths_ref.shape[1] - 1):
        end = end + lengths_ref[0, index]
        offset = jnp.where(row >= end, row - end, offset)
    taps = lax.broadcasted_iota(jnp.int32, mask_ref.shape, 1)
    mask_ref[...] = jnp.where((offset >= taps) & (row < rows), 1.0, 0.0)


def fill_square(heads_ref, square_ref):
    square_ref[...] = jnp.zeros(square_ref.shape, BF)
    width = heads_ref.shape[1]
    for head in range(heads_ref.shape[0]):
        span = slice(head * width, (head + 1) * width)
        square_ref[span, span] = heads_ref[head].astype(BF)


def mixer_kernel(count, lengths_ref, tokens_ref, gain_ref, live_ref, taps_ref, shift_ref, rate_bias_ref,
                 inlet_bias_ref, decay_ref, rate_heads_ref, inlet_heads_ref,
                 cot_hbm, value_hbm, gate_hbm, out_hbm,
                 middle_ref, stat_ref, mask_ref, vec_ref, rate_ref, inlet_ref,
                 normed_all, cot_all, mixed_out, vp_out, gp_out, state_out, conv_out, forget_out, input_out,
                 normed, value_w, gate_w, out_w, vp, gp, mixed, state, conv, forget, inlet_gate, low, carry, held,
                 slots, load_sem, own_sem, out_sem, block_sem, ag_send, ag_recv, cot_send, cot_recv, rs_send, rs_recv):
    me = lax.axis_index("mp")
    rows, columns = tokens_ref.shape
    channels = value_w.shape[1]
    width = columns // PARTS
    own_copy = pltpu.make_async_copy(cot_hbm, cot_all.at[me], own_sem)
    own_copy.start()
    loads = [pltpu.make_async_copy(source, target, load_sem.at[index]) for index, (source, target) in enumerate(
        ((value_hbm, value_w), (gate_hbm, gate_w), (out_hbm, out_w)))]
    for load in loads:
        load.start()
    norm_rows(tokens_ref, gain_ref, normed.at[me])
    greet(count)
    gather = Gather(count, normed, ag_send, ag_recv)
    cots = Gather(count, cot_all, cot_send, cot_recv)
    scatter = Scatter(count, held, slots, rs_send, rs_recv)
    gather.start()
    zeros = jnp.zeros((8, channels), F32)
    vp[0:8, :] = zeros
    state[0:8, :] = zeros
    carry[...] = zeros
    fill_masks(lengths_ref, count * rows, mask_ref)
    fill_square(rate_heads_ref, rate_ref)
    fill_square(inlet_heads_ref, inlet_ref)
    vec_ref[0:4, :] = taps_ref[...]
    vec_ref[V_BIAS:V_BIAS + 1, :] = shift_ref[...].reshape(1, channels)
    vec_ref[V_RATE:V_RATE + 1, :] = rate_bias_ref[...].reshape(1, channels)
    vec_ref[V_INLET:V_INLET + 1, :] = inlet_bias_ref[...].reshape(1, channels)
    vec_ref[V_DECAY:V_DECAY + 1, :] = -8.0 * jnp.log1p(jnp.exp(-decay_ref[...].reshape(1, channels)))
    own_copy.wait()
    for load in loads:
        load.wait()

    def block_copy(block):
        return pltpu.make_async_copy(normed.at[block], normed_all.at[block], block_sem.at[block])

    def project(block):
        block_copy(block).start()
        rows_in = normed[block]
        vp[pl.ds(pl.multiple_of(block * rows + 8, 8), rows), :] = dot_nn(rows_in, value_w[...])
        gp[pl.ds(pl.multiple_of(block * rows, rows), rows), :] = dot_nn(rows_in, gate_w[...])

    def mix(block):
        base = block * rows
        rec_forward(base, rows, vp, gp, mask_ref, vec_ref, rate_ref, inlet_ref,
                    mixed, state, conv, forget, inlet_gate, low, carry)
        rows_in = mixed[pl.ds(pl.multiple_of(base, rows), rows), :]
        for part in range(PARTS):
            held[block, part] = dot_nn(rows_in, out_w[:, part * width:(part + 1) * width]).astype(BF)
            scatter.first(block, part)

    def mixed_by(block, distance):
        return (distance >= count - 1) | ((distance >= me) & (block <= me + distance)
                                          & (block < 2 * (distance - me + 1)))

    def arrive(distance, unused):
        pl.when(distance > 0)(lambda: gather.take(distance))
        pl.when((distance == me + 1) & (me < count - 1))(cots.copy(me, 1).start)
        pl.when((distance == count - me) & (me > 0))(cots.copy(me, -1).start)

        def side(which, inner):
            block = me - distance + 2 * distance * which
            pl.when((block >= 0) & (block < count) & ((distance > 0) | (which == 0)))(lambda: project(block))
            return inner

        lax.fori_loop(0, 2, side, unused)

        def turn(block, inner):
            before = (distance > 0) & mixed_by(block, distance - 1)
            pl.when(mixed_by(block, distance) & jnp.logical_not(before))(lambda: mix(block))
            return inner

        return lax.fori_loop(0, count, turn, unused)

    lax.fori_loop(0, count, arrive, 0)
    saves = [pltpu.make_async_copy(source, target, out_sem.at[index]) for index, (source, target) in enumerate(
        ((mixed, mixed_out), (vp, vp_out), (gp, gp_out), (state, state_out), (conv, conv_out),
         (forget, forget_out), (inlet_gate, input_out)))]
    for save in saves:
        save.start()
    cots.take(1)
    below, above = 2, 2
    for time in scatter.times():
        if below < count and time >= 2 * below - 2:
            cots.take_low(below)
            below += 1
        if above < count and time >= 2 * above - 1:
            cots.take_high(above)
            above += 1
        scatter.pass_on(time, True, False)
    for distance in range(below, count):
        cots.take_low(distance)
    for distance in range(above, count):
        cots.take_high(distance)
    row_sums = jnp.zeros((rows, 1), F32)
    token_sums = jnp.zeros((rows, 1), F32)
    for part in range(PARTS):
        span = slice(part * width, (part + 1) * width)
        scatter.wait_total(part)
        total = scatter.total(part)
        tokens = tokens_ref[:, span].astype(F32)
        row_sums = row_sums + jnp.sum(total * total, axis=1, keepdims=True)
        token_sums = token_sums + jnp.sum(tokens * tokens, axis=1, keepdims=True)
        middle_ref[:, span] = tokens + total
    stat_ref[...] = jnp.zeros(stat_ref.shape, F32)
    stat_ref[0:1, :] += live_total(live_ref, token_sums)
    stat_ref[1:2, :] += live_total(live_ref, row_sums)
    stat_ref[2:3, :] += live_total(live_ref, jnp.ones((rows, 1), F32))
    for save in saves:
        save.wait()
    for block in range(count):
        block_copy(block).wait()
    gather.drain()
    cots.drain()
    scatter.drain()


def call_mixer(count, lengths, tokens, gain, live, taps, vectors, rate_heads, inlet_heads, cotangent, value_proj, gate_proj, mixer_out):
    rows, columns = tokens.shape
    channels = value_proj.shape[1]
    total = count * rows
    wide = jax.ShapeDtypeStruct((total, channels), F32)
    ahead = jax.ShapeDtypeStruct((total + 8, channels), F32)
    blocks = jax.ShapeDtypeStruct((count, rows, columns), BF)
    square = jax.ShapeDtypeStruct((channels, channels), BF)
    return pl.pallas_call(
        functools.partial(mixer_kernel, count),
        out_shape=(
            jax.ShapeDtypeStruct((rows, columns), F32), jax.ShapeDtypeStruct((8, 128), F32),
            jax.ShapeDtypeStruct((total + 8, 8), F32), jax.ShapeDtypeStruct((8, channels), F32), square, square,
            blocks, blocks, jax.ShapeDtypeStruct((total, channels), BF), ahead, wide, ahead, wide, wide, wide,
        ),
        in_specs=[pl.BlockSpec(memory_space=pltpu.SMEM)] + [IN_VMEM] * 10 + [ANYWHERE] * 4,
        out_specs=(IN_VMEM,) * 6 + (ANYWHERE,) * 9,
        scratch_shapes=[
            pltpu.VMEM((count, rows, columns), BF),
            pltpu.VMEM((columns, channels), BF),
            pltpu.VMEM((columns, channels), BF),
            pltpu.VMEM((channels, columns), BF),
            pltpu.VMEM((total + 8, channels), F32),
            pltpu.VMEM((total, channels), F32),
            pltpu.VMEM((total, channels), BF),
            pltpu.VMEM((total + 8, channels), F32),
            pltpu.VMEM((total, channels), F32),
            pltpu.VMEM((total, channels), F32),
            pltpu.VMEM((total, channels), F32),
            pltpu.VMEM((rows, channels), BF),
            pltpu.VMEM((8, channels), F32),
            pltpu.VMEM((count, PARTS, rows, columns // PARTS), BF),
            pltpu.VMEM((count + 1, PARTS, rows, columns // PARTS), BF),
            DMA((3,)), DMA, DMA((7,)), DMA((count,)),
            DMA((2, count)), DMA((count,)), DMA((2, count)), DMA((count,)),
            DMA((count, PARTS)), DMA((count + 1, PARTS)),
        ],
        compiler_params=pltpu.CompilerParams(vmem_limit_bytes=VMEM_LIMIT, collective_id=1, has_side_effects=True),
        cost_estimate=pl.CostEstimate(flops=6 * total * columns * channels, bytes_accessed=40 * total * channels,
                                      transcendentals=6 * total * channels),
    )(lengths, tokens, gain, live, taps, *vectors, rate_heads, inlet_heads, cotangent,
      value_proj, gate_proj, mixer_out)


def middle_kernel(count, groups, middle_grad_ref, live_ref, middle_hbm, terms_hbm, out_hbm, mixed_hbm,
                  gate_hbm, value_hbm, layer_ref, stat_ref, out_grad_ref, gate_out, value_out, dm_hbm,
                  low, out_w, mixed, dm, held, slots, cube_a, slots_a, cube_b, slots_b, gate_held, gate_slots, value_held, value_slots,
                  middle_ref, gate_sum_ref, value_sum_ref,
                  load_sem, dm_sem, ag_send, ag_recv, rs_send, rs_recv, a_send, a_recv, b_send, b_recv,
                  gate_send, gate_recv, value_send, value_recv, own_sem):
    me = lax.axis_index("mp")
    rows, columns = middle_ref.shape
    channels = out_w.shape[0]
    width = columns // PARTS
    chunk = columns // groups
    half = channels // 2
    loads = [pltpu.make_async_copy(source, target, load_sem.at[index]) for index, (source, target) in enumerate(
        ((gate_hbm, gate_held), (value_hbm, value_held), (out_hbm, out_w), (mixed_hbm, mixed), (terms_hbm, held)))]
    for load in loads:
        load.start()
    middle_load = pltpu.make_async_copy(middle_hbm, middle_ref, own_sem.at[0])
    middle_load.start()
    sum_saves = [pltpu.make_async_copy(gate_sum_ref, gate_out, own_sem.at[1]),
                 pltpu.make_async_copy(value_sum_ref, value_out, own_sem.at[2])]
    low[me] = middle_grad_ref[...].astype(BF)
    greet(count, groups)
    gather = Gather(count, low, ag_send, ag_recv)
    scatter = Scatter(count, held, slots, rs_send, rs_recv)
    order_a, order_b = orders(groups)
    cubes = (Cube(groups, order_a, cube_a, slots_a, a_send, a_recv),
             Cube(groups, order_b, cube_b, slots_b, b_send, b_recv))
    dense_cubes = (Cube(groups, order_a, gate_held, gate_slots, gate_send, gate_recv),
                   Cube(groups, order_b, value_held, value_slots, value_send, value_recv))
    levels = len(order_a)
    gather.start()
    for load in loads:
        load.wait()
    for cube in dense_cubes:
        cube.start(0)

    def dense_advance(level):
        for cube in dense_cubes:
            cube.finish(level)
            if level + 1 < levels:
                cube.start(level + 1)

    def dm_copy(block):
        return pltpu.make_async_copy(dm.at[block], dm_hbm.at[pl.ds(pl.multiple_of(block * rows, rows), rows)],
                                     dm_sem.at[block])

    def back(block):
        dm[block] = dot_nt(low[block], out_w[...])
        dm_copy(block).start()

    back(me)
    dense_advance(0)
    for distance in range(1, count):
        gather.take(distance)
        if distance == 1:
            for step in range(count - 1):
                for part in range(PARTS):
                    pl.when(me == 0)(scatter.copy(count - 1 - step, part, 1).start)
                    pl.when(me == count - 1)(scatter.copy(step, part, -1).start)
        pl.when(me - distance >= 0)(lambda: back(me - distance))
        pl.when(me + distance < count)(lambda: back(me + distance))
        if distance == count - 2:
            scatter.pass_on(1, False, False)
            dense_advance(1)

    def out_grad(index, unused):
        right = low[:, :, pl.ds(pl.multiple_of(index * chunk, chunk), chunk)].reshape(count * rows, chunk)
        both = dot_tn(mixed[...], right).astype(BF)
        cube_a[index] = both[:half]
        cube_b[index] = both[half:]
        return unused

    lax.fori_loop(0, groups, out_grad, 0)
    for cube in cubes:
        cube.start(0)
    level = 0
    for time in list(scatter.times())[1:]:
        scatter.pass_on(time, False, False)
        if time == 2:
            for rest in range(2, levels):
                dense_advance(rest)
            dense_cubes[0].result(gate_sum_ref)
            dense_cubes[1].result(value_sum_ref)
            for save in sum_saves:
                save.start()
        if level < levels:
            for cube in cubes:
                cube.finish(level)
                if level + 1 < levels:
                    cube.start(level + 1)
            level += 1
    for rest in range(level, levels):
        for cube in cubes:
            cube.finish(rest)
            if rest + 1 < levels:
                cube.start(rest + 1)
    cubes[0].result(out_grad_ref.at[0:half])
    cubes[1].result(out_grad_ref.at[half:channels])
    middle_load.wait()
    row_sums = jnp.zeros((rows, 1), F32)
    for part in range(PARTS):
        span = slice(part * width, (part + 1) * width)
        scatter.wait_total(part)
        total = scatter.total(part)
        row_sums = row_sums + jnp.sum(total * total, axis=1, keepdims=True)
        layer_ref[:, span] = (middle_ref[:, span] + total).astype(BF)
    stat_ref[...] = jnp.zeros(stat_ref.shape, F32) + live_total(live_ref, row_sums)
    for save in sum_saves:
        save.wait()
    for block in range(count):
        dm_copy(block).wait()
    gather.drain()
    scatter.drain()


def call_middle(count, groups, middle_grad, middle, live, terms, mixer_out, mixed, gate_weights, value_weights):
    rows, columns = middle.shape
    channels = mixer_out.shape[0]
    total = count * rows
    chunk = columns // groups
    units = gate_weights.shape[1]
    split = (groups, chunk, units)
    return pl.pallas_call(
        functools.partial(middle_kernel, count, groups),
        out_shape=(
            jax.ShapeDtypeStruct((rows, columns), BF), jax.ShapeDtypeStruct((8, 128), F32),
            jax.ShapeDtypeStruct((channels, chunk), F32), jax.ShapeDtypeStruct((chunk, units), F32),
            jax.ShapeDtypeStruct((chunk, units), F32), jax.ShapeDtypeStruct((total, channels), F32),
        ),
        in_specs=[IN_VMEM] * 2 + [ANYWHERE] * 6,
        out_specs=(IN_VMEM,) * 3 + (ANYWHERE,) * 3,
        scratch_shapes=[
            pltpu.VMEM((count, rows, columns), BF),
            pltpu.VMEM((channels, columns), BF),
            pltpu.VMEM((total, channels), BF),
            pltpu.VMEM((count, rows, channels), F32),
            pltpu.VMEM((count, PARTS, rows, columns // PARTS), BF),
            pltpu.VMEM((count + 1, PARTS, rows, columns // PARTS), BF),
            pltpu.VMEM((groups, channels // 2, chunk), BF),
            pltpu.VMEM((groups - 1, channels // 2, chunk), BF),
            pltpu.VMEM((groups, channels // 2, chunk), BF),
            pltpu.VMEM((groups - 1, channels // 2, chunk), BF),
            pltpu.VMEM(split, BF), pltpu.VMEM((groups - 1, chunk, units), BF),
            pltpu.VMEM(split, BF), pltpu.VMEM((groups - 1, chunk, units), BF),
            pltpu.VMEM((rows, columns), F32), pltpu.VMEM((chunk, units), F32), pltpu.VMEM((chunk, units), F32),
            DMA((5,)), DMA((count,)), DMA((2, count)), DMA((count,)), DMA((count, PARTS)), DMA((count + 1, PARTS)),
            DMA((groups - 1,)), DMA((groups - 1,)), DMA((groups - 1,)), DMA((groups - 1,)),
            DMA((groups - 1,)), DMA((groups - 1,)), DMA((groups - 1,)), DMA((groups - 1,)), DMA((3,)),
        ],
        compiler_params=pltpu.CompilerParams(vmem_limit_bytes=VMEM_LIMIT, collective_id=2, has_side_effects=True),
        cost_estimate=pl.CostEstimate(flops=4 * total * columns * channels, bytes_accessed=40 * total * channels,
                                      transcendentals=0),
    )(middle_grad, live, middle, terms, mixer_out, mixed, gate_weights.reshape(split), value_weights.reshape(split))


def input_kernel(count, groups, heads, tokens_hbm, gain_ref, middle_grad_hbm, mask_ref, vec_ref, rate_ref, inlet_ref,
                 dense_gain_ref, stat_ref, dense_stat_ref, value_hbm, gate_hbm, normed_hbm, dm_hbm, vp_hbm, gp_hbm, state_hbm, conv_hbm, forget_hbm, input_hbm,
                 input_grad_ref, flat_ref, value_grad_ref, gate_grad_ref, full, vec_grad_ref,
                 value_w, gate_w, dm, vp, gp, state, conv, forget, inlet_gate, normed, vlow, glow, dzf, dzi, dconv,
                 clow, sums, carry, held, slots, cube_a, slots_a, cube_b, slots_b, cube_c, slots_c,
                 vec_held, vec_slots, flat_held, flat_slots, tokens_ref, middle_grad_ref,
                 load_sem, block_sem, normed_sem, rs_send, rs_recv, a_send, a_recv, b_send, b_recv, c_send, c_recv,
                 f_send, f_recv, v_send, v_recv, flat_send, flat_recv, own_sem):
    me = lax.axis_index("mp")
    rows, columns = tokens_ref.shape
    channels = value_w.shape[1]
    width = columns // PARTS
    chunk = columns // groups
    total_rows = count * rows
    head = channels // heads
    loads = [pltpu.make_async_copy(value_hbm, value_w, load_sem.at[0]),
             pltpu.make_async_copy(gate_hbm, gate_w, load_sem.at[1])]
    for load in loads:
        load.start()

    own_loads = [pltpu.make_async_copy(tokens_hbm, tokens_ref, own_sem.at[0]),
                 pltpu.make_async_copy(middle_grad_hbm, middle_grad_ref, own_sem.at[1])]

    def block_loads(block, slot):
        at = pl.multiple_of(block * rows, rows)
        plain = pl.ds(at, rows)
        ahead = pl.ds(at, rows + 8)
        return [pltpu.make_async_copy(source.at[window], target.at[slot], block_sem.at[slot, index])
                for index, (source, window, target) in enumerate((
                    (dm_hbm, plain, dm), (vp_hbm, ahead, vp), (gp_hbm, plain, gp), (state_hbm, ahead, state),
                    (conv_hbm, plain, conv), (forget_hbm, plain, forget), (input_hbm, plain, inlet_gate)))]

    for load in block_loads(count - 1, 0):
        load.start()
    for load in own_loads:
        load.start()
    zeros = jnp.zeros((8, channels), F32)
    dconv[rows:rows + 8, :] = zeros
    carry[...] = zeros
    for row in range(8):
        sums[row] = zeros
    greet(count, groups, True)
    scatter = Scatter(count, held, slots, rs_send, rs_recv)
    order_a, order_b = orders(groups)
    cubes = (Cube(groups, order_a, cube_a, slots_a, a_send, a_recv),
             Cube(groups, order_b, cube_b, slots_b, b_send, b_recv),
             Cube(groups, order_b, cube_c, slots_c, c_send, c_recv))
    spread = Spread(cubes[2], full, f_send, f_recv)
    for load in loads:
        load.wait()

    def back(step, unused):
        block = count - 1 - step
        slot = step % 2
        for load in block_loads(block, slot):
            load.wait()

        @pl.when(step + 1 < count)
        def _():
            for load in block_loads(block - 1, 1 - slot):
                load.start()

        base = block * rows
        rec_backward(base, rows, dm.at[slot], vp.at[slot], gp.at[slot], mask_ref, vec_ref, rate_ref, inlet_ref,
                     state.at[slot], conv.at[slot], forget.at[slot], inlet_gate.at[slot],
                     vlow, glow, dzf, dzi, dconv, clow, sums, carry)
        window = pl.ds(pl.multiple_of(base, rows), rows)
        for part in range(PARTS):
            span = slice(part * width, (part + 1) * width)
            held[block, part] = (dot_nt(vlow[window, :], value_w[span, :])
                                 + dot_nt(glow[window, :], gate_w[span, :])).astype(BF)
            pl.when((me == 0) & (block > 0))(scatter.copy(block, part, 1).start)
            pl.when((me == count - 1) & (block == count - 2))(scatter.copy(block, part, -1).start)
        return unused

    def normed_copy(index, slot):
        return pltpu.make_async_copy(
            normed_hbm.at[:, :, pl.ds(pl.multiple_of(index * chunk, chunk), chunk)], normed.at[slot],
            normed_sem.at[slot])

    normed_copy(0, 0).start()
    lax.fori_loop(0, count, back, 0)
    for block in range(count - 2):
        for part in range(PARTS):
            pl.when(me == count - 1)(scatter.copy(block, part, -1).start)

    def weights(index, unused):
        slot = index % 2
        normed_copy(index, slot).wait()
        pl.when(index + 1 < groups)(lambda: normed_copy(index + 1, 1 - slot).start())
        left = normed[slot].reshape(total_rows, chunk)
        cube_a[index] = dot_tn(left, vlow[...]).astype(BF)
        cube_b[index] = dot_tn(left, glow[...]).astype(BF)
        part = index * chunk // width
        inside = pl.ds(pl.multiple_of(index * chunk % width, chunk), chunk)
        gain_row = jnp.zeros((1, chunk), F32)
        for block in range(count):
            gain_row = gain_row + jnp.sum(
                normed[slot, block].astype(F32) * held[block, part, :, inside].astype(F32), axis=0, keepdims=True)
        flat_held[0:1, pl.ds(pl.multiple_of(index * chunk, chunk), chunk)] = gain_row
        return unused

    flat_held[...] = jnp.zeros(flat_held.shape, F32)
    lax.fori_loop(0, groups, weights, 0)
    flat_held[0:1, :] = flat_held[0:1, :] / gain_ref[...]
    flat_held[1:2, :] = dense_gain_ref[...]
    for index, value in enumerate((stat_ref[0:1], stat_ref[1:2], dense_stat_ref[0:1], stat_ref[2:3])):
        flat_held[2:3, index * 128:(index + 1) * 128] = value
    peers = [("dp", bit) for bit in range(groups.bit_length() - 1)]
    peers += [("mp", bit) for bit in range(count.bit_length() - 1)]

    def flat_copy(index):
        axis, bit = peers[index]
        return pltpu.make_async_remote_copy(
            src_ref=flat_held, dst_ref=flat_slots.at[index], send_sem=flat_send.at[index],
            recv_sem=flat_recv.at[index], device_id={axis: partner_of(bit, axis)}, device_id_type=MESH)

    flat_copy(0).start()
    cubes[0].start(0)
    cubes[1].start(0)
    slab = 2 * channels // groups
    for which, source in enumerate((dzf, dzi)):
        for index in range(heads):
            span = slice(index * head, (index + 1) * head)
            square = dot_tn(clow[:, span], source[:, span])
            first = (which * channels + index * head) // slab
            for piece in range(head // slab):
                cube_c[first + piece] = square[piece * slab:(piece + 1) * slab]
    cubes[2].start(0)
    for row in range(8):
        vec_held[0, row:row + 1, :] = jnp.sum(sums[row], axis=0, keepdims=True)

    def vec_copy(level):
        return pltpu.make_async_remote_copy(
            src_ref=vec_held.at[level], dst_ref=vec_slots.at[level], send_sem=v_send.at[level],
            recv_sem=v_recv.at[level], device_id={"dp": partner_of(level)}, device_id_type=MESH)

    levels = len(order_a)
    vec_copy(0).start()

    def advance(level):
        if level < len(peers):
            flat_copy(level).wait()
            flat_held[...] += flat_slots[level]
            if level + 1 < len(peers):
                flat_copy(level + 1).start()
        if level < levels:
            for cube in cubes:
                cube.finish(level)
                if level + 1 < levels:
                    cube.start(level + 1)
            vec_copy(level).wait()
            if level + 1 < levels:
                vec_held[level + 1] = vec_held[level] + vec_slots[level]
                vec_copy(level + 1).start()
            else:
                vec_grad_ref[...] = vec_held[level] + vec_slots[level]
                cubes[0].result(value_grad_ref)
                cubes[1].result(gate_grad_ref)
                cubes[2].result(full.at[lax.axis_index("dp")])
                spread.start(levels - 1)
        elif level < 2 * levels:
            back_level = 2 * levels - 1 - level
            spread.finish(back_level)
            if back_level > 0:
                spread.start(back_level - 1)

    stages = max(2 * levels, len(peers))
    slots_all = [(time, part) for time in scatter.times() for part in range(PARTS)]
    early = max(len(slots_all) - 5 - 2 * (stages - 4), 0)
    for time in range(1, early // PARTS + 1):
        scatter.pass_on(time, False, None)
    level = 0
    for index in range(early // PARTS * PARTS, len(slots_all)):
        scatter.pass_one(*slots_all[index], False, None)
        turn = len(slots_all) - index - 1
        if level < stages and (turn <= 4 or turn % 2 == 0) and turn > 0 and stages - level >= min(turn, 4):
            advance(level)
            level += 1
    for rest in range(level, stages):
        advance(rest)
    flat_ref[...] = flat_held[...]
    def write(span, change):
        input_grad_ref[:, span] = (middle_grad_ref[:, span] + change).astype(BF)

    for load in own_loads:
        load.wait()
    norm_back(tokens_ref, gain_ref, scatter, None, write)
    scatter.drain()


def call_input(count, groups, heads, tokens, gain, middle_grad, masks, vec, rate, inlet, dense_gain_grad, stat,
               dense_stat, value_proj, gate_proj, normed_all, dm, vp, gp, state, conv, forget, inp):
    rows, columns = tokens.shape
    channels = value_proj.shape[1]
    total = count * rows
    chunk = columns // groups
    head = channels // heads
    slab = 2 * channels // groups
    plain = pltpu.VMEM((2, rows, channels), F32)
    ahead = pltpu.VMEM((2, rows + 8, channels), F32)
    low = pltpu.VMEM((total, channels), BF)
    levels = groups.bit_length() - 1
    flats = levels + count.bit_length() - 1
    return pl.pallas_call(
        functools.partial(input_kernel, count, groups, heads),
        out_shape=(
            jax.ShapeDtypeStruct((rows, columns), BF), jax.ShapeDtypeStruct((8, columns), F32),
            jax.ShapeDtypeStruct((chunk, channels), F32), jax.ShapeDtypeStruct((chunk, channels), F32),
            jax.ShapeDtypeStruct((groups, slab, head), F32), jax.ShapeDtypeStruct((8, channels), F32),
        ),
        in_specs=[ANYWHERE, IN_VMEM, ANYWHERE] + [IN_VMEM] * 7 + [ANYWHERE] * 10,
        out_specs=(IN_VMEM,) * 6,
        scratch_shapes=[
            pltpu.VMEM((columns, channels), BF),
            pltpu.VMEM((columns, channels), BF),
            plain, ahead, plain, ahead, plain, plain, plain,
            pltpu.VMEM((2, count, rows, chunk), BF),
            low, low, low, low,
            pltpu.VMEM((rows + 8, channels), F32),
            low,
            pltpu.VMEM((8, 8, channels), F32),
            pltpu.VMEM((8, channels), F32),
            pltpu.VMEM((count, PARTS, rows, columns // PARTS), BF),
            pltpu.VMEM((count + 1, PARTS, rows, columns // PARTS), BF),
            pltpu.VMEM((groups, chunk, channels), BF), pltpu.VMEM((groups - 1, chunk, channels), BF),
            pltpu.VMEM((groups, chunk, channels), BF), pltpu.VMEM((groups - 1, chunk, channels), BF),
            pltpu.VMEM((groups, slab, head), F32), pltpu.VMEM((groups - 1, slab, head), F32),
            pltpu.VMEM((levels, 8, channels), F32), pltpu.VMEM((levels, 8, channels), F32),
            pltpu.VMEM((8, columns), F32), pltpu.VMEM((flats, 8, columns), F32),
            pltpu.VMEM((rows, columns), BF), pltpu.VMEM((rows, columns), F32),
            DMA((2,)), DMA((2, 7)), DMA((2,)), DMA((count, PARTS)), DMA((count + 1, PARTS)),
            DMA((groups - 1,)), DMA((groups - 1,)), DMA((groups - 1,)), DMA((groups - 1,)),
            DMA((groups - 1,)), DMA((groups - 1,)), DMA((groups - 1,)), DMA((groups - 1,)),
            DMA((levels,)), DMA((levels,)), DMA((flats,)), DMA((flats,)), DMA((2,)),
        ],
        compiler_params=pltpu.CompilerParams(vmem_limit_bytes=VMEM_LIMIT, collective_id=3, has_side_effects=True),
        cost_estimate=pl.CostEstimate(flops=8 * total * columns * channels, bytes_accessed=60 * total * channels,
                                      transcendentals=4 * total * channels),
    )(tokens, gain, middle_grad, masks, vec, rate, inlet, dense_gain_grad, stat, dense_stat, value_proj, gate_proj,
      normed_all, dm, vp, gp, state, conv, forget, inp)


def spans(total):
    size = 512 if total % 512 == 0 else 256
    return [slice(at, at + size) for at in range(0, total, size)]


def dense_kernel(count, groups, middle_ref, gain_ref, cot_hbm, gate_hbm, value_hbm, down_hbm,
                 middle_grad_ref, gain_grad_ref, dense_part_hbm, gate_out, value_out, down_out,
                 normed, cot, gate_w, value_w, down_w, hidden, gate_g, value_g, dense_part, held, slots, stage,
                 load_sem, cot_sem, part_sem, stage_sem, ag_send, ag_recv, rs_send, rs_recv):
    me = lax.axis_index("mp")
    rows, columns = middle_ref.shape
    units = gate_w.shape[1]
    width = columns // PARTS
    loads = [pltpu.make_async_copy(gate_hbm, gate_w, load_sem.at[0]),
             pltpu.make_async_copy(value_hbm, value_w, load_sem.at[1]),
             pltpu.make_async_copy(down_hbm, down_w, load_sem.at[2])]
    for load in loads:
        load.start()

    def cot_copy(block):
        return pltpu.make_async_copy(cot_hbm.at[block],
                                     cot.at[block], cot_sem.at[block])

    for block in range(count):
        cot_copy(block).start()
    greet(count)
    gather = Gather(count, normed, ag_send, ag_recv)
    scatter = Scatter(count, held, slots, rs_send, rs_recv)
    norm_rows(middle_ref, gain_ref, normed.at[me])
    gather.start()
    for load in loads:
        load.wait()
    pieces = 3
    piece = units // pieces

    def part_copy(block, slot):
        return pltpu.make_async_copy(dense_part.at[slot], dense_part_hbm.at[block], part_sem.at[slot])

    def compute(block, slot, reuse):
        cot_copy(block).wait()
        rows_in = normed[block]
        rows_cot = cot[block]
        for index in range(pieces):
            span = slice(index * piece, (index + 1) * piece)
            gate_linear = dot_nn(rows_in, gate_w[:, span])
            value_linear = dot_nn(rows_in, value_w[:, span])
            hidden_grad = dot_nt(rows_cot, down_w[span, :])
            act, slope = gelu_both(gate_linear)
            hidden[block, :, span] = (act * value_linear).astype(BF)
            gate_g[block, :, span] = (hidden_grad * value_linear * slope).astype(BF)
            value_g[block, :, span] = (hidden_grad * act).astype(BF)
        for part in range(PARTS):
            span = slice(part * width, (part + 1) * width)
            held[block, part] = (dot_nt(gate_g[block], gate_w[span, :])
                                 + dot_nt(value_g[block], value_w[span, :])).astype(BF)
            scatter.first(block, part)
        pl.when(reuse)(lambda: part_copy(block, slot).wait())
        for part in range(PARTS):
            span = slice(part * width, (part + 1) * width)
            dense_part[slot, part] = dot_nn(hidden[block], down_w[:, span]).astype(BF)
        part_copy(block, slot).start()

    def arrive(distance, unused):
        pl.when(distance > 0)(lambda: gather.take(distance))

        def side(which, inner):
            block = me - distance + 2 * distance * which
            pl.when((block >= 0) & (block < count) & ((distance > 0) | (which == 0)))(
                lambda: compute(block, which, (distance > 1) | ((distance == 1) & (which == 0))))
            return inner

        return lax.fori_loop(0, 2, side, unused)

    lax.fori_loop(0, count, arrive, 0)

    total_rows = count * rows
    left_rows = columns // 4
    unit_rows = units // 4
    group_width = columns // groups

    def stage_copy(kind, index, slot):
        if kind == 2:
            half = columns // 2
            return pltpu.make_async_copy(
                stage.at[slot, pl.ds(0, unit_rows), pl.ds(0, half)],
                down_out.at[pl.ds(index // 2 * unit_rows, unit_rows), pl.ds(index % 2 * half, half)],
                stage_sem.at[slot])
        target = gate_out if kind == 0 else value_out
        return pltpu.make_async_copy(
            stage.at[slot, pl.ds(0, left_rows), pl.ds(0, units)],
            target.at[pl.ds(index * left_rows, left_rows)], stage_sem.at[slot])

    def grads(kind, index, slot):
        if kind == 2:
            low = index // 2 * unit_rows
            left = hidden[:, :, low:low + unit_rows].reshape(total_rows, unit_rows)
            for span in spans(columns // 2):
                at = index % 2 * (columns // 2) + span.start
                size = span.stop - span.start
                right = cot[:, :, at:at + size].reshape(total_rows, size)
                stage[slot, 0:unit_rows, span] = dot_tn(left, right).astype(BF)
        else:
            left = normed[:, :, index * left_rows:(index + 1) * left_rows].reshape(total_rows, left_rows)
            source = gate_g if kind == 0 else value_g
            for span in spans(units):
                right = source[:, :, span].reshape(total_rows, span.stop - span.start)
                stage[slot, 0:left_rows, span] = dot_tn(left, right).astype(BF)

    work = [(kind, index) for kind in (0, 1, 2) for index in range((4, 4, 8)[kind])]
    started = []
    times = scatter.times()
    per_step = -(-len(work) // (len(times) + 1))
    for step in range(len(times) + 1):
        if step > 0:
            scatter.pass_on(step, True, True)
        for kind, index in work[step * per_step:(step + 1) * per_step]:
            slot = len(started) % 2
            if len(started) >= 2:
                stage_copy(*started[-2], slot).wait()
            grads(kind, index, slot)
            stage_copy(kind, index, slot).start()
            started.append((kind, index))
    for back in (2, 1):
        stage_copy(*started[-back], (len(started) - back) % 2).wait()

    def write(span, change):
        middle_grad_ref[:, span] = cot[me, :, span].astype(F32) + change

    norm_back(middle_ref, gain_ref, scatter, gain_grad_ref, write)
    part_copy(0, 0).wait()
    pl.when(me < count - 1)(part_copy(0, 1).wait)
    gather.drain()
    scatter.drain()


def call_dense(count, groups, middle, gain, cot_all, dense_gate, dense_value, dense_down):
    rows, columns = middle.shape
    units = dense_gate.shape[1]
    width = columns // PARTS
    any_spec = pl.BlockSpec(memory_space=pl.ANY)
    vmem = pl.BlockSpec(memory_space=pltpu.VMEM)
    dma = pltpu.SemaphoreType.DMA
    return pl.pallas_call(
        functools.partial(dense_kernel, count, groups),
        out_shape=(
            jax.ShapeDtypeStruct((rows, columns), F32),
            jax.ShapeDtypeStruct((1, columns), F32),
            jax.ShapeDtypeStruct((count, PARTS, rows, width), BF),
            jax.ShapeDtypeStruct((columns, units), BF),
            jax.ShapeDtypeStruct((columns, units), BF),
            jax.ShapeDtypeStruct((units, columns), BF),
        ),
        in_specs=[vmem, vmem, any_spec, any_spec, any_spec, any_spec],
        out_specs=(vmem, vmem, any_spec, any_spec, any_spec, any_spec),
        scratch_shapes=[
            pltpu.VMEM((count, rows, columns), BF),
            pltpu.VMEM((count, rows, columns), BF),
            pltpu.VMEM((columns, units), BF),
            pltpu.VMEM((columns, units), BF),
            pltpu.VMEM((units, columns), BF),
            pltpu.VMEM((count, rows, units), BF),
            pltpu.VMEM((count, rows, units), BF),
            pltpu.VMEM((count, rows, units), BF),
            pltpu.VMEM((2, PARTS, rows, width), BF),
            pltpu.VMEM((count, PARTS, rows, width), BF),
            pltpu.VMEM((count + 1, PARTS, rows, width), BF),
            pltpu.VMEM((2, columns // 4, max(units, columns // 2)), BF),
            dma((3,)), dma((count,)), dma((2,)), dma((2,)),
            dma((2, count)), dma((count,)), dma((count, PARTS)), dma((count + 1, PARTS)),
        ],
        compiler_params=pltpu.CompilerParams(
            vmem_limit_bytes=VMEM_LIMIT, collective_id=0, has_side_effects=True),
        cost_estimate=pl.CostEstimate(flops=18 * count * rows * columns * units,
                                      bytes_accessed=12 * columns * units, transcendentals=count * rows * units),
    )(middle, gain, cot_all, dense_gate, dense_value, dense_down)


def scatter_dp(values, dimension):
    return lax.psum_scatter(values, "dp", scatter_dimension=dimension, tiled=True).astype(F32)


def local(groups, tokens, cotangent, lengths, live_mask, mixer_gain, value_proj, gate_proj, conv_taps, conv_bias,
          rate_weight, rate_bias, inlet_weight, inlet_bias, decay_param, mixer_out, dense_gain,
          dense_gate, dense_value, dense_down):
    columns = tokens.shape[1]
    head_count, head_width = rate_weight.shape[:2]
    channels = head_count * head_width
    count = lax.axis_size("mp")
    live = live_mask[None, :]
    middle, stat, masks, vec, rate_square, inlet_square, normed_all, cot_all, mixed, *saved = call_mixer(
        count, lengths, tokens, mixer_gain[None, :], live, conv_taps,
        (conv_bias, rate_bias, inlet_bias, decay_param), rate_weight, inlet_weight, cotangent,
        value_proj, gate_proj, mixer_out)
    middle_grad, dense_gain_grad, dense_terms, gate_weights, value_weights, down_weights = call_dense(
        count, groups, middle, dense_gain[None, :], cot_all, dense_gate, dense_value, dense_down)
    layer_out, dense_stat, mixer_out_sum, gate_sum, value_sum, dm = call_middle(
        count, groups, middle_grad, middle, live, dense_terms, mixer_out, mixed, gate_weights, value_weights)
    dm, down_weights = lax.optimization_barrier((dm, down_weights))
    input_grad, flat, value_proj_sum, gate_proj_sum, small, vec_sum = call_input(
        count, groups, head_count, tokens, mixer_gain[None, :], middle_grad, masks, vec, rate_square, inlet_square,
        dense_gain_grad, stat, dense_stat, value_proj, gate_proj, normed_all, dm, *saved)
    branch_rms = jnp.sqrt(flat[2, 0:384:128] / (flat[2, 384] * columns))
    decay_scale = 8.0 * jax.nn.sigmoid(-decay_param)
    return (
        layer_out,
        input_grad,
        flat[0],
        value_proj_sum,
        gate_proj_sum,
        vec_sum[0:4],
        vec_sum[4],
        small[:groups // 2].reshape(rate_weight.shape),
        vec_sum[V_RATE],
        small[groups // 2:].reshape(rate_weight.shape),
        vec_sum[V_INLET],
        vec_sum[V_DECAY] * decay_scale,
        mixer_out_sum,
        flat[1],
        gate_sum,
        value_sum,
        scatter_dp(down_weights, 1),
        branch_rms,
    )


def solution(mesh):
    rows = P(("dp", "mp"), None)
    return jax.shard_map(
        functools.partial(local, mesh.shape["dp"]),
        mesh=mesh,
        in_specs=(
            rows, rows, P("dp", None), P(("dp", "mp")), P(),
            P(None, "mp"), P(None, "mp"), P(None, "mp"), P("mp"),
            P("mp", None, None), P("mp"), P("mp", None, None), P("mp"), P("mp"),
            P("mp", None), P(), P(None, "mp"), P(None, "mp"), P("mp", None),
        ),
        out_specs=(
            rows, rows, P(), P("dp", "mp"), P("dp", "mp"),
            P(None, "mp"), P("mp"), P("mp", None, None), P("mp"), P("mp", None, None), P("mp"), P("mp"),
            P("mp", "dp"), P(), P("dp", "mp"), P("dp", "mp"), P("mp", "dp"), P(),
        ),
        check_vma=False,
    )
```
